256 devices in a mesh: ctx: 32 (over x, z), head: 8 (over y, core).
Axes of the slice: x: 4, y: 4, z: 8, core: 2. Of those that a mesh axis runs over, the one named last changes fastest.
Arguments:
- queries: bfloat16 [32768, 2048], P(('ctx', 'head')), may hold values from -6 to 6
- key_rows: bfloat16 [32768, 2048], P(('ctx', 'head')), may hold values from -6 to 6
- value_rows: bfloat16 [32768, 2048], P(('ctx', 'head')), may hold values from -6 to 6
- out_grad: bfloat16 [32768, 2048], P(('ctx', 'head')), may hold values from -48 to 48
- bounds: int32 [65], replicated, may hold values from 0 to 32768, as said below
Outputs:
- query_grad: bfloat16 [32768, 2048], P(('ctx', 'head'))
- key_grad: bfloat16 [32768, 2048], P(('ctx', 'head'))
- value_grad: bfloat16 [32768, 2048], P(('ctx', 'head'))
The draws below stay inside these ranges and needn't reach their ends.
Inputs may be any that keep to these rules, and one draw needn't show every extreme that they name: bounds rises from 0 to 32768; every document holds 2 to 2048 tokens, exactly one holds 2048 and at least one holds 2.
All inputs are finite; a program needn't handle non-finite values.
Results may differ from the reference program's by a relative error of at most 0.0072.
Values may be sent and summed in bfloat16 or wider, within the bound.
No kernel may reach another device: no remote copies, remote signals or barrier semaphores. Data moves between devices by JAX's collectives and lax.ppermute only.
A program may use at most 128 MiB of HBM per device.

```python
import jax
import jax.numpy as jnp
from jax import lax

HD = 128
HEADS = 16
TILE = 512
D_WIN = 2048
TOKENS = 32768
NDOC = 64
MOST = 2048


def bound_table(key):
    first_key, second_key, third_key = jax.random.split(key, 3)
    order = jnp.arange(NDOC, dtype=jnp.int32)
    chosen = jax.random.randint(first_key, (), 0, NDOC)
    shortest = (chosen + 1 + jax.random.randint(third_key, (), 0, NDOC - 1)) % NDOC
    weight = jax.random.randint(second_key, (NDOC,), 1, 5)
    others = order != chosen
    receivers = others & (order != shortest)
    weight = jnp.where(receivers, weight, 0)
    spare = TOKENS - 2 * NDOC - (MOST - 2)
    extra = spare * weight // jnp.sum(weight)
    leftover = spare - jnp.sum(extra)
    receiver_rank = jnp.cumsum(receivers.astype(jnp.int32)) - 1
    extra = extra + jnp.where(receivers & (receiver_rank < leftover), 1, 0)
    lengths = 2 + extra + jnp.where(others, 0, MOST - 2)
    return jnp.concatenate([jnp.zeros((1,), jnp.int32), jnp.cumsum(lengths).astype(jnp.int32)])


def draw_bounds(key, part):
    key = jax.random.fold_in(key, 100)
    return bound_table(key)


def draw_queries(key, part):
    key = jax.random.fold_in(key, 1)
    values_drawn = jnp.clip(jax.random.normal(key, (TOKENS, D_WIN), jnp.float32), -6.0, 6.0)
    return values_drawn.astype(jnp.bfloat16)


def draw_key_rows(key, part):
    key = jax.random.fold_in(key, 2)
    values_drawn = jnp.clip(jax.random.normal(key, (TOKENS, D_WIN), jnp.float32), -6.0, 6.0)
    return values_drawn.astype(jnp.bfloat16)


def steps_of(rng, dims, cuts, low, top_value):
    gain, own = 1.0, jax.random.fold_in(rng, 6)
    for position, blocks in cuts:
        heights = jnp.exp(jax.random.uniform(jax.random.fold_in(own, position), (blocks,), jnp.float32, low / len(cuts), top_value / len(cuts)))
        gain = gain * jnp.repeat(heights, dims[position] // blocks).reshape([-1 if axis == position else 1 for axis in range(len(dims))])
    return gain


def normal_values(own_key, dims, width, limit, cuts=(), kind=jnp.bfloat16):
    gain = steps_of(own_key, dims, cuts, -0.22, 0.18) if cuts else 1.0
    drawn = jax.random.normal(own_key, dims, jnp.float32) * width * gain
    return jnp.minimum(jnp.maximum(drawn, -limit), limit).astype(kind)


def setup_inputs(seed: int = 0) -> dict:
    seeds = jax.random.split(jax.random.key(seed), 6)
    queries = draw_queries(jax.random.fold_in(seeds[5], 71), 0)
    key_rows = draw_key_rows(jax.random.fold_in(seeds[5], 71), 0)
    value_rows = normal_values(seeds[2], (TOKENS, D_WIN), 1.0, 6.0, ((0, 256),))
    out_grad = normal_values(seeds[3], (TOKENS, D_WIN), 8.0, 48.0, ((0, 256),))
    bounds = draw_bounds(jax.random.fold_in(seeds[5], 71), 0)
    return {"queries": queries, "key_rows": key_rows, "value_rows": value_rows, "out_grad": out_grad, "bounds": bounds}


MASKED_LOW = -1.0e30


def segment_table(bounds, total):
    positions = jnp.arange(total, dtype=jnp.int32)
    inside = (bounds[1:][None, :] <= positions[:, None]).astype(jnp.int32)
    return jnp.sum(inside, axis=1).astype(jnp.int32)


def reference(queries, key_rows, value_rows, out_grad, bounds):
    three_dims = (TOKENS, HEADS, HD)
    query_all = queries.reshape(three_dims)
    grad_all = out_grad.reshape(three_dims)
    key_pad = jnp.pad(key_rows.reshape(three_dims), ((MOST, MOST), (0, 0), (0, 0)))
    value_pad = jnp.pad(value_rows.reshape(three_dims), ((MOST, MOST), (0, 0), (0, 0)))
    segment = segment_table(bounds, TOKENS)
    segment_pad = jnp.pad(segment, (MOST, MOST), constant_values=-1).astype(jnp.int32)
    window = TILE + 2 * MOST
    softmax_scale = HD ** -0.5
    block_count = TOKENS // TILE

    def block_inputs(block_index):
        row_start = (block_index * TILE).astype(jnp.int32)
        query_block = lax.dynamic_slice_in_dim(query_all, row_start, TILE, 0).astype(jnp.float32)
        grad_block = lax.dynamic_slice_in_dim(grad_all, row_start, TILE, 0).astype(jnp.float32)
        key_block = lax.dynamic_slice_in_dim(key_pad, row_start, window, 0).astype(jnp.float32)
        value_block = lax.dynamic_slice_in_dim(value_pad, row_start, window, 0).astype(jnp.float32)
        row_segment = lax.dynamic_slice_in_dim(segment, row_start, TILE, 0)
        col_segment = lax.dynamic_slice_in_dim(segment_pad, row_start, window, 0)
        allowed = (row_segment[:, None] == col_segment[None, :])[None]
        logits = jnp.einsum("qhd,khd->hqk", query_block, key_block) * softmax_scale
        prob_grad = jnp.einsum("qhd,khd->hqk", grad_block, value_block)
        return query_block, grad_block, key_block, value_block, allowed, logits, prob_grad

    def block_stats(block_index):
        parts = block_inputs(block_index)
        allowed, logits, prob_grad = parts[4], parts[5], parts[6]
        row_max = jnp.max(jnp.where(allowed, logits, MASKED_LOW), axis=2)
        unnormed = jnp.where(allowed, jnp.exp(logits - row_max[:, :, None]), 0.0)
        row_sum = jnp.sum(unnormed, axis=2)
        return row_max + jnp.log(row_sum), jnp.sum(unnormed * prob_grad, axis=2) / row_sum

    log_norm, delta_rows = lax.map(block_stats, jnp.arange(block_count, dtype=jnp.int32))

    def block_grads(carry_in, block_index):
        key_acc, value_acc = carry_in
        query_block, grad_block, key_block, value_block, allowed, logits, prob_grad = block_inputs(block_index)
        norm_block = log_norm[block_index]
        delta_block = delta_rows[block_index]
        weights = jnp.where(allowed, jnp.exp(logits - norm_block[:, :, None]), 0.0)
        weights_low = lax.optimization_barrier(weights.astype(jnp.bfloat16)).astype(jnp.float32)
        score_raw = weights * (prob_grad - delta_block[:, :, None])
        score_grad = lax.optimization_barrier(score_raw.astype(jnp.bfloat16)).astype(jnp.float32)
        query_part = (jnp.einsum("hqk,khd->qhd", score_grad, key_block) * softmax_scale).astype(jnp.bfloat16)
        row_start = (block_index * TILE).astype(jnp.int32)
        key_now = lax.dynamic_slice_in_dim(key_acc, row_start, window, 0)
        key_acc = lax.dynamic_update_slice_in_dim(key_acc, key_now + jnp.einsum("hqk,qhd->khd", score_grad, query_block), row_start, 0)
        value_now = lax.dynamic_slice_in_dim(value_acc, row_start, window, 0)
        value_acc = lax.dynamic_update_slice_in_dim(value_acc, value_now + jnp.einsum("hqk,qhd->khd", weights_low, grad_block), row_start, 0)
        return (key_acc, value_acc), query_part

    empty_acc = jnp.zeros((TOKENS + 2 * MOST, HEADS, HD), jnp.float32)
    (key_acc, value_acc), query_parts = lax.scan(block_grads, (empty_acc, empty_acc), jnp.arange(block_count, dtype=jnp.int32))
    query_grad = query_parts.reshape(TOKENS, HEADS * HD)
    key_grad = (key_acc[MOST:MOST + TOKENS] * softmax_scale).astype(jnp.bfloat16).reshape(TOKENS, HEADS * HD)
    value_grad = value_acc[MOST:MOST + TOKENS].astype(jnp.bfloat16).reshape(TOKENS, HEADS * HD)
    return (query_grad, key_grad, value_grad)
```

```python
import jax
import jax.numpy as jnp
from jax import lax
from jax.experimental import pallas as pl
from jax.experimental.pallas import tpu as pltpu
from jax.sharding import PartitionSpec as P

HD = 128
NDOC = 64
BLOCK = 1024
SHARD = 128
SHARDS = BLOCK // SHARD
STEP = 256
MOST = 2048
SCALE = HD ** -0.5
LOG2E = 1.4426950408889634
LOW = -1.0e30
VMEM_LIMIT = 48 * 1024 * 1024


def pack_kernel(q_ref, k_ref, v_ref, g_ref, even_ref, odd_ref):
    for slot, ref in enumerate((q_ref, k_ref, v_ref, g_ref)):
        for peer in range(SHARDS):
            even_ref[peer, slot] = ref[:, pl.ds(2 * peer * HD, HD)]
            odd_ref[peer, slot] = ref[:, pl.ds((2 * peer + 1) * HD, HD)]


def pack(queries, key_rows, value_rows, out_grad):
    shape = jax.ShapeDtypeStruct((SHARDS, 4, SHARD, HD), jnp.bfloat16)
    return pl.pallas_call(
        pack_kernel,
        out_shape=(shape, shape),
        compiler_params=pltpu.CompilerParams(vmem_limit_bytes=VMEM_LIMIT),
        name="pack",
    )(queries, key_rows, value_rows, out_grad)


def unpack_kernel(even_ref, odd_ref, dq_ref, dk_ref, dv_ref):
    for slot, ref in enumerate((dq_ref, dk_ref, dv_ref)):
        for peer in range(SHARDS):
            ref[:, pl.ds(2 * peer * HD, HD)] = even_ref[peer, slot]
            ref[:, pl.ds((2 * peer + 1) * HD, HD)] = odd_ref[peer, slot]


def unpack(even, odd):
    shape = jax.ShapeDtypeStruct((SHARD, 2 * SHARDS * HD), jnp.bfloat16)
    return pl.pallas_call(
        unpack_kernel,
        out_shape=(shape, shape, shape),
        compiler_params=pltpu.CompilerParams(vmem_limit_bytes=VMEM_LIMIT),
        name="unpack",
    )(even, odd)


def document_owner(first, end):
    first_block = first // BLOCK
    last_block = (end - 1) // BLOCK
    edge = last_block * BLOCK
    span = last_block - first_block
    right_larger = (end - edge) > (edge - first)
    return first_block + jnp.where(
        span == 2, 1, jnp.where((span == 1) & right_larger, 1, 0)
    )


def attention_kernel(
    bounds_ref, left_ref, own_ref, right_ref,
    left_out, own_out, right_out,
    rows, grads, q_doc, k_doc, v_doc, g_doc, dk_acc, dv_acc, s_buf, p_buf,
):
    me = lax.axis_index("ctx")
    window = (me - 1) * BLOCK
    pieces = ((left_ref, left_out), (own_ref, own_out), (right_ref, right_out))

    def count(doc, carry):
        lo, hi = carry
        owner = document_owner(bounds_ref[doc], bounds_ref[doc + 1])
        return lo + jnp.where(owner < me, 1, 0), hi + jnp.where(owner <= me, 1, 0)

    doc_lo, doc_hi = lax.fori_loop(0, NDOC, count, (jnp.int32(0), jnp.int32(0)))
    row_lo = bounds_ref[doc_lo] - window
    row_hi = bounds_ref[doc_hi] - window
    some = doc_hi > doc_lo

    for piece, (ref, _) in enumerate(pieces):
        lo = jnp.clip(row_lo // SHARD - piece * SHARDS, 0, SHARDS)
        hi = jnp.clip((row_hi + SHARD - 1) // SHARD - piece * SHARDS, 0, SHARDS)
        hi = jnp.where(some, hi, lo)

        def load(shard, carry, ref=ref, piece=piece):
            at = pl.multiple_of((piece * SHARDS + shard) * SHARD, SHARD)
            for slot in range(4):
                rows[slot, pl.ds(at, SHARD), :] = ref[shard, slot].astype(jnp.float32)
            return carry

        lax.fori_loop(lo, hi, load, 0)

    zero_tile = jnp.zeros((STEP, HD), jnp.float32)

    def clear(tile, carry):
        at = pl.multiple_of(tile * STEP, STEP)
        for slot in range(3):
            grads[slot, pl.ds(at, STEP), :] = zero_tile
        return carry

    lax.fori_loop(0, 3 * BLOCK // STEP, clear, 0)

    def one_document(doc, carry):
        first = bounds_ref[doc] - window
        length = bounds_ref[doc + 1] - bounds_ref[doc]
        tiles = (length + STEP - 1) // STEP

        def fetch(tile, carry):
            at = pl.multiple_of(tile * STEP, STEP)
            inside = lax.broadcasted_iota(jnp.int32, (STEP, HD), 0) + at < length
            for slot, ref in enumerate((q_doc, k_doc, v_doc, g_doc)):
                part = rows[slot, pl.ds(first + at, STEP), :]
                ref[pl.ds(at, STEP), :] = jnp.where(inside, part, 0.0).astype(jnp.bfloat16)
            dk_acc[pl.ds(at, STEP), :] = zero_tile
            dv_acc[pl.ds(at, STEP), :] = zero_tile
            return carry

        lax.fori_loop(0, tiles, fetch, 0)

        def query_tile(tile, carry):
            at = pl.multiple_of(tile * STEP, STEP)
            q = q_doc[pl.ds(at, STEP), :]
            g = g_doc[pl.ds(at, STEP), :]

            def stats(key_tile, carry):
                top, total, dot = carry
                to = pl.multiple_of(key_tile * STEP, STEP)
                k = k_doc[pl.ds(to, STEP), :]
                v = v_doc[pl.ds(to, STEP), :]
                s = lax.dot_general(k, q, (((1,), (1,)), ((), ())), preferred_element_type=jnp.float32)
                p = lax.dot_general(v, g, (((1,), (1,)), ((), ())), preferred_element_type=jnp.float32)
                inside = lax.broadcasted_iota(jnp.int32, (STEP, STEP), 0) + to < length
                s = jnp.where(inside, s * (SCALE * LOG2E), LOW)
                s_buf[pl.ds(to, STEP), :] = s
                p_buf[pl.ds(to, STEP), :] = p
                new_top = jnp.maximum(top, jnp.max(s, axis=0, keepdims=True))
                shrink = jnp.exp2(top - new_top)
                e = jnp.exp2(s - new_top)
                total = total * shrink + jnp.sum(e, axis=0, keepdims=True)
                dot = dot * shrink + jnp.sum(e * p, axis=0, keepdims=True)
                return new_top, total, dot

            flat = jnp.zeros((1, STEP), jnp.float32)
            top, total, dot = lax.fori_loop(0, tiles, stats, (flat + LOW, flat, flat))
            norm = top + jnp.log2(total)
            delta = dot / total

            def gradients(key_tile, dq):
                to = pl.multiple_of(key_tile * STEP, STEP)
                k = k_doc[pl.ds(to, STEP), :]
                e = jnp.exp2(s_buf[pl.ds(to, STEP), :] - norm)
                score = (e * (p_buf[pl.ds(to, STEP), :] - delta)).astype(jnp.bfloat16)
                weights = e.astype(jnp.bfloat16)
                dv_acc[pl.ds(to, STEP), :] += lax.dot_general(
                    weights, g, (((1,), (0,)), ((), ())), preferred_element_type=jnp.float32)
                dk_acc[pl.ds(to, STEP), :] += lax.dot_general(
                    score, q, (((1,), (0,)), ((), ())), preferred_element_type=jnp.float32)
                return dq + lax.dot_general(
                    score, k, (((0,), (0,)), ((), ())), preferred_element_type=jnp.float32)

            dq = lax.fori_loop(0, tiles, gradients, zero_tile)
            grads[0, pl.ds(first + at, STEP), :] = dq * SCALE
            return carry

        lax.fori_loop(0, tiles, query_tile, 0)

        def put(tile, carry):
            at = pl.multiple_of(tile * STEP, STEP)
            grads[1, pl.ds(first + at, STEP), :] = dk_acc[pl.ds(at, STEP), :] * SCALE
            grads[2, pl.ds(first + at, STEP), :] = dv_acc[pl.ds(at, STEP), :]
            return carry

        lax.fori_loop(0, tiles, put, 0)
        return carry

    lax.fori_loop(doc_lo, doc_hi, one_document, 0)

    for piece, (_, ref) in enumerate(pieces):

        def store(shard, carry, ref=ref, piece=piece):
            at = pl.multiple_of((piece * SHARDS + shard) * SHARD, SHARD)
            for slot in range(3):
                ref[shard, slot] = grads[slot, pl.ds(at, SHARD), :].astype(jnp.bfloat16)
            return carry

        lax.fori_loop(0, SHARDS, store, 0)


def attention(bounds, left, own, right):
    shape = jax.ShapeDtypeStruct((SHARDS, 3, SHARD, HD), jnp.bfloat16)
    vmem = pl.BlockSpec(memory_space=pltpu.VMEM)
    padded = 3 * BLOCK + STEP
    return pl.pallas_call(
        attention_kernel,
        out_shape=(shape, shape, shape),
        in_specs=[pl.BlockSpec(memory_space=pltpu.SMEM), vmem, vmem, vmem],
        out_specs=(vmem, vmem, vmem),
        scratch_shapes=[
            pltpu.VMEM((4, padded, HD), jnp.float32),
            pltpu.VMEM((3, padded, HD), jnp.float32),
            pltpu.VMEM((MOST, HD), jnp.bfloat16),
            pltpu.VMEM((MOST, HD), jnp.bfloat16),
            pltpu.VMEM((MOST, HD), jnp.bfloat16),
            pltpu.VMEM((MOST, HD), jnp.bfloat16),
            pltpu.VMEM((MOST, HD), jnp.float32),
            pltpu.VMEM((MOST, HD), jnp.float32),
            pltpu.VMEM((MOST, STEP), jnp.float32),
            pltpu.VMEM((MOST, STEP), jnp.float32),
        ],
        compiler_params=pltpu.CompilerParams(vmem_limit_bytes=VMEM_LIMIT),
        cost_estimate=pl.CostEstimate(
            flops=5 * 2 * MOST * MOST * HD, bytes_accessed=6 * 1024 * 1024, transcendentals=2 * MOST * MOST
        ),
        name="attention",
    )(bounds, left, own, right)


def from_left(shard):
    devices = lax.axis_size("ctx")
    return lax.ppermute(shard, "ctx", [(i, i + 1) for i in range(devices - 1)])


def from_right(shard):
    devices = lax.axis_size("ctx")
    return lax.ppermute(shard, "ctx", [(i + 1, i) for i in range(devices - 1)])


def swap_heads(shard):
    return lax.all_to_all(shard, "head", split_axis=0, concat_axis=0, tiled=True)


def on_device(queries, key_rows, value_rows, out_grad, bounds):
    done = []
    for packed in pack(queries, key_rows, value_rows, out_grad):
        own = swap_heads(packed)
        left = from_left(own)
        right = from_right(own)
        left_grad, own_grad, right_grad = attention(bounds, left, own, right)
        own_grad = own_grad + from_left(right_grad) + from_right(left_grad)
        done.append(swap_heads(own_grad))
    return unpack(*done)


def solution(mesh):
    rows = P(("ctx", "head"), None)
    return jax.shard_map(
        on_device,
        mesh=mesh,
        in_specs=(rows, rows, rows, rows, P()),
        out_specs=(rows, rows, rows),
        check_vma=False,
    )
```

```python
import jax
import jax.numpy as jnp
from jax import lax
from jax.experimental import pallas as pl
from jax.experimental.pallas import tpu as pltpu
from jax.sharding import PartitionSpec as P

HD = 128
NDOC = 64
BLOCK = 1024
SHARD = 128
SHARDS = BLOCK // SHARD
STEP = 256
MOST = 2048
SCALE = HD ** -0.5
LOG2E = 1.4426950408889634
LOW = -1.0e30
VMEM_LIMIT = 48 * 1024 * 1024


def pack_kernel(q_ref, k_ref, v_ref, g_ref, even_ref, odd_ref):
    for slot, ref in enumerate((q_ref, k_ref, v_ref, g_ref)):
        for peer in range(SHARDS):
            even_ref[peer, slot] = ref[:, pl.ds(2 * peer * HD, HD)]
            odd_ref[peer, slot] = ref[:, pl.ds((2 * peer + 1) * HD, HD)]


def pack(queries, key_rows, value_rows, out_grad):
    shape = jax.ShapeDtypeStruct((SHARDS, 4, SHARD, HD), jnp.bfloat16)
    return pl.pallas_call(
        pack_kernel,
        out_shape=(shape, shape),
        compiler_params=pltpu.CompilerParams(vmem_limit_bytes=VMEM_LIMIT),
        name="pack",
    )(queries, key_rows, value_rows, out_grad)


def unpack_kernel(even_ref, odd_ref, dq_ref, dk_ref, dv_ref):
    for slot, ref in enumerate((dq_ref, dk_ref, dv_ref)):
        for peer in range(SHARDS):
            ref[:, pl.ds(2 * peer * HD, HD)] = even_ref[peer, slot]
            ref[:, pl.ds((2 * peer + 1) * HD, HD)] = odd_ref[peer, slot]


def unpack(even, odd):
    shape = jax.ShapeDtypeStruct((SHARD, 2 * SHARDS * HD), jnp.bfloat16)
    return pl.pallas_call(
        unpack_kernel,
        out_shape=(shape, shape, shape),
        compiler_params=pltpu.CompilerParams(vmem_limit_bytes=VMEM_LIMIT),
        name="unpack",
    )(even, odd)


def document_owner(first, end):
    first_block = first // BLOCK
    last_block = (end - 1) // BLOCK
    edge = last_block * BLOCK
    span = last_block - first_block
    right_larger = (end - edge) > (edge - first)
    return first_block + jnp.where(
        span == 2, 1, jnp.where((span == 1) & right_larger, 1, 0)
    )


def attention_kernel(
    bounds_ref, left_ref, own_ref, right_ref,
    left_out, own_out, right_out,
    rows, grads, q_doc, k_doc, v_doc, g_doc, kt_doc, dk_acc, dv_acc, dq_acc, e_buf, p_buf, tops,
):
    me = lax.axis_index("ctx")
    window = (me - 1) * BLOCK
    pieces = ((left_ref, left_out), (own_ref, own_out), (right_ref, right_out))

    def count(doc, carry):
        lo, hi = carry
        owner = document_owner(bounds_ref[doc], bounds_ref[doc + 1])
        return lo + jnp.where(owner < me, 1, 0), hi + jnp.where(owner <= me, 1, 0)

    doc_lo, doc_hi = lax.fori_loop(0, NDOC, count, (jnp.int32(0), jnp.int32(0)))
    row_lo = bounds_ref[doc_lo] - window
    row_hi = bounds_ref[doc_hi] - window
    some = doc_hi > doc_lo

    for piece, (ref, _) in enumerate(pieces):
        lo = jnp.clip(row_lo // SHARD - piece * SHARDS, 0, SHARDS)
        hi = jnp.clip((row_hi + SHARD - 1) // SHARD - piece * SHARDS, 0, SHARDS)
        hi = jnp.where(some, hi, lo)

        def load(shard, carry, ref=ref, piece=piece):
            at = pl.multiple_of((piece * SHARDS + shard) * SHARD, SHARD)
            for slot in range(4):
                rows[slot, pl.ds(at, SHARD), :] = ref[shard, slot].astype(jnp.float32)
            return carry

        lax.fori_loop(lo, hi, load, 0)

    zero_tile = jnp.zeros((STEP, HD), jnp.float32)

    def clear(tile, carry):
        at = pl.multiple_of(tile * STEP, STEP)
        for slot in range(3):
            grads[slot, pl.ds(at, STEP), :] = zero_tile
        return carry

    lax.fori_loop(0, 3 * BLOCK // STEP, clear, 0)

    def one_document(doc, carry):
        first = bounds_ref[doc] - window
        length = bounds_ref[doc + 1] - bounds_ref[doc]
        tiles = (length + STEP - 1) // STEP

        def fetch(tile, carry):
            at = pl.multiple_of(tile * STEP, STEP)
            inside = lax.broadcasted_iota(jnp.int32, (STEP, HD), 0) + at < length
            for slot, ref in enumerate((q_doc, k_doc, v_doc, g_doc)):
                part = jnp.where(inside, rows[slot, pl.ds(first + at, STEP), :], 0.0)
                ref[pl.ds(at, STEP), :] = part.astype(jnp.bfloat16)
                if slot == 1:
                    kt_doc[:, pl.ds(at, STEP)] = part.T.astype(jnp.bfloat16)
            dk_acc[pl.ds(at, STEP), :] = zero_tile
            dv_acc[pl.ds(at, STEP), :] = zero_tile
            return carry

        lax.fori_loop(0, tiles, fetch, 0)

        def stats(tile, key_tile, carry, last):
            top, total, dot = carry
            at = pl.multiple_of(tile * STEP, STEP)
            to = pl.multiple_of(key_tile * STEP, STEP)
            slot = lax.rem(tile, 2)
            s = lax.dot_general(
                k_doc[pl.ds(to, STEP), :], q_doc[pl.ds(at, STEP), :],
                (((1,), (1,)), ((), ())), preferred_element_type=jnp.float32) * (SCALE * LOG2E)
            p = lax.dot_general(
                v_doc[pl.ds(to, STEP), :], g_doc[pl.ds(at, STEP), :],
                (((1,), (1,)), ((), ())), preferred_element_type=jnp.float32)
            if last:
                inside = lax.broadcasted_iota(jnp.int32, (STEP, STEP), 0) + to < length
                s = jnp.where(inside, s, LOW)
            s = s.reshape(STEP // 8, 8, STEP)
            new_top = jnp.maximum(top, jnp.max(s, axis=0))
            e = jnp.exp2(s - new_top[None])
            e_buf[slot, pl.ds(to, STEP), :] = e.reshape(STEP, STEP)
            p_buf[slot, pl.ds(to, STEP), :] = p
            tops[slot, key_tile] = new_top
            shrink = jnp.exp2(top - new_top)
            total = total * shrink + jnp.sum(e, axis=0)
            dot = dot * shrink + jnp.sum(e * p.reshape(STEP // 8, 8, STEP), axis=0)
            return new_top, total, dot

        def gradients(tile, key_tile, norm, delta):
            at = pl.multiple_of(tile * STEP, STEP)
            to = pl.multiple_of(key_tile * STEP, STEP)
            slot = lax.rem(tile, 2)
            factor = jnp.exp2(tops[slot, key_tile] - norm)
            e = e_buf[slot, pl.ds(to, STEP), :].reshape(STEP // 8, 8, STEP) * factor[None]
            p = p_buf[slot, pl.ds(to, STEP), :].reshape(STEP // 8, 8, STEP)
            score = (e * (p - delta[None])).reshape(STEP, STEP).astype(jnp.bfloat16)
            weights = e.reshape(STEP, STEP).astype(jnp.bfloat16)
            dv_acc[pl.ds(to, STEP), :] += jnp.dot(
                weights, g_doc[pl.ds(at, STEP), :], preferred_element_type=jnp.float32)
            dk_acc[pl.ds(to, STEP), :] += jnp.dot(
                score, q_doc[pl.ds(at, STEP), :], preferred_element_type=jnp.float32)
            dq_acc[...] += jnp.dot(
                kt_doc[:, pl.ds(to, STEP)], score, preferred_element_type=jnp.float32)

        flat = jnp.zeros((8, STEP), jnp.float32)
        fresh = (flat + LOW, flat, flat)

        def joined(top, total, dot):
            peak = jnp.max(top, axis=0, keepdims=True)
            weight = jnp.exp2(top - peak)
            total = jnp.sum(total * weight, axis=0, keepdims=True)
            dot = jnp.sum(dot * weight, axis=0, keepdims=True)
            return flat + (peak + jnp.log2(total)), flat + dot / total

        def put_queries(tile):
            at = pl.multiple_of(tile * STEP, STEP)
            grads[0, pl.ds(first + at, STEP), :] = dq_acc[...].T * SCALE
            dq_acc[...] = jnp.zeros((HD, STEP), jnp.float32)

        dq_acc[...] = jnp.zeros((HD, STEP), jnp.float32)
        carry_now = lax.fori_loop(0, tiles - 1, lambda c, now: stats(0, c, now, False), fresh)
        norm_now = joined(*stats(0, tiles - 1, carry_now, True))

        def query_tile(tile, norms):
            norm, delta = norms

            def both(key_tile, now):
                gradients(tile - 1, key_tile, norm, delta)
                return stats(tile, key_tile, now, False)

            now = lax.fori_loop(0, tiles - 1, both, fresh)
            gradients(tile - 1, tiles - 1, norm, delta)
            now = stats(tile, tiles - 1, now, True)
            put_queries(tile - 1)
            return joined(*now)

        norm, delta = lax.fori_loop(1, tiles, query_tile, norm_now)

        def rest(key_tile, carry):
            gradients(tiles - 1, key_tile, norm, delta)
            return carry

        lax.fori_loop(0, tiles, rest, 0)
        put_queries(tiles - 1)

        def put(tile, carry):
            at = pl.multiple_of(tile * STEP, STEP)
            grads[1, pl.ds(first + at, STEP), :] = dk_acc[pl.ds(at, STEP), :] * SCALE
            grads[2, pl.ds(first + at, STEP), :] = dv_acc[pl.ds(at, STEP), :]
            return carry

        lax.fori_loop(0, tiles, put, 0)
        return carry

    lax.fori_loop(doc_lo, doc_hi, one_document, 0)

    for piece, (_, ref) in enumerate(pieces):

        def store(shard, carry, ref=ref, piece=piece):
            at = pl.multiple_of((piece * SHARDS + shard) * SHARD, SHARD)
            for slot in range(3):
                ref[shard, slot] = grads[slot, pl.ds(at, SHARD), :].astype(jnp.bfloat16)
            return carry

        lax.fori_loop(0, SHARDS, store, 0)


def attention(bounds, left, own, right):
    shape = jax.ShapeDtypeStruct((SHARDS, 3, SHARD, HD), jnp.bfloat16)
    vmem = pl.BlockSpec(memory_space=pltpu.VMEM)
    padded = 3 * BLOCK + STEP
    return pl.pallas_call(
        attention_kernel,
        out_shape=(shape, shape, shape),
        in_specs=[pl.BlockSpec(memory_space=pltpu.SMEM), vmem, vmem, vmem],
        out_specs=(vmem, vmem, vmem),
        scratch_shapes=[
            pltpu.VMEM((4, padded, HD), jnp.float32),
            pltpu.VMEM((3, padded, HD), jnp.float32),
            pltpu.VMEM((MOST, HD), jnp.bfloat16),
            pltpu.VMEM((MOST, HD), jnp.bfloat16),
            pltpu.VMEM((MOST, HD), jnp.bfloat16),
            pltpu.VMEM((MOST, HD), jnp.bfloat16),
            pltpu.VMEM((HD, MOST), jnp.bfloat16),
            pltpu.VMEM((MOST, HD), jnp.float32),
            pltpu.VMEM((MOST, HD), jnp.float32),
            pltpu.VMEM((HD, STEP), jnp.float32),
            pltpu.VMEM((2, MOST, STEP), jnp.float32),
            pltpu.VMEM((2, MOST, STEP), jnp.float32),
            pltpu.VMEM((2, MOST // STEP, 8, STEP), jnp.float32),
        ],
        compiler_params=pltpu.CompilerParams(vmem_limit_bytes=VMEM_LIMIT),
        cost_estimate=pl.CostEstimate(
            flops=5 * 2 * MOST * MOST * HD, bytes_accessed=6 * 1024 * 1024, transcendentals=2 * MOST * MOST
        ),
        name="attention",
    )(bounds, left, own, right)


def from_left(shard):
    devices = lax.axis_size("ctx")
    return lax.ppermute(shard, "ctx", [(i, i + 1) for i in range(devices - 1)])


def from_right(shard):
    devices = lax.axis_size("ctx")
    return lax.ppermute(shard, "ctx", [(i + 1, i) for i in range(devices - 1)])


def swap_heads(shard):
    return lax.all_to_all(shard, "head", split_axis=0, concat_axis=0, tiled=True)


def on_device(queries, key_rows, value_rows, out_grad, bounds):
    done = []
    for packed in pack(queries, key_rows, value_rows, out_grad):
        own = swap_heads(packed)
        left = from_left(own)
        right = from_right(own)
        left_grad, own_grad, right_grad = attention(bounds, left, own, right)
        own_grad = own_grad + from_left(right_grad) + from_right(left_grad)
        done.append(swap_heads(own_grad))
    return unpack(*done)


def solution(mesh):
    rows = P(("ctx", "head"), None)
    return jax.shard_map(
        on_device,
        mesh=mesh,
        in_specs=(rows, rows, rows, rows, P()),
        out_specs=(rows, rows, rows),
        check_vma=False,
    )
```

```python
import functools

import jax
import jax.numpy as jnp
from jax import lax
from jax.experimental import pallas as pl
from jax.experimental.pallas import tpu as pltpu
from jax.sharding import PartitionSpec as P

HD = 128
NDOC = 64
BLOCK = 1024
SHARD = 128
SHARDS = BLOCK // SHARD
STEP = 256
MOST = 2048
SCALE = HD ** -0.5
LOG2E = 1.4426950408889634
LOW = -1.0e30
VMEM_LIMIT = 48 * 1024 * 1024


def pack_kernel(parity, q_ref, k_ref, v_ref, g_ref, out_ref, sems):
    copies = []
    for slot, ref in enumerate((q_ref, k_ref, v_ref, g_ref)):
        for peer in range(SHARDS):
            copies.append(pltpu.make_async_copy(
                ref.at[:, pl.ds((2 * peer + parity) * HD, HD)], out_ref.at[peer, slot],
                sems.at[slot * SHARDS + peer]))
    for copy in copies:
        copy.start()
    for copy in copies:
        copy.wait()


def pack(parity, queries, key_rows, value_rows, out_grad):
    hbm = pl.BlockSpec(memory_space=pl.ANY)
    return pl.pallas_call(
        functools.partial(pack_kernel, parity),
        out_shape=jax.ShapeDtypeStruct((SHARDS, 4, SHARD, HD), jnp.bfloat16),
        in_specs=[hbm] * 4,
        out_specs=hbm,
        scratch_shapes=[pltpu.SemaphoreType.DMA((4 * SHARDS,))],
        cost_estimate=pl.CostEstimate(flops=0, bytes_accessed=8 * SHARDS * SHARD * HD * 2, transcendentals=0),
        name="pack",
    )(queries, key_rows, value_rows, out_grad)


def unpack_kernel(even_ref, odd_ref, dq_ref, dk_ref, dv_ref):
    for slot, ref in enumerate((dq_ref, dk_ref, dv_ref)):
        for peer in range(SHARDS):
            ref[:, pl.ds(2 * peer * HD, HD)] = even_ref[peer, slot]
            ref[:, pl.ds((2 * peer + 1) * HD, HD)] = odd_ref[peer, slot]


def unpack(even, odd):
    shape = jax.ShapeDtypeStruct((SHARD, 2 * SHARDS * HD), jnp.bfloat16)
    return pl.pallas_call(
        unpack_kernel,
        out_shape=(shape, shape, shape),
        compiler_params=pltpu.CompilerParams(vmem_limit_bytes=VMEM_LIMIT),
        name="unpack",
    )(even, odd)


def document_owner(first, end):
    first_block = first // BLOCK
    last_block = (end - 1) // BLOCK
    edge = last_block * BLOCK
    span = last_block - first_block
    right_larger = (end - edge) > (edge - first)
    return first_block + jnp.where(
        span == 2, 1, jnp.where((span == 1) & right_larger, 1, 0)
    )


def attention_kernel(
    bounds_ref, left_ref, own_ref, right_ref,
    left_out, own_out, right_out,
    rows, grads, q_doc, k_doc, v_doc, g_doc, kt_doc, dk_acc, dv_acc, dq_acc, e_buf, p_buf, tops,
):
    me = lax.axis_index("ctx")
    window = (me - 1) * BLOCK
    pieces = ((left_ref, left_out), (own_ref, own_out), (right_ref, right_out))

    def count(doc, carry):
        lo, hi = carry
        owner = document_owner(bounds_ref[doc], bounds_ref[doc + 1])
        return lo + jnp.where(owner < me, 1, 0), hi + jnp.where(owner <= me, 1, 0)

    doc_lo, doc_hi = lax.fori_loop(0, NDOC, count, (jnp.int32(0), jnp.int32(0)))
    row_lo = bounds_ref[doc_lo] - window
    row_hi = bounds_ref[doc_hi] - window
    some = doc_hi > doc_lo

    shard_lo = jnp.where(some, row_lo // SHARD, 0)
    shard_hi = jnp.where(some, (row_hi + SHARD - 1) // SHARD, 0)
    zero_tile = jnp.zeros((STEP, HD), jnp.float32)
    zero_shard = jnp.zeros((SHARD, HD), jnp.float32)

    for piece, (ref, _) in enumerate(pieces):
        lo = jnp.clip(shard_lo - piece * SHARDS, 0, SHARDS)
        hi = jnp.clip(shard_hi - piece * SHARDS, 0, SHARDS)

        def load(shard, carry, ref=ref, piece=piece):
            at = pl.multiple_of((piece * SHARDS + shard) * SHARD, SHARD)
            for slot in range(4):
                rows[slot, pl.ds(at, SHARD), :] = ref[shard, slot].astype(jnp.float32)
            return carry

        lax.fori_loop(lo, hi, load, 0)

    for edge in (shard_lo, jnp.maximum(shard_hi - 1, 0)):
        at = pl.multiple_of(edge * SHARD, SHARD)
        for slot in range(3):
            grads[slot, pl.ds(at, SHARD), :] = zero_shard

    def one_document(doc, carry):
        first = bounds_ref[doc] - window
        length = bounds_ref[doc + 1] - bounds_ref[doc]
        tiles = (length + STEP - 1) // STEP

        def fetch(tile, carry):
            at = pl.multiple_of(tile * STEP, STEP)
            inside = lax.broadcasted_iota(jnp.int32, (STEP, HD), 0) + at < length
            for slot, ref in enumerate((q_doc, k_doc, v_doc, g_doc)):
                part = jnp.where(inside, rows[slot, pl.ds(first + at, STEP), :], 0.0)
                ref[pl.ds(at, STEP), :] = part.astype(jnp.bfloat16)
                if slot == 1:
                    kt_doc[:, pl.ds(at, STEP)] = part.T.astype(jnp.bfloat16)
            dk_acc[pl.ds(at, STEP), :] = zero_tile
            dv_acc[pl.ds(at, STEP), :] = zero_tile
            return carry

        lax.fori_loop(0, tiles, fetch, 0)

        def stats(tile, to, size, carry, last):
            top, total, dot = carry
            at = pl.multiple_of(tile * STEP, STEP)
            slot = lax.rem(tile, 2)
            s = lax.dot_general(
                k_doc[pl.ds(to, size), :], q_doc[pl.ds(at, STEP), :],
                (((1,), (1,)), ((), ())), preferred_element_type=jnp.float32) * (SCALE * LOG2E)
            p = lax.dot_general(
                v_doc[pl.ds(to, size), :], g_doc[pl.ds(at, STEP), :],
                (((1,), (1,)), ((), ())), preferred_element_type=jnp.float32)
            if last:
                inside = lax.broadcasted_iota(jnp.int32, (size, STEP), 0) + to < length
                s = jnp.where(inside, s, LOW)
            s = s.reshape(size // 8, 8, STEP)
            new_top = jnp.maximum(top, jnp.max(s, axis=0))
            e = jnp.exp2(s - new_top[None])
            e_buf[slot, pl.ds(to, size), :] = e.reshape(size, STEP)
            p_buf[slot, pl.ds(to, size), :] = p
            tops[slot, to // STEP] = new_top
            shrink = jnp.exp2(top - new_top)
            total = total * shrink + jnp.sum(e, axis=0)
            dot = dot * shrink + jnp.sum(e * p.reshape(size // 8, 8, STEP), axis=0)
            return new_top, total, dot

        def gradients(tile, to, size, norm, delta):
            at = pl.multiple_of(tile * STEP, STEP)
            slot = lax.rem(tile, 2)
            factor = jnp.exp2(tops[slot, to // STEP] - norm)
            e = e_buf[slot, pl.ds(to, size), :].reshape(size // 8, 8, STEP) * factor[None]
            p = p_buf[slot, pl.ds(to, size), :].reshape(size // 8, 8, STEP)
            score = (e * (p - delta[None])).reshape(size, STEP).astype(jnp.bfloat16)
            weights = e.reshape(size, STEP).astype(jnp.bfloat16)
            dv_acc[pl.ds(to, size), :] += jnp.dot(
                weights, g_doc[pl.ds(at, STEP), :], preferred_element_type=jnp.float32)
            dk_acc[pl.ds(to, size), :] += jnp.dot(
                score, q_doc[pl.ds(at, STEP), :], preferred_element_type=jnp.float32)
            dq_acc[...] += jnp.dot(
                kt_doc[:, pl.ds(to, size)], score, preferred_element_type=jnp.float32)

        pairs = (tiles - 1) // 2
        two_left = 1 - lax.rem(tiles, 2)

        def over_keys(body, carry):
            carry = lax.fori_loop(
                0, pairs, lambda c, now: body(pl.multiple_of(c * 2 * STEP, STEP), 2 * STEP, now, False), carry)
            to = pl.multiple_of(pairs * 2 * STEP, STEP)
            carry = lax.fori_loop(0, two_left, lambda c, now: body(to, 2 * STEP, now, True), carry)
            return lax.fori_loop(0, 1 - two_left, lambda c, now: body(to, STEP, now, True), carry)

        flat = jnp.zeros((8, STEP), jnp.float32)
        fresh = (flat + LOW, flat, flat)

        def joined(top, total, dot):
            peak = jnp.max(top, axis=0, keepdims=True)
            weight = jnp.exp2(top - peak)
            total = jnp.sum(total * weight, axis=0, keepdims=True)
            dot = jnp.sum(dot * weight, axis=0, keepdims=True)
            return flat + (peak + jnp.log2(total)), flat + dot / total

        def put_queries(tile):
            at = pl.multiple_of(tile * STEP, STEP)
            grads[0, pl.ds(first + at, STEP), :] = dq_acc[...].T * SCALE
            dq_acc[...] = jnp.zeros((HD, STEP), jnp.float32)

        dq_acc[...] = jnp.zeros((HD, STEP), jnp.float32)
        norm_now = joined(*over_keys(lambda to, size, now, last: stats(0, to, size, now, last), fresh))

        def query_tile(tile, norms):
            norm, delta = norms

            def both(to, size, now, last):
                gradients(tile - 1, to, size, norm, delta)
                return stats(tile, to, size, now, last)

            now = over_keys(both, fresh)
            put_queries(tile - 1)
            return joined(*now)

        norm, delta = lax.fori_loop(1, tiles, query_tile, norm_now)

        def rest(to, size, now, last):
            gradients(tiles - 1, to, size, norm, delta)
            return now

        over_keys(rest, 0)
        put_queries(tiles - 1)

        def put(tile, carry):
            at = pl.multiple_of(tile * STEP, STEP)
            grads[1, pl.ds(first + at, STEP), :] = dk_acc[pl.ds(at, STEP), :] * SCALE
            grads[2, pl.ds(first + at, STEP), :] = dv_acc[pl.ds(at, STEP), :]
            return carry

        lax.fori_loop(0, tiles, put, 0)
        return carry

    lax.fori_loop(doc_lo, doc_hi, one_document, 0)

    for piece, (_, ref) in enumerate(pieces):
        lo = jnp.clip(shard_lo - piece * SHARDS, 0, SHARDS)
        hi = jnp.clip(shard_hi - piece * SHARDS, 0, SHARDS)

        def empty(shard, carry, ref=ref):
            for slot in range(3):
                ref[shard, slot] = zero_shard.astype(jnp.bfloat16)
            return carry

        def store(shard, carry, ref=ref, piece=piece):
            at = pl.multiple_of((piece * SHARDS + shard) * SHARD, SHARD)
            for slot in range(3):
                ref[shard, slot] = grads[slot, pl.ds(at, SHARD), :].astype(jnp.bfloat16)
            return carry

        lax.fori_loop(0, lo, empty, 0)
        lax.fori_loop(lo, hi, store, 0)
        lax.fori_loop(hi, SHARDS, empty, 0)


def attention(bounds, left, own, right):
    shape = jax.ShapeDtypeStruct((SHARDS, 3, SHARD, HD), jnp.bfloat16)
    vmem = pl.BlockSpec(memory_space=pltpu.VMEM)
    padded = 3 * BLOCK + STEP
    return pl.pallas_call(
        attention_kernel,
        out_shape=(shape, shape, shape),
        in_specs=[pl.BlockSpec(memory_space=pltpu.SMEM), vmem, vmem, vmem],
        out_specs=(vmem, vmem, vmem),
        scratch_shapes=[
            pltpu.VMEM((4, padded, HD), jnp.float32),
            pltpu.VMEM((3, padded, HD), jnp.float32),
            pltpu.VMEM((MOST, HD), jnp.bfloat16),
            pltpu.VMEM((MOST, HD), jnp.bfloat16),
            pltpu.VMEM((MOST, HD), jnp.bfloat16),
            pltpu.VMEM((MOST, HD), jnp.bfloat16),
            pltpu.VMEM((HD, MOST), jnp.bfloat16),
            pltpu.VMEM((MOST, HD), jnp.float32),
            pltpu.VMEM((MOST, HD), jnp.float32),
            pltpu.VMEM((HD, STEP), jnp.float32),
            pltpu.VMEM((2, MOST, STEP), jnp.float32),
            pltpu.VMEM((2, MOST, STEP), jnp.float32),
            pltpu.VMEM((2, MOST // STEP, 8, STEP), jnp.float32),
        ],
        compiler_params=pltpu.CompilerParams(vmem_limit_bytes=VMEM_LIMIT),
        cost_estimate=pl.CostEstimate(
            flops=5 * 2 * MOST * MOST * HD, bytes_accessed=6 * 1024 * 1024, transcendentals=2 * MOST * MOST
        ),
        name="attention",
    )(bounds, left, own, right)


def from_left(shard):
    devices = lax.axis_size("ctx")
    return lax.ppermute(shard, "ctx", [(i, i + 1) for i in range(devices - 1)])


def from_right(shard):
    devices = lax.axis_size("ctx")
    return lax.ppermute(shard, "ctx", [(i + 1, i) for i in range(devices - 1)])


def swap_heads(shard):
    return lax.all_to_all(shard, "head", split_axis=0, concat_axis=0, tiled=True)


def on_device(queries, key_rows, value_rows, out_grad, bounds):
    done = []
    for parity in range(2):
        own = swap_heads(pack(parity, queries, key_rows, value_rows, out_grad))
        left = from_left(own)
        right = from_right(own)
        left_grad, own_grad, right_grad = attention(bounds, left, own, right)
        own_grad = own_grad + from_left(right_grad) + from_right(left_grad)
        done.append(swap_heads(own_grad))
    return unpack(*done)


def solution(mesh):
    rows = P(("ctx", "head"), None)
    return jax.shard_map(
        on_device,
        mesh=mesh,
        in_specs=(rows, rows, rows, rows, P()),
        out_specs=(rows, rows, rows),
        check_vma=False,
    )
```

```python
import jax
import jax.numpy as jnp
from jax import lax
from jax.experimental import pallas as pl
from jax.experimental.pallas import tpu as pltpu
from jax.sharding import PartitionSpec as P

HD = 128
NDOC = 64
BLOCK = 1024
SHARD = 128
SHARDS = BLOCK // SHARD
STEP = 256
PART = 128
MOST = 2048
SCALE = HD ** -0.5
LOG2E = 1.4426950408889634
LOW = -1.0e30
VMEM_LIMIT = 48 * 1024 * 1024


def pack_kernel(q_ref, k_ref, v_ref, g_ref, even_ref, odd_ref, held, sems):
    copies = []
    for slot, ref in enumerate((q_ref, k_ref, v_ref, g_ref)):
        copies.append(pltpu.make_async_copy(ref, held.at[slot], sems.at[slot]))
    for copy in copies:
        copy.start()
    for slot, copy in enumerate(copies):
        copy.wait()
        for peer in range(SHARDS):
            even_ref[peer, slot] = held[slot, :, pl.ds(2 * peer * HD, HD)]
            odd_ref[peer, slot] = held[slot, :, pl.ds((2 * peer + 1) * HD, HD)]


def pack(queries, key_rows, value_rows, out_grad):
    shape = jax.ShapeDtypeStruct((SHARDS, 4, SHARD, HD), jnp.bfloat16)
    return pl.pallas_call(
        pack_kernel,
        out_shape=(shape, shape),
        in_specs=[pl.BlockSpec(memory_space=pl.ANY)] * 4,
        scratch_shapes=[
            pltpu.VMEM((4, SHARD, 2 * SHARDS * HD), jnp.bfloat16),
            pltpu.SemaphoreType.DMA((4,)),
        ],
        compiler_params=pltpu.CompilerParams(vmem_limit_bytes=VMEM_LIMIT),
        name="pack",
    )(queries, key_rows, value_rows, out_grad)


def unpack_kernel(even_ref, odd_ref, dq_ref, dk_ref, dv_ref):
    for slot, ref in enumerate((dq_ref, dk_ref, dv_ref)):
        for peer in range(SHARDS):
            ref[:, pl.ds(2 * peer * HD, HD)] = even_ref[peer, slot]
            ref[:, pl.ds((2 * peer + 1) * HD, HD)] = odd_ref[peer, slot]


def unpack(even, odd):
    shape = jax.ShapeDtypeStruct((SHARD, 2 * SHARDS * HD), jnp.bfloat16)
    return pl.pallas_call(
        unpack_kernel,
        out_shape=(shape, shape, shape),
        compiler_params=pltpu.CompilerParams(vmem_limit_bytes=VMEM_LIMIT),
        name="unpack",
    )(even, odd)


def document_owner(first, end):
    first_block = first // BLOCK
    last_block = (end - 1) // BLOCK
    edge = last_block * BLOCK
    span = last_block - first_block
    right_larger = (end - edge) > (edge - first)
    return first_block + jnp.where(
        span == 2, 1, jnp.where((span == 1) & right_larger, 1, 0)
    )


def attention_kernel(
    bounds_ref, left_ref, own_ref, right_ref,
    left_out, own_out, right_out,
    rows, grads, q_doc, k_doc, v_doc, g_doc, kt_doc, dk_acc, dv_acc, dq_acc, e_buf, p_buf, tops,
):
    me = lax.axis_index("ctx")
    window = (me - 1) * BLOCK
    pieces = ((left_ref, left_out), (own_ref, own_out), (right_ref, right_out))

    def count(doc, carry):
        lo, hi = carry
        owner = document_owner(bounds_ref[doc], bounds_ref[doc + 1])
        return lo + jnp.where(owner < me, 1, 0), hi + jnp.where(owner <= me, 1, 0)

    doc_lo, doc_hi = lax.fori_loop(0, NDOC, count, (jnp.int32(0), jnp.int32(0)))
    row_lo = bounds_ref[doc_lo] - window
    row_hi = bounds_ref[doc_hi] - window
    some = doc_hi > doc_lo

    shard_lo = jnp.where(some, row_lo // SHARD, 0)
    shard_hi = jnp.where(some, (row_hi + SHARD - 1) // SHARD, 0)
    zero_tile = jnp.zeros((STEP, HD), jnp.float32)
    zero_shard = jnp.zeros((SHARD, HD), jnp.float32)

    for piece, (ref, _) in enumerate(pieces):
        lo = jnp.clip(shard_lo - piece * SHARDS, 0, SHARDS)
        hi = jnp.clip(shard_hi - piece * SHARDS, 0, SHARDS)

        def load(shard, carry, ref=ref, piece=piece):
            at = pl.multiple_of((piece * SHARDS + shard) * SHARD, SHARD)
            for slot in range(4):
                rows[slot, pl.ds(at, SHARD), :] = ref[shard, slot].astype(jnp.float32)
            return carry

        lax.fori_loop(lo, hi, load, 0)

    for edge in (shard_lo, jnp.maximum(shard_hi - 1, 0)):
        at = pl.multiple_of(edge * SHARD, SHARD)
        for slot in range(3):
            grads[slot, pl.ds(at, SHARD), :] = zero_shard

    def one_document(doc, carry):
        first = bounds_ref[doc] - window
        length = bounds_ref[doc + 1] - bounds_ref[doc]
        tiles = (length + STEP - 1) // STEP

        def fetch(tile, carry):
            at = pl.multiple_of(tile * STEP, STEP)
            inside = lax.broadcasted_iota(jnp.int32, (STEP, HD), 0) + at < length
            for slot, ref in enumerate((q_doc, k_doc, v_doc, g_doc)):
                part = jnp.where(inside, rows[slot, pl.ds(first + at, STEP), :], 0.0)
                ref[pl.ds(at, STEP), :] = part.astype(jnp.bfloat16)
                if slot == 1:
                    kt_doc[:, pl.ds(at, STEP)] = part.T.astype(jnp.bfloat16)
            dk_acc[pl.ds(at, STEP), :] = zero_tile
            dv_acc[pl.ds(at, STEP), :] = zero_tile
            return carry

        lax.fori_loop(0, tiles, fetch, 0)

        def stats(tile, to, size, carry, last):
            at = pl.multiple_of(tile * STEP, STEP)
            s_all = lax.dot_general(
                k_doc[pl.ds(to, size), :], q_doc[pl.ds(at, STEP), :],
                (((1,), (1,)), ((), ())), preferred_element_type=jnp.float32)
            p_all = lax.dot_general(
                v_doc[pl.ds(to, size), :], g_doc[pl.ds(at, STEP), :],
                (((1,), (1,)), ((), ())), preferred_element_type=jnp.float32)
            for part in range(size // PART):
                top, total, dot = carry
                here = to + part * PART
                s = s_all[part * PART:(part + 1) * PART] * (SCALE * LOG2E)
                p = p_all[part * PART:(part + 1) * PART]
                if last:
                    inside = lax.broadcasted_iota(jnp.int32, (PART, STEP), 0) + here < length
                    s = jnp.where(inside, s, LOW)
                s = s.reshape(PART // 8, 8, STEP)
                new_top = jnp.maximum(top, jnp.max(s, axis=0))
                e = jnp.exp2(s - new_top[None])
                e_buf[pl.ds(here, PART), :] = e.reshape(PART, STEP)
                p_buf[pl.ds(here, PART), :] = p
                tops[to // PART + part] = new_top
                shrink = jnp.exp2(top - new_top)
                total = total * shrink + jnp.sum(e, axis=0)
                dot = dot * shrink + jnp.sum(e * p.reshape(PART // 8, 8, STEP), axis=0)
                carry = new_top, total, dot
            return carry

        def gradients(tile, to, size, norm, delta):
            at = pl.multiple_of(tile * STEP, STEP)
            weights, scores = [], []
            for part in range(size // PART):
                here = to + part * PART
                factor = jnp.exp2(tops[to // PART + part] - norm)
                e = e_buf[pl.ds(here, PART), :].reshape(PART // 8, 8, STEP) * factor[None]
                p = p_buf[pl.ds(here, PART), :].reshape(PART // 8, 8, STEP)
                scores.append((e * (p - delta[None])).reshape(PART, STEP).astype(jnp.bfloat16))
                weights.append(e.reshape(PART, STEP).astype(jnp.bfloat16))
            weights = jnp.concatenate(weights, axis=0)
            scores = jnp.concatenate(scores, axis=0)
            dv_acc[pl.ds(to, size), :] += jnp.dot(
                weights, g_doc[pl.ds(at, STEP), :], preferred_element_type=jnp.float32)
            dk_acc[pl.ds(to, size), :] += jnp.dot(
                scores, q_doc[pl.ds(at, STEP), :], preferred_element_type=jnp.float32)
            dq_acc[...] += jnp.dot(
                kt_doc[:, pl.ds(to, size)], scores, preferred_element_type=jnp.float32)

        pairs = (tiles - 1) // 2
        two_left = 1 - lax.rem(tiles, 2)

        def over_keys(body, carry):
            carry = lax.fori_loop(
                0, pairs, lambda c, now: body(pl.multiple_of(c * 2 * STEP, STEP), 2 * STEP, now, False), carry)
            to = pl.multiple_of(pairs * 2 * STEP, STEP)
            carry = lax.fori_loop(0, two_left, lambda c, now: body(to, 2 * STEP, now, True), carry)
            return lax.fori_loop(0, 1 - two_left, lambda c, now: body(to, STEP, now, True), carry)

        flat = jnp.zeros((8, STEP), jnp.float32)
        fresh = (flat + LOW, flat, flat)

        def joined(top, total, dot):
            peak = jnp.max(top, axis=0, keepdims=True)
            weight = jnp.exp2(top - peak)
            total = jnp.sum(total * weight, axis=0, keepdims=True)
            dot = jnp.sum(dot * weight, axis=0, keepdims=True)
            return flat + (peak + jnp.log2(total)), flat + dot / total

        def put_queries(tile):
            at = pl.multiple_of(tile * STEP, STEP)
            grads[0, pl.ds(first + at, STEP), :] = dq_acc[...].T * SCALE
            dq_acc[...] = jnp.zeros((HD, STEP), jnp.float32)

        dq_acc[...] = jnp.zeros((HD, STEP), jnp.float32)
        norm_now = joined(*over_keys(lambda to, size, now, last: stats(0, to, size, now, last), fresh))

        def query_tile(tile, norms):
            norm, delta = norms

            def both(to, size, now, last):
                gradients(tile - 1, to, size, norm, delta)
                return stats(tile, to, size, now, last)

            now = over_keys(both, fresh)
            put_queries(tile - 1)
            return joined(*now)

        norm, delta = lax.fori_loop(1, tiles, query_tile, norm_now)

        def rest(to, size, now, last):
            gradients(tiles - 1, to, size, norm, delta)
            return now

        over_keys(rest, 0)
        put_queries(tiles - 1)

        def put(tile, carry):
            at = pl.multiple_of(tile * STEP, STEP)
            grads[1, pl.ds(first + at, STEP), :] = dk_acc[pl.ds(at, STEP), :] * SCALE
            grads[2, pl.ds(first + at, STEP), :] = dv_acc[pl.ds(at, STEP), :]
            return carry

        lax.fori_loop(0, tiles, put, 0)
        return carry

    lax.fori_loop(doc_lo, doc_hi, one_document, 0)

    for piece, (_, ref) in enumerate(pieces):
        lo = jnp.clip(shard_lo - piece * SHARDS, 0, SHARDS)
        hi = jnp.clip(shard_hi - piece * SHARDS, 0, SHARDS)

        def empty(shard, carry, ref=ref):
            for slot in range(3):
                ref[shard, slot] = zero_shard.astype(jnp.bfloat16)
            return carry

        def store(shard, carry, ref=ref, piece=piece):
            at = pl.multiple_of((piece * SHARDS + shard) * SHARD, SHARD)
            for slot in range(3):
                ref[shard, slot] = grads[slot, pl.ds(at, SHARD), :].astype(jnp.bfloat16)
            return carry

        lax.fori_loop(0, lo, empty, 0)
        lax.fori_loop(lo, hi, store, 0)
        lax.fori_loop(hi, SHARDS, empty, 0)


def attention(bounds, left, own, right):
    shape = jax.ShapeDtypeStruct((SHARDS, 3, SHARD, HD), jnp.bfloat16)
    vmem = pl.BlockSpec(memory_space=pltpu.VMEM)
    padded = 3 * BLOCK + STEP
    return pl.pallas_call(
        attention_kernel,
        out_shape=(shape, shape, shape),
        in_specs=[pl.BlockSpec(memory_space=pltpu.SMEM), vmem, vmem, vmem],
        out_specs=(vmem, vmem, vmem),
        scratch_shapes=[
            pltpu.VMEM((4, padded, HD), jnp.float32),
            pltpu.VMEM((3, padded, HD), jnp.float32),
            pltpu.VMEM((MOST, HD), jnp.bfloat16),
            pltpu.VMEM((MOST, HD), jnp.bfloat16),
            pltpu.VMEM((MOST, HD), jnp.bfloat16),
            pltpu.VMEM((MOST, HD), jnp.bfloat16),
            pltpu.VMEM((HD, MOST), jnp.bfloat16),
            pltpu.VMEM((MOST, HD), jnp.float32),
            pltpu.VMEM((MOST, HD), jnp.float32),
            pltpu.VMEM((HD, STEP), jnp.float32),
            pltpu.VMEM((MOST, STEP), jnp.float32),
            pltpu.VMEM((MOST, STEP), jnp.float32),
            pltpu.VMEM((MOST // PART, 8, STEP), jnp.float32),
        ],
        compiler_params=pltpu.CompilerParams(vmem_limit_bytes=VMEM_LIMIT),
        cost_estimate=pl.CostEstimate(
            flops=5 * 2 * MOST * MOST * HD, bytes_accessed=6 * 1024 * 1024, transcendentals=2 * MOST * MOST
        ),
        name="attention",
    )(bounds, left, own, right)


def from_left(shard):
    devices = lax.axis_size("ctx")
    return lax.ppermute(shard, "ctx", [(i, i + 1) for i in range(devices - 1)])


def from_right(shard):
    devices = lax.axis_size("ctx")
    return lax.ppermute(shard, "ctx", [(i + 1, i) for i in range(devices - 1)])


def swap_heads(shard):
    return lax.all_to_all(shard, "head", split_axis=0, concat_axis=0, tiled=True)


def on_device(queries, key_rows, value_rows, out_grad, bounds):
    done = []
    for packed in pack(queries, key_rows, value_rows, out_grad):
        own = swap_heads(packed)
        left = from_left(own)
        right = from_right(own)
        left_grad, own_grad, right_grad = attention(bounds, left, own, right)
        own_grad = own_grad + from_left(right_grad) + from_right(left_grad)
        done.append(swap_heads(own_grad))
    return unpack(*done)


def solution(mesh):
    rows = P(("ctx", "head"), None)
    return jax.shard_map(
        on_device,
        mesh=mesh,
        in_specs=(rows, rows, rows, rows, P()),
        out_specs=(rows, rows, rows),
        check_vma=False,
    )
```

```python
import jax
import jax.numpy as jnp
from jax import lax
from jax.experimental import pallas as pl
from jax.experimental.pallas import tpu as pltpu
from jax.sharding import PartitionSpec as P

HD = 128
NDOC = 64
BLOCK = 1024
SHARD = 128
SHARDS = BLOCK // SHARD
STEP = 256
PART = 128
MOST = 2048
SCALE = HD ** -0.5
LOG2E = 1.4426950408889634
LOW = -1.0e30
VMEM_LIMIT = 48 * 1024 * 1024
VMEM_ALL = 64 * 1024 * 1024 - 256 * 1024


def pack_kernel(q_ref, k_ref, v_ref, g_ref, even_ref, odd_ref, held, sems):
    copies = []
    for slot, ref in enumerate((q_ref, k_ref, v_ref, g_ref)):
        copies.append(pltpu.make_async_copy(ref, held.at[slot], sems.at[slot]))
    for copy in copies:
        copy.start()
    for slot, copy in enumerate(copies):
        copy.wait()
        for peer in range(SHARDS):
            even_ref[peer, slot] = held[slot, :, pl.ds(2 * peer * HD, HD)]
            odd_ref[peer, slot] = held[slot, :, pl.ds((2 * peer + 1) * HD, HD)]


def pack(queries, key_rows, value_rows, out_grad):
    shape = jax.ShapeDtypeStruct((SHARDS, 4, SHARD, HD), jnp.bfloat16)
    return pl.pallas_call(
        pack_kernel,
        out_shape=(shape, shape),
        in_specs=[pl.BlockSpec(memory_space=pltpu.HBM)] * 4,
        scratch_shapes=[
            pltpu.VMEM((4, SHARD, 2 * SHARDS * HD), jnp.bfloat16),
            pltpu.SemaphoreType.DMA((4,)),
        ],
        compiler_params=pltpu.CompilerParams(vmem_limit_bytes=VMEM_ALL),
        name="pack",
    )(queries, key_rows, value_rows, out_grad)


def unpack_kernel(even_ref, odd_ref, dq_ref, dk_ref, dv_ref):
    for slot, ref in enumerate((dq_ref, dk_ref, dv_ref)):
        for peer in range(SHARDS):
            ref[:, pl.ds(2 * peer * HD, HD)] = even_ref[peer, slot]
            ref[:, pl.ds((2 * peer + 1) * HD, HD)] = odd_ref[peer, slot]


def unpack(even, odd):
    shape = jax.ShapeDtypeStruct((SHARD, 2 * SHARDS * HD), jnp.bfloat16)
    return pl.pallas_call(
        unpack_kernel,
        out_shape=(shape, shape, shape),
        compiler_params=pltpu.CompilerParams(vmem_limit_bytes=VMEM_LIMIT),
        name="unpack",
    )(even, odd)


def document_owner(first, end):
    first_block = first // BLOCK
    last_block = (end - 1) // BLOCK
    edge = last_block * BLOCK
    span = last_block - first_block
    right_larger = (end - edge) > (edge - first)
    return first_block + jnp.where(
        span == 2, 1, jnp.where((span == 1) & right_larger, 1, 0)
    )


def attention_kernel(
    bounds_ref, left_ref, own_ref, right_ref,
    left_out, own_out, right_out,
    rows, grads, q_doc, k_doc, v_doc, g_doc, qt_doc, kt_doc, gt_doc, dk_acc, dv_acc, dq_acc, e_buf, p_buf, tops,
):
    me = lax.axis_index("ctx")
    window = (me - 1) * BLOCK
    pieces = ((left_ref, left_out), (own_ref, own_out), (right_ref, right_out))

    def count(doc, carry):
        lo, hi = carry
        owner = document_owner(bounds_ref[doc], bounds_ref[doc + 1])
        return lo + jnp.where(owner < me, 1, 0), hi + jnp.where(owner <= me, 1, 0)

    doc_lo, doc_hi = lax.fori_loop(0, NDOC, count, (jnp.int32(0), jnp.int32(0)))
    row_lo = bounds_ref[doc_lo] - window
    row_hi = bounds_ref[doc_hi] - window
    some = doc_hi > doc_lo

    shard_lo = jnp.where(some, row_lo // SHARD, 0)
    shard_hi = jnp.where(some, (row_hi + SHARD - 1) // SHARD, 0)
    zero_tile = jnp.zeros((STEP, HD), jnp.float32)
    zero_shard = jnp.zeros((SHARD, HD), jnp.float32)

    for piece, (ref, _) in enumerate(pieces):
        lo = jnp.clip(shard_lo - piece * SHARDS, 0, SHARDS)
        hi = jnp.clip(shard_hi - piece * SHARDS, 0, SHARDS)

        def load(shard, carry, ref=ref, piece=piece):
            at = pl.multiple_of((piece * SHARDS + shard) * SHARD, SHARD)
            for slot in range(4):
                rows[slot, pl.ds(at, SHARD), :] = ref[shard, slot].astype(jnp.float32)
            return carry

        lax.fori_loop(lo, hi, load, 0)

    for edge in (shard_lo, jnp.maximum(shard_hi - 1, 0)):
        at = pl.multiple_of(edge * SHARD, SHARD)
        for slot in range(3):
            grads[slot, pl.ds(at, SHARD), :] = zero_shard

    def one_document(doc, carry):
        first = bounds_ref[doc] - window
        length = bounds_ref[doc + 1] - bounds_ref[doc]
        tiles = (length + STEP - 1) // STEP

        def fetch(tile, carry):
            at = pl.multiple_of(tile * STEP, STEP)
            inside = lax.broadcasted_iota(jnp.int32, (STEP, HD), 0) + at < length
            for slot, ref in enumerate((q_doc, k_doc, v_doc, g_doc)):
                part = jnp.where(inside, rows[slot, pl.ds(first + at, STEP), :], 0.0)
                ref[pl.ds(at, STEP), :] = part.astype(jnp.bfloat16)
                if slot != 2:
                    flipped = {0: qt_doc, 1: kt_doc, 3: gt_doc}[slot]
                    flipped[:, pl.ds(at, STEP)] = part.T.astype(jnp.bfloat16)
            dk_acc[pl.ds(at, STEP), :] = zero_tile
            dv_acc[pl.ds(at, STEP), :] = zero_tile
            return carry

        lax.fori_loop(0, tiles, fetch, 0)

        def products(tile, to, size):
            at = pl.multiple_of(tile * STEP, STEP)
            s = jnp.dot(k_doc[pl.ds(to, size), :], qt_doc[:, pl.ds(at, STEP)], preferred_element_type=jnp.float32)
            p = jnp.dot(v_doc[pl.ds(to, size), :], gt_doc[:, pl.ds(at, STEP)], preferred_element_type=jnp.float32)
            return s, p

        def stats(scores, to, size, carry, last):
            s_all, p_all = scores
            for part in range(size // PART):
                top, total, dot = carry
                here = to + part * PART
                s = s_all[part * PART:(part + 1) * PART] * (SCALE * LOG2E)
                p = p_all[part * PART:(part + 1) * PART]
                if last:
                    inside = lax.broadcasted_iota(jnp.int32, (PART, STEP), 0) + here < length
                    s = jnp.where(inside, s, LOW)
                s = s.reshape(PART // 8, 8, STEP)
                new_top = jnp.maximum(top, jnp.max(s, axis=0))
                e = jnp.exp2(s - new_top[None])
                e_buf[pl.ds(here, PART), :] = e.reshape(PART, STEP)
                p_buf[pl.ds(here, PART), :] = p
                tops[to // PART + part] = new_top
                shrink = jnp.exp2(top - new_top)
                total = total * shrink + jnp.sum(e, axis=0)
                dot = dot * shrink + jnp.sum(e * p.reshape(PART // 8, 8, STEP), axis=0)
                carry = new_top, total, dot
            return carry

        def gradients(tile, to, size, norm, delta):
            at = pl.multiple_of(tile * STEP, STEP)
            weights, scores = [], []
            for part in range(size // PART):
                here = to + part * PART
                factor = jnp.exp2(tops[to // PART + part] - norm)
                e = e_buf[pl.ds(here, PART), :].reshape(PART // 8, 8, STEP) * factor[None]
                p = p_buf[pl.ds(here, PART), :].reshape(PART // 8, 8, STEP)
                scores.append((e * (p - delta[None])).reshape(PART, STEP).astype(jnp.bfloat16))
                weights.append(e.reshape(PART, STEP).astype(jnp.bfloat16))
            weights = jnp.concatenate(weights, axis=0)
            scores = jnp.concatenate(scores, axis=0)
            dv_acc[pl.ds(to, size), :] += jnp.dot(
                weights, g_doc[pl.ds(at, STEP), :], preferred_element_type=jnp.float32)
            dk_acc[pl.ds(to, size), :] += jnp.dot(
                scores, q_doc[pl.ds(at, STEP), :], preferred_element_type=jnp.float32)
            dq_acc[...] += jnp.dot(
                kt_doc[:, pl.ds(to, size)], scores, preferred_element_type=jnp.float32)

        pairs = (tiles - 1) // 2
        two_left = 1 - lax.rem(tiles, 2)

        def over_keys(body, carry):
            carry = lax.fori_loop(
                0, pairs, lambda c, now: body(pl.multiple_of(c * 2 * STEP, STEP), 2 * STEP, now, False), carry)
            to = pl.multiple_of(pairs * 2 * STEP, STEP)
            carry = lax.fori_loop(0, two_left, lambda c, now: body(to, 2 * STEP, now, True), carry)
            return lax.fori_loop(0, 1 - two_left, lambda c, now: body(to, STEP, now, True), carry)

        flat = jnp.zeros((8, STEP), jnp.float32)
        fresh = (flat + LOW, flat, flat)

        def joined(top, total, dot):
            peak = jnp.max(top, axis=0, keepdims=True)
            weight = jnp.exp2(top - peak)
            total = jnp.sum(total * weight, axis=0, keepdims=True)
            dot = jnp.sum(dot * weight, axis=0, keepdims=True)
            return flat + (peak + jnp.log2(total)), flat + dot / total

        def put_queries(tile):
            at = pl.multiple_of(tile * STEP, STEP)
            grads[0, pl.ds(first + at, STEP), :] = dq_acc[...].T * SCALE
            dq_acc[...] = jnp.zeros((HD, STEP), jnp.float32)

        dq_acc[...] = jnp.zeros((HD, STEP), jnp.float32)
        norm_now = joined(*over_keys(lambda to, size, now, last: stats(products(0, to, size), to, size, now, last), fresh))

        def query_tile(tile, norms):
            norm, delta = norms

            def both(to, size, now, last):
                scores = products(tile, to, size)
                gradients(tile - 1, to, size, norm, delta)
                return stats(scores, to, size, now, last)

            now = over_keys(both, fresh)
            put_queries(tile - 1)
            return joined(*now)

        norm, delta = lax.fori_loop(1, tiles, query_tile, norm_now)

        def rest(to, size, now, last):
            gradients(tiles - 1, to, size, norm, delta)
            return now

        over_keys(rest, 0)
        put_queries(tiles - 1)

        def put(tile, carry):
            at = pl.multiple_of(tile * STEP, STEP)
            grads[1, pl.ds(first + at, STEP), :] = dk_acc[pl.ds(at, STEP), :] * SCALE
            grads[2, pl.ds(first + at, STEP), :] = dv_acc[pl.ds(at, STEP), :]
            return carry

        lax.fori_loop(0, tiles, put, 0)
        return carry

    lax.fori_loop(doc_lo, doc_hi, one_document, 0)

    for piece, (_, ref) in enumerate(pieces):
        lo = jnp.clip(shard_lo - piece * SHARDS, 0, SHARDS)
        hi = jnp.clip(shard_hi - piece * SHARDS, 0, SHARDS)

        def empty(shard, carry, ref=ref):
            for slot in range(3):
                ref[shard, slot] = zero_shard.astype(jnp.bfloat16)
            return carry

        def store(shard, carry, ref=ref, piece=piece):
            at = pl.multiple_of((piece * SHARDS + shard) * SHARD, SHARD)
            for slot in range(3):
                ref[shard, slot] = grads[slot, pl.ds(at, SHARD), :].astype(jnp.bfloat16)
            return carry

        lax.fori_loop(0, lo, empty, 0)
        lax.fori_loop(lo, hi, store, 0)
        lax.fori_loop(hi, SHARDS, empty, 0)


def attention(bounds, left, own, right):
    shape = jax.ShapeDtypeStruct((SHARDS, 3, SHARD, HD), jnp.bfloat16)
    vmem = pl.BlockSpec(memory_space=pltpu.VMEM)
    padded = 3 * BLOCK + STEP
    return pl.pallas_call(
        attention_kernel,
        out_shape=(shape, shape, shape),
        in_specs=[pl.BlockSpec(memory_space=pltpu.SMEM), vmem, vmem, vmem],
        out_specs=(vmem, vmem, vmem),
        scratch_shapes=[
            pltpu.VMEM((4, padded, HD), jnp.float32),
            pltpu.VMEM((3, padded, HD), jnp.float32),
            pltpu.VMEM((MOST, HD), jnp.bfloat16),
            pltpu.VMEM((MOST, HD), jnp.bfloat16),
            pltpu.VMEM((MOST, HD), jnp.bfloat16),
            pltpu.VMEM((MOST, HD), jnp.bfloat16),
            pltpu.VMEM((HD, MOST), jnp.bfloat16),
            pltpu.VMEM((HD, MOST), jnp.bfloat16),
            pltpu.VMEM((HD, MOST), jnp.bfloat16),
            pltpu.VMEM((MOST, HD), jnp.float32),
            pltpu.VMEM((MOST, HD), jnp.float32),
            pltpu.VMEM((HD, STEP), jnp.float32),
            pltpu.VMEM((MOST, STEP), jnp.float32),
            pltpu.VMEM((MOST, STEP), jnp.float32),
            pltpu.VMEM((MOST // PART, 8, STEP), jnp.float32),
        ],
        compiler_params=pltpu.CompilerParams(vmem_limit_bytes=VMEM_LIMIT),
        cost_estimate=pl.CostEstimate(
            flops=5 * 2 * MOST * MOST * HD, bytes_accessed=6 * 1024 * 1024, transcendentals=2 * MOST * MOST
        ),
        name="attention",
    )(bounds, left, own, right)


def from_left(shard):
    devices = lax.axis_size("ctx")
    return lax.ppermute(shard, "ctx", [(i, i + 1) for i in range(devices - 1)])


def from_right(shard):
    devices = lax.axis_size("ctx")
    return lax.ppermute(shard, "ctx", [(i + 1, i) for i in range(devices - 1)])


def swap_heads(shard):
    return lax.all_to_all(shard, "head", split_axis=0, concat_axis=0, tiled=True)


def on_device(queries, key_rows, value_rows, out_grad, bounds):
    done = []
    for packed in pack(queries, key_rows, value_rows, out_grad):
        own = swap_heads(packed)
        left = from_left(own)
        right = from_right(own)
        left_grad, own_grad, right_grad = attention(bounds, left, own, right)
        own_grad = own_grad + from_left(right_grad) + from_right(left_grad)
        done.append(swap_heads(own_grad))
    return unpack(*done)


def solution(mesh):
    rows = P(("ctx", "head"), None)
    return jax.shard_map(
        on_device,
        mesh=mesh,
        in_specs=(rows, rows, rows, rows, P()),
        out_specs=(rows, rows, rows),
        check_vma=False,
    )
```

```python
import functools

import jax
import jax.numpy as jnp
from jax import lax
from jax.experimental import pallas as pl
from jax.experimental.pallas import tpu as pltpu
from jax.sharding import PartitionSpec as P

HD = 128
NDOC = 64
BLOCK_BITS = 10
BLOCK = 1 << BLOCK_BITS
SHARD = 128
SHARDS = BLOCK // SHARD
STEP = 256
PART = 128
MOST = 2048
FEWEST = 5
SCALE = HD ** -0.5
LOG2E = 1.4426950408889634
LOW = -1.0e30
VMEM_LIMIT = 48 * 1024 * 1024
VMEM_ALL = 64 * 1024 * 1024 - 256 * 1024


def pack_kernel(q_ref, k_ref, v_ref, g_ref, even_ref, odd_ref, held, sems):
    copies = []
    for slot, ref in enumerate((q_ref, k_ref, v_ref, g_ref)):
        copies.append(pltpu.make_async_copy(ref, held.at[slot], sems.at[slot]))
    for copy in copies:
        copy.start()
    for slot, copy in enumerate(copies):
        copy.wait()
        for peer in range(SHARDS):
            even_ref[peer, slot] = held[slot, :, pl.ds(2 * peer * HD, HD)]
            odd_ref[peer, slot] = held[slot, :, pl.ds((2 * peer + 1) * HD, HD)]


def pack(queries, key_rows, value_rows, out_grad):
    shape = jax.ShapeDtypeStruct((SHARDS, 4, SHARD, HD), jnp.bfloat16)
    return pl.pallas_call(
        pack_kernel,
        out_shape=(shape, shape),
        in_specs=[pl.BlockSpec(memory_space=pltpu.HBM)] * 4,
        scratch_shapes=[
            pltpu.VMEM((4, SHARD, 2 * SHARDS * HD), jnp.bfloat16),
            pltpu.SemaphoreType.DMA((4,)),
        ],
        compiler_params=pltpu.CompilerParams(vmem_limit_bytes=VMEM_ALL),
        name="pack",
    )(queries, key_rows, value_rows, out_grad)


def unpack_kernel(even_ref, odd_ref, dq_ref, dk_ref, dv_ref):
    for slot, ref in enumerate((dq_ref, dk_ref, dv_ref)):
        for peer in range(SHARDS):
            ref[:, pl.ds(2 * peer * HD, HD)] = even_ref[peer, slot]
            ref[:, pl.ds((2 * peer + 1) * HD, HD)] = odd_ref[peer, slot]


def unpack(even, odd):
    shape = jax.ShapeDtypeStruct((SHARD, 2 * SHARDS * HD), jnp.bfloat16)
    return pl.pallas_call(
        unpack_kernel,
        out_shape=(shape, shape, shape),
        compiler_params=pltpu.CompilerParams(vmem_limit_bytes=VMEM_LIMIT),
        name="unpack",
    )(even, odd)


def document_owner(first, end):
    first_block = first >> BLOCK_BITS
    last_block = (end - 1) >> BLOCK_BITS
    edge = last_block << BLOCK_BITS
    right_larger = (end - edge) > (edge - first)
    span = last_block - first_block
    return first_block + jnp.where((span == 2) | ((span == 1) & right_larger), 1, 0)


def attention_kernel(
    bounds_ref, left_ref, own_ref, right_ref,
    left_out, own_out, right_out,
    rows, grads, q_doc, k_doc, v_doc, g_doc, kt_doc, dk_acc, dv_acc, dq_acc, e_buf, p_buf, tops,
):
    me = lax.axis_index("ctx")
    window = (me - 1) * BLOCK
    pieces = (
        (left_ref, left_out, SHARDS - left_ref.shape[0]),
        (own_ref, own_out, SHARDS),
        (right_ref, right_out, 2 * SHARDS),
    )

    def count(doc, carry):
        lo, hi = carry
        owner = document_owner(bounds_ref[doc], bounds_ref[doc + 1])
        return lo + jnp.where(owner < me, 1, 0), hi + jnp.where(owner <= me, 1, 0)

    doc_lo, doc_hi = lax.fori_loop(0, NDOC, count, (jnp.int32(0), jnp.int32(0)))
    row_lo = bounds_ref[doc_lo] - window
    row_hi = bounds_ref[doc_hi] - window
    some = doc_hi > doc_lo

    shard_lo = jnp.where(some, row_lo // SHARD, 0)
    shard_hi = jnp.where(some, (row_hi + SHARD - 1) // SHARD, 0)
    zero_tile = jnp.zeros((STEP, HD), jnp.float32)
    zero_shard = jnp.zeros((SHARD, HD), jnp.float32)

    for ref, _, base in pieces:
        lo = jnp.clip(shard_lo - base, 0, ref.shape[0])
        hi = jnp.clip(shard_hi - base, 0, ref.shape[0])

        def load(shard, carry, ref=ref, base=base):
            at = pl.multiple_of((base + shard) * SHARD, SHARD)
            for slot in range(4):
                rows[slot, pl.ds(at, SHARD), :] = ref[shard, slot].astype(jnp.float32)
            return carry

        lax.fori_loop(lo, hi, load, 0)

    for edge in (shard_lo, jnp.maximum(shard_hi - 1, 0)):
        at = pl.multiple_of(edge * SHARD, SHARD)
        for slot in range(3):
            grads[slot, pl.ds(at, SHARD), :] = zero_shard

    def one_document(doc, carry):
        first = bounds_ref[doc] - window
        length = bounds_ref[doc + 1] - bounds_ref[doc]
        tiles = (length + STEP - 1) // STEP

        def fetch(tile, carry):
            at = pl.multiple_of(tile * STEP, STEP)
            inside = lax.broadcasted_iota(jnp.int32, (STEP, HD), 0) + at < length
            for slot, ref in enumerate((q_doc, k_doc, v_doc, g_doc)):
                part = jnp.where(inside, rows[slot, pl.ds(first + at, STEP), :], 0.0)
                ref[pl.ds(at, STEP), :] = part.astype(jnp.bfloat16)
                if slot == 1:
                    kt_doc[:, pl.ds(at, STEP)] = part.astype(jnp.bfloat16).T
            dk_acc[pl.ds(at, STEP), :] = zero_tile
            dv_acc[pl.ds(at, STEP), :] = zero_tile
            return carry

        lax.fori_loop(0, tiles, fetch, 0)

        def products(tile, to, size):
            at = pl.multiple_of(tile * STEP, STEP)
            s = lax.dot_general(
                k_doc[pl.ds(to, size), :], q_doc[pl.ds(at, STEP), :],
                (((1,), (1,)), ((), ())), preferred_element_type=jnp.float32)
            p = lax.dot_general(
                v_doc[pl.ds(to, size), :], g_doc[pl.ds(at, STEP), :],
                (((1,), (1,)), ((), ())), preferred_element_type=jnp.float32)
            return s, p

        def stats(scores, to, size, carry, last):
            s_all, p_all = scores
            for part in range(size // PART):
                top, total, dot = carry
                here = to + part * PART
                s = s_all[part * PART:(part + 1) * PART] * (SCALE * LOG2E)
                p = p_all[part * PART:(part + 1) * PART]
                if last:
                    inside = lax.broadcasted_iota(jnp.int32, (PART, STEP), 0) + here < length
                    s = jnp.where(inside, s, LOW)
                s = s.reshape(PART // 8, 8, STEP)
                new_top = jnp.maximum(top, jnp.max(s, axis=0))
                e = jnp.exp2(s - new_top[None])
                e_buf[pl.ds(here, PART), :] = e.reshape(PART, STEP)
                p_buf[pl.ds(here, PART), :] = p
                tops[to // PART + part] = new_top
                shrink = jnp.exp2(top - new_top)
                total = total * shrink + jnp.sum(e, axis=0)
                dot = dot * shrink + jnp.sum(e * p.reshape(PART // 8, 8, STEP), axis=0)
                carry = new_top, total, dot
            return carry

        def gradients(tile, to, size, norm, delta):
            at = pl.multiple_of(tile * STEP, STEP)
            weights, scores = [], []
            for part in range(size // PART):
                here = to + part * PART
                factor = jnp.exp2(tops[to // PART + part] - norm)
                e = e_buf[pl.ds(here, PART), :].reshape(PART // 8, 8, STEP) * factor[None]
                p = p_buf[pl.ds(here, PART), :].reshape(PART // 8, 8, STEP)
                scores.append((e * (p - delta[None])).reshape(PART, STEP).astype(jnp.bfloat16))
                weights.append(e.reshape(PART, STEP).astype(jnp.bfloat16))
            weights = jnp.concatenate(weights, axis=0)
            scores = jnp.concatenate(scores, axis=0)
            dv_acc[pl.ds(to, size), :] += jnp.dot(
                weights, g_doc[pl.ds(at, STEP), :], preferred_element_type=jnp.float32)
            dk_acc[pl.ds(to, size), :] += jnp.dot(
                scores, q_doc[pl.ds(at, STEP), :], preferred_element_type=jnp.float32)
            dq_acc[...] += jnp.dot(
                kt_doc[:, pl.ds(to, size)], scores, preferred_element_type=jnp.float32)

        pairs = (tiles - 1) // 2
        two_left = 1 - lax.rem(tiles, 2)

        def over_keys(body, carry):
            carry = lax.fori_loop(
                0, pairs, lambda c, now: body(pl.multiple_of(c * 2 * STEP, STEP), 2 * STEP, now, False), carry)
            to = pl.multiple_of(pairs * 2 * STEP, STEP)
            carry = lax.fori_loop(0, two_left, lambda c, now: body(to, 2 * STEP, now, True), carry)
            return lax.fori_loop(0, 1 - two_left, lambda c, now: body(to, STEP, now, True), carry)

        flat = jnp.zeros((8, STEP), jnp.float32)
        fresh = (flat + LOW, flat, flat)

        def joined(top, total, dot):
            peak = jnp.max(top, axis=0, keepdims=True)
            weight = jnp.exp2(top - peak)
            total = jnp.sum(total * weight, axis=0, keepdims=True)
            dot = jnp.sum(dot * weight, axis=0, keepdims=True)
            return flat + (peak + jnp.log2(total)), flat + dot / total

        def put_queries(tile):
            at = pl.multiple_of(tile * STEP, STEP)
            grads[0, pl.ds(first + at, STEP), :] = dq_acc[...].T * SCALE
            dq_acc[...] = jnp.zeros((HD, STEP), jnp.float32)

        dq_acc[...] = jnp.zeros((HD, STEP), jnp.float32)
        norm_now = joined(*over_keys(lambda to, size, now, last: stats(products(0, to, size), to, size, now, last), fresh))

        def query_tile(tile, norms):
            norm, delta = norms

            def both(to, size, now, last):
                scores = products(tile, to, size)
                gradients(tile - 1, to, size, norm, delta)
                return stats(scores, to, size, now, last)

            now = over_keys(both, fresh)
            put_queries(tile - 1)
            return joined(*now)

        norm, delta = lax.fori_loop(1, tiles, query_tile, norm_now)

        def rest(to, size, now, last):
            gradients(tiles - 1, to, size, norm, delta)
            return now

        over_keys(rest, 0)
        put_queries(tiles - 1)

        def put(tile, carry):
            at = pl.multiple_of(tile * STEP, STEP)
            grads[1, pl.ds(first + at, STEP), :] = dk_acc[pl.ds(at, STEP), :] * SCALE
            grads[2, pl.ds(first + at, STEP), :] = dv_acc[pl.ds(at, STEP), :]
            return carry

        lax.fori_loop(0, tiles, put, 0)
        return carry

    lax.fori_loop(doc_lo, doc_hi, one_document, 0)

    for _, ref, base in pieces:
        lo = jnp.clip(shard_lo - base, 0, ref.shape[0])
        hi = jnp.clip(shard_hi - base, 0, ref.shape[0])

        def empty(shard, carry, ref=ref):
            for slot in range(3):
                ref[shard, slot] = zero_shard.astype(jnp.bfloat16)
            return carry

        def store(shard, carry, ref=ref, base=base):
            at = pl.multiple_of((base + shard) * SHARD, SHARD)
            for slot in range(3):
                ref[shard, slot] = grads[slot, pl.ds(at, SHARD), :].astype(jnp.bfloat16)
            return carry

        lax.fori_loop(0, lo, empty, 0)
        lax.fori_loop(lo, hi, store, 0)
        lax.fori_loop(hi, ref.shape[0], empty, 0)


def attention(bounds, left, own, right):
    def shape(like):
        return jax.ShapeDtypeStruct((like.shape[0], 3, SHARD, HD), jnp.bfloat16)

    vmem = pl.BlockSpec(memory_space=pltpu.VMEM)
    padded = 3 * BLOCK + STEP
    return pl.pallas_call(
        attention_kernel,
        out_shape=(shape(left), shape(own), shape(right)),
        in_specs=[pl.BlockSpec(memory_space=pltpu.SMEM), vmem, vmem, vmem],
        out_specs=(vmem, vmem, vmem),
        scratch_shapes=[
            pltpu.VMEM((4, padded, HD), jnp.float32),
            pltpu.VMEM((3, padded, HD), jnp.float32),
            pltpu.VMEM((MOST, HD), jnp.bfloat16),
            pltpu.VMEM((MOST, HD), jnp.bfloat16),
            pltpu.VMEM((MOST, HD), jnp.bfloat16),
            pltpu.VMEM((MOST, HD), jnp.bfloat16),
            pltpu.VMEM((HD, MOST), jnp.bfloat16),
            pltpu.VMEM((MOST, HD), jnp.float32),
            pltpu.VMEM((MOST, HD), jnp.float32),
            pltpu.VMEM((HD, STEP), jnp.float32),
            pltpu.VMEM((MOST, STEP), jnp.float32),
            pltpu.VMEM((MOST, STEP), jnp.float32),
            pltpu.VMEM((MOST // PART, 8, STEP), jnp.float32),
        ],
        compiler_params=pltpu.CompilerParams(vmem_limit_bytes=VMEM_LIMIT),
        cost_estimate=pl.CostEstimate(
            flops=5 * 2 * MOST * MOST * HD, bytes_accessed=6 * 1024 * 1024, transcendentals=2 * MOST * MOST
        ),
        name="attention",
    )(bounds, left, own, right)


def from_left(shard):
    devices = lax.axis_size("ctx")
    return lax.ppermute(shard, "ctx", [(i, i + 1) for i in range(devices - 1)])


def from_right(shard):
    devices = lax.axis_size("ctx")
    return lax.ppermute(shard, "ctx", [(i + 1, i) for i in range(devices - 1)])


def swap_heads(shard):
    return lax.all_to_all(shard, "head", split_axis=0, concat_axis=0, tiled=True)


def halo_rows(bounds):
    first, end = bounds[:-1], bounds[1:]
    first_block, last_block = first >> BLOCK_BITS, (end - 1) >> BLOCK_BITS
    before = ((first_block + 1) << BLOCK_BITS) - first
    after = end - (last_block << BLOCK_BITS)
    span = last_block - first_block
    moved = jnp.where(span == 2, jnp.maximum(before, after), jnp.where(span == 1, jnp.minimum(before, after), 0))
    return jnp.max(moved)


def with_halo(halo, bounds, even, odd):
    done = []
    for parity in range(2):
        own = even if parity == 0 else swap_heads(odd)
        left = from_left(own[SHARDS - halo:])
        right = from_right(own[:halo])
        left_grad, own_grad, right_grad = attention(bounds, left, own, right)
        rest = ((0, SHARDS - halo), (0, 0), (0, 0), (0, 0))
        own_grad = own_grad + jnp.pad(from_left(right_grad), rest) + jnp.pad(from_right(left_grad), (rest[0][::-1],) + rest[1:])
        done.append(swap_heads(own_grad))
    return tuple(done)


def on_device(queries, key_rows, value_rows, out_grad, bounds):
    even, odd = pack(queries, key_rows, value_rows, out_grad)
    even = swap_heads(even)
    rows = halo_rows(bounds)
    branch = sum((rows > halo * SHARD).astype(jnp.int32) for halo in range(FEWEST, SHARDS))
    done = lax.switch(
        branch,
        [functools.partial(with_halo, halo) for halo in range(FEWEST, SHARDS + 1)],
        bounds, even, odd)
    return unpack(*done)


def solution(mesh):
    rows = P(("ctx", "head"), None)
    return jax.shard_map(
        on_device,
        mesh=mesh,
        in_specs=(rows, rows, rows, rows, P()),
        out_specs=(rows, rows, rows),
        check_vma=False,
    )
```

```python
import functools

import jax
import jax.numpy as jnp
from jax import lax
from jax.experimental import pallas as pl
from jax.experimental.pallas import tpu as pltpu
from jax.sharding import PartitionSpec as P

HD = 128
NDOC = 64
BLOCK_BITS = 10
BLOCK = 1 << BLOCK_BITS
SHARD = 128
SHARDS = BLOCK // SHARD
STEP = 256
PART = 128
MOST = 2048
FEWEST = 5
SCALE = HD ** -0.5
LOG2E = 1.4426950408889634
LOW = -1.0e30
VMEM_LIMIT = 48 * 1024 * 1024
VMEM_ALL = 64 * 1024 * 1024 - 256 * 1024


def pack_kernel(parity, q_ref, k_ref, v_ref, g_ref, *refs):
    out_ref, held, sems = refs[-3:]
    copies = []
    for slot, ref in enumerate((q_ref, k_ref, v_ref, g_ref)):
        copies.append(pltpu.make_async_copy(ref, held.at[slot], sems.at[slot]))
    for copy in copies:
        copy.start()
    for slot, copy in enumerate(copies):
        copy.wait()
        for peer in range(SHARDS):
            out_ref[peer, slot] = held[slot, :, pl.ds((2 * peer + parity) * HD, HD)]


def pack(parity, arrays, after, vmem):
    return pl.pallas_call(
        functools.partial(pack_kernel, parity),
        out_shape=jax.ShapeDtypeStruct((SHARDS, 4, SHARD, HD), jnp.bfloat16),
        in_specs=[pl.BlockSpec(memory_space=pl.ANY)] * (4 + len(after)),
        scratch_shapes=[
            pltpu.VMEM((4, SHARD, 2 * SHARDS * HD), jnp.bfloat16),
            pltpu.SemaphoreType.DMA((4,)),
        ],
        compiler_params=pltpu.CompilerParams(vmem_limit_bytes=vmem),
        cost_estimate=pl.CostEstimate(flops=0, bytes_accessed=3 * 1024 * 1024, transcendentals=0),
        name="pack",
    )(*arrays, *after)


def unpack_kernel(even_ref, odd_ref, dq_ref, dk_ref, dv_ref):
    for slot, ref in enumerate((dq_ref, dk_ref, dv_ref)):
        for peer in range(SHARDS):
            ref[:, pl.ds(2 * peer * HD, HD)] = even_ref[peer, slot]
            ref[:, pl.ds((2 * peer + 1) * HD, HD)] = odd_ref[peer, slot]


def unpack(even, odd):
    shape = jax.ShapeDtypeStruct((SHARD, 2 * SHARDS * HD), jnp.bfloat16)
    return pl.pallas_call(
        unpack_kernel,
        out_shape=(shape, shape, shape),
        compiler_params=pltpu.CompilerParams(vmem_limit_bytes=VMEM_LIMIT),
        name="unpack",
    )(even, odd)


def document_owner(first, end):
    first_block = first >> BLOCK_BITS
    last_block = (end - 1) >> BLOCK_BITS
    edge = last_block << BLOCK_BITS
    right_larger = (end - edge) > (edge - first)
    span = last_block - first_block
    return first_block + jnp.where((span == 2) | ((span == 1) & right_larger), 1, 0)


def attention_kernel(
    bounds_ref, left_ref, own_ref, right_ref,
    left_out, own_out, right_out,
    rows, grads, q_doc, k_doc, v_doc, g_doc, kt_doc, dk_acc, dv_acc, dq_acc, e_buf, p_buf, tops,
):
    me = lax.axis_index("ctx")
    window = (me - 1) * BLOCK
    pieces = (
        (left_ref, left_out, SHARDS - left_ref.shape[0]),
        (own_ref, own_out, SHARDS),
        (right_ref, right_out, 2 * SHARDS),
    )

    def count(doc, carry):
        lo, hi = carry
        owner = document_owner(bounds_ref[doc], bounds_ref[doc + 1])
        return lo + jnp.where(owner < me, 1, 0), hi + jnp.where(owner <= me, 1, 0)

    doc_lo, doc_hi = lax.fori_loop(0, NDOC, count, (jnp.int32(0), jnp.int32(0)))
    row_lo = bounds_ref[doc_lo] - window
    row_hi = bounds_ref[doc_hi] - window
    some = doc_hi > doc_lo

    shard_lo = jnp.where(some, row_lo // SHARD, 0)
    shard_hi = jnp.where(some, (row_hi + SHARD - 1) // SHARD, 0)
    zero_tile = jnp.zeros((STEP, HD), jnp.float32)
    zero_shard = jnp.zeros((SHARD, HD), jnp.float32)

    for ref, _, base in pieces:
        lo = jnp.clip(shard_lo - base, 0, ref.shape[0])
        hi = jnp.clip(shard_hi - base, 0, ref.shape[0])

        def load(shard, carry, ref=ref, base=base):
            at = pl.multiple_of((base + shard) * SHARD, SHARD)
            for slot in range(4):
                rows[slot, pl.ds(at, SHARD), :] = ref[shard, slot].astype(jnp.float32)
            return carry

        lax.fori_loop(lo, hi, load, 0)

    for edge in (shard_lo, jnp.maximum(shard_hi - 1, 0)):
        at = pl.multiple_of(edge * SHARD, SHARD)
        for slot in range(3):
            grads[slot, pl.ds(at, SHARD), :] = zero_shard

    def one_document(doc, carry):
        first = bounds_ref[doc] - window
        length = bounds_ref[doc + 1] - bounds_ref[doc]
        tiles = (length + STEP - 1) // STEP

        def fetch(tile, carry):
            at = pl.multiple_of(tile * STEP, STEP)
            inside = lax.broadcasted_iota(jnp.int32, (STEP, HD), 0) + at < length
            for slot, ref in enumerate((q_doc, k_doc, v_doc, g_doc)):
                part = jnp.where(inside, rows[slot, pl.ds(first + at, STEP), :], 0.0)
                ref[pl.ds(at, STEP), :] = part.astype(jnp.bfloat16)
                if slot == 1:
                    kt_doc[:, pl.ds(at, STEP)] = part.astype(jnp.bfloat16).T
            dk_acc[pl.ds(at, STEP), :] = zero_tile
            dv_acc[pl.ds(at, STEP), :] = zero_tile
            return carry

        lax.fori_loop(0, tiles, fetch, 0)

        def products(tile, to, size):
            at = pl.multiple_of(tile * STEP, STEP)
            s = lax.dot_general(
                k_doc[pl.ds(to, size), :], q_doc[pl.ds(at, STEP), :],
                (((1,), (1,)), ((), ())), preferred_element_type=jnp.float32)
            p = lax.dot_general(
                v_doc[pl.ds(to, size), :], g_doc[pl.ds(at, STEP), :],
                (((1,), (1,)), ((), ())), preferred_element_type=jnp.float32)
            return s, p

        def stats(scores, to, size, carry):
            s_all, p_all = scores
            for part in range(size // PART):
                top, total, dot = carry
                here = to + part * PART
                s = s_all[part * PART:(part + 1) * PART] * (SCALE * LOG2E)
                p = p_all[part * PART:(part + 1) * PART]
                if part >= (size - STEP) // PART:
                    inside = lax.broadcasted_iota(jnp.int32, (PART, STEP), 0) + here < length
                    s = jnp.where(inside, s, LOW)
                s = s.reshape(PART // 8, 8, STEP)
                new_top = jnp.maximum(top, jnp.max(s, axis=0))
                e = jnp.exp2(s - new_top[None])
                e_buf[pl.ds(here, PART), :] = e.reshape(PART, STEP)
                p_buf[pl.ds(here, PART), :] = p
                tops[to // PART + part] = new_top
                shrink = jnp.exp2(top - new_top)
                total = total * shrink + jnp.sum(e, axis=0)
                dot = dot * shrink + jnp.sum(e * p.reshape(PART // 8, 8, STEP), axis=0)
                carry = new_top, total, dot
            return carry

        def gradients(tile, to, size, norm, delta):
            at = pl.multiple_of(tile * STEP, STEP)
            weights, scores = [], []
            for part in range(size // PART):
                here = to + part * PART
                factor = jnp.exp2(tops[to // PART + part] - norm)
                e = e_buf[pl.ds(here, PART), :].reshape(PART // 8, 8, STEP) * factor[None]
                p = p_buf[pl.ds(here, PART), :].reshape(PART // 8, 8, STEP)
                scores.append((e * (p - delta[None])).reshape(PART, STEP).astype(jnp.bfloat16))
                weights.append(e.reshape(PART, STEP).astype(jnp.bfloat16))
            weights = jnp.concatenate(weights, axis=0)
            scores = jnp.concatenate(scores, axis=0)
            dv_acc[pl.ds(to, size), :] += jnp.dot(
                weights, g_doc[pl.ds(at, STEP), :], preferred_element_type=jnp.float32)
            dk_acc[pl.ds(to, size), :] += jnp.dot(
                scores, q_doc[pl.ds(at, STEP), :], preferred_element_type=jnp.float32)
            dq_acc[...] += jnp.dot(
                kt_doc[:, pl.ds(to, size)], scores, preferred_element_type=jnp.float32)

        def over_keys(body, carry):
            to = 0
            for wide in (4, 2, 1):
                size = wide * STEP
                steps = tiles // 4 if wide == 4 else (tiles // wide) % 2
                start = to

                def step(c, now, start=start, size=size):
                    return body(pl.multiple_of(start + c * size, STEP), size, now)

                carry = lax.fori_loop(0, steps, step, carry)
                to = start + steps * size
            return carry

        flat = jnp.zeros((8, STEP), jnp.float32)
        fresh = (flat + LOW, flat, flat)

        def joined(top, total, dot):
            peak = jnp.max(top, axis=0, keepdims=True)
            weight = jnp.exp2(top - peak)
            total = jnp.sum(total * weight, axis=0, keepdims=True)
            dot = jnp.sum(dot * weight, axis=0, keepdims=True)
            return flat + (peak + jnp.log2(total)), flat + dot / total

        def put_queries(tile):
            at = pl.multiple_of(tile * STEP, STEP)
            grads[0, pl.ds(first + at, STEP), :] = dq_acc[...].T * SCALE
            dq_acc[...] = jnp.zeros((HD, STEP), jnp.float32)

        dq_acc[...] = jnp.zeros((HD, STEP), jnp.float32)
        norm_now = joined(*over_keys(lambda to, size, now: stats(products(0, to, size), to, size, now), fresh))

        def query_tile(tile, norms):
            norm, delta = norms

            def both(to, size, now):
                scores = products(tile, to, size)
                gradients(tile - 1, to, size, norm, delta)
                return stats(scores, to, size, now)

            now = over_keys(both, fresh)
            put_queries(tile - 1)
            return joined(*now)

        norm, delta = lax.fori_loop(1, tiles, query_tile, norm_now)

        def rest(to, size, now):
            gradients(tiles - 1, to, size, norm, delta)
            return now

        over_keys(rest, 0)
        put_queries(tiles - 1)

        def put(tile, carry):
            at = pl.multiple_of(tile * STEP, STEP)
            grads[1, pl.ds(first + at, STEP), :] = dk_acc[pl.ds(at, STEP), :] * SCALE
            grads[2, pl.ds(first + at, STEP), :] = dv_acc[pl.ds(at, STEP), :]
            return carry

        lax.fori_loop(0, tiles, put, 0)
        return carry

    lax.fori_loop(doc_lo, doc_hi, one_document, 0)

    for _, ref, base in pieces:
        lo = jnp.clip(shard_lo - base, 0, ref.shape[0])
        hi = jnp.clip(shard_hi - base, 0, ref.shape[0])

        def empty(shard, carry, ref=ref):
            for slot in range(3):
                ref[shard, slot] = zero_shard.astype(jnp.bfloat16)
            return carry

        def store(shard, carry, ref=ref, base=base):
            at = pl.multiple_of((base + shard) * SHARD, SHARD)
            for slot in range(3):
                ref[shard, slot] = grads[slot, pl.ds(at, SHARD), :].astype(jnp.bfloat16)
            return carry

        lax.fori_loop(0, lo, empty, 0)
        lax.fori_loop(lo, hi, store, 0)
        lax.fori_loop(hi, ref.shape[0], empty, 0)


def attention(bounds, left, own, right):
    def shape(like):
        return jax.ShapeDtypeStruct((like.shape[0], 3, SHARD, HD), jnp.bfloat16)

    vmem = pl.BlockSpec(memory_space=pltpu.VMEM)
    padded = 3 * BLOCK + STEP
    return pl.pallas_call(
        attention_kernel,
        out_shape=(shape(left), shape(own), shape(right)),
        in_specs=[pl.BlockSpec(memory_space=pltpu.SMEM), vmem, vmem, vmem],
        out_specs=(vmem, vmem, vmem),
        scratch_shapes=[
            pltpu.VMEM((4, padded, HD), jnp.float32),
            pltpu.VMEM((3, padded, HD), jnp.float32),
            pltpu.VMEM((MOST, HD), jnp.bfloat16),
            pltpu.VMEM((MOST, HD), jnp.bfloat16),
            pltpu.VMEM((MOST, HD), jnp.bfloat16),
            pltpu.VMEM((MOST, HD), jnp.bfloat16),
            pltpu.VMEM((HD, MOST), jnp.bfloat16),
            pltpu.VMEM((MOST, HD), jnp.float32),
            pltpu.VMEM((MOST, HD), jnp.float32),
            pltpu.VMEM((HD, STEP), jnp.float32),
            pltpu.VMEM((MOST, STEP), jnp.float32),
            pltpu.VMEM((MOST, STEP), jnp.float32),
            pltpu.VMEM((MOST // PART, 8, STEP), jnp.float32),
        ],
        compiler_params=pltpu.CompilerParams(vmem_limit_bytes=VMEM_LIMIT),
        cost_estimate=pl.CostEstimate(
            flops=5 * 2 * MOST * MOST * HD, bytes_accessed=6 * 1024 * 1024, transcendentals=2 * MOST * MOST
        ),
        name="attention",
    )(bounds, left, own, right)


def from_left(shard):
    devices = lax.axis_size("ctx")
    return lax.ppermute(shard, "ctx", [(i, i + 1) for i in range(devices - 1)])


def from_right(shard):
    devices = lax.axis_size("ctx")
    return lax.ppermute(shard, "ctx", [(i + 1, i) for i in range(devices - 1)])


def swap_heads(shard):
    return lax.all_to_all(shard, "head", split_axis=0, concat_axis=0, tiled=True)


def halo_rows(bounds):
    first, end = bounds[:-1], bounds[1:]
    first_block, last_block = first >> BLOCK_BITS, (end - 1) >> BLOCK_BITS
    before = ((first_block + 1) << BLOCK_BITS) - first
    after = end - (last_block << BLOCK_BITS)
    span = last_block - first_block
    moved = jnp.where(span == 2, jnp.maximum(before, after), jnp.where(span == 1, jnp.minimum(before, after), 0))
    return jnp.max(moved)


def with_halo(halo, arrays, bounds, even):
    done = []
    for parity in range(2):
        if parity == 0:
            own = even
        else:
            own = swap_heads(pack(1, arrays, (to_right, to_left), VMEM_LIMIT))
        to_right, to_left = own[SHARDS - halo:], own[:halo]
        left, right = from_left(to_right), from_right(to_left)
        left_grad, own_grad, right_grad = attention(bounds, left, own, right)
        rest = ((0, SHARDS - halo), (0, 0), (0, 0), (0, 0))
        own_grad = own_grad + jnp.pad(from_left(right_grad), rest) + jnp.pad(from_right(left_grad), (rest[0][::-1],) + rest[1:])
        done.append(swap_heads(own_grad))
    return tuple(done)


def on_device(queries, key_rows, value_rows, out_grad, bounds):
    arrays = (queries, key_rows, value_rows, out_grad)
    even = swap_heads(pack(0, arrays, (), VMEM_ALL))
    rows = halo_rows(bounds)
    branch = sum((rows > halo * SHARD).astype(jnp.int32) for halo in range(FEWEST, SHARDS))
    done = lax.switch(
        branch,
        [functools.partial(with_halo, halo) for halo in range(FEWEST, SHARDS + 1)],
        arrays, bounds, even)
    return unpack(*done)


def solution(mesh):
    rows = P(("ctx", "head"), None)
    return jax.shard_map(
        on_device,
        mesh=mesh,
        in_specs=(rows, rows, rows, rows, P()),
        out_specs=(rows, rows, rows),
        check_vma=False,
    )
```

```python
import jax
import jax.numpy as jnp
from jax import lax
from jax.experimental import pallas as pl
from jax.experimental.pallas import tpu as pltpu
from jax.sharding import PartitionSpec as P

HD = 128
NDOC = 64
BLOCK_BITS = 10
BLOCK = 1 << BLOCK_BITS
SHARD_BITS = 7
SHARD = 1 << SHARD_BITS
SHARDS = BLOCK // SHARD
STEP = 256
PART = 128
MOST = 2048
SCALE = HD ** -0.5
LOG2E = 1.4426950408889634
LOW = -1.0e30
VMEM_LIMIT = 48 * 1024 * 1024
VMEM_ALL = 64 * 1024 * 1024 - 256 * 1024


def pack_kernel(q_ref, k_ref, v_ref, g_ref, even_ref, odd_ref, held, sems):
    copies = []
    for slot, ref in enumerate((q_ref, k_ref, v_ref, g_ref)):
        copies.append(pltpu.make_async_copy(ref, held.at[slot], sems.at[slot]))
    for copy in copies:
        copy.start()
    for slot, copy in enumerate(copies):
        copy.wait()
        for peer in range(SHARDS):
            even_ref[peer, slot] = held[slot, :, pl.ds(2 * peer * HD, HD)]
            odd_ref[peer, slot] = held[slot, :, pl.ds((2 * peer + 1) * HD, HD)]


def pack(queries, key_rows, value_rows, out_grad):
    shape = jax.ShapeDtypeStruct((SHARDS, 4, SHARD, HD), jnp.bfloat16)
    return pl.pallas_call(
        pack_kernel,
        out_shape=(shape, shape),
        in_specs=[pl.BlockSpec(memory_space=pltpu.HBM)] * 4,
        scratch_shapes=[
            pltpu.VMEM((4, SHARD, 2 * SHARDS * HD), jnp.bfloat16),
            pltpu.SemaphoreType.DMA((4,)),
        ],
        compiler_params=pltpu.CompilerParams(vmem_limit_bytes=VMEM_ALL),
        name="pack",
    )(queries, key_rows, value_rows, out_grad)


def unpack_kernel(even_ref, odd_ref, dq_ref, dk_ref, dv_ref):
    for slot, ref in enumerate((dq_ref, dk_ref, dv_ref)):
        for peer in range(SHARDS):
            ref[:, pl.ds(2 * peer * HD, HD)] = even_ref[peer, slot]
            ref[:, pl.ds((2 * peer + 1) * HD, HD)] = odd_ref[peer, slot]


def unpack(even, odd):
    shape = jax.ShapeDtypeStruct((SHARD, 2 * SHARDS * HD), jnp.bfloat16)
    return pl.pallas_call(
        unpack_kernel,
        out_shape=(shape, shape, shape),
        compiler_params=pltpu.CompilerParams(vmem_limit_bytes=VMEM_LIMIT),
        name="unpack",
    )(even, odd)


def document_owner(first, end):
    first_block = first >> BLOCK_BITS
    last_block = (end - 1) >> BLOCK_BITS
    edge = last_block << BLOCK_BITS
    right_larger = (end - edge) > (edge - first)
    span = last_block - first_block
    return first_block + jnp.where((span == 2) | ((span == 1) & right_larger), 1, 0)


def attention_kernel(
    bounds_ref, span_ref, left_ref, own_ref, right_ref,
    left_out, own_out, right_out,
    held, put_out, zeros, in_sems, out_sems,
    rows, grads, q_doc, k_doc, v_doc, g_doc, kt_doc, dk_acc, dv_acc, dq_acc, e_buf, p_buf, tops,
):
    window = (lax.axis_index("ctx") - 1) * BLOCK
    pieces = ((left_ref, left_out), (own_ref, own_out), (right_ref, right_out))

    doc_lo, doc_hi = span_ref[0], span_ref[1]
    some = doc_hi > doc_lo
    shard_lo = jnp.where(some, (bounds_ref[doc_lo] - window) >> SHARD_BITS, 0)
    shard_hi = jnp.where(some, (bounds_ref[doc_hi] - window + SHARD - 1) >> SHARD_BITS, 0)
    zero_tile = jnp.zeros((STEP, HD), jnp.float32)
    zero_shard = jnp.zeros((SHARD, HD), jnp.float32)

    def owned_in(piece):
        return tuple(jnp.clip(edge - piece * SHARDS, 0, SHARDS) for edge in (shard_lo, shard_hi))

    def copy_in(piece, shard):
        at = piece * SHARDS + shard
        return pltpu.make_async_copy(pieces[piece][0].at[shard], held.at[at], in_sems.at[at])

    def copy_out(piece, shard):
        at = piece * SHARDS + shard
        return pltpu.make_async_copy(put_out.at[at], pieces[piece][1].at[shard], out_sems.at[at])

    def copy_zero(piece, shard):
        at = piece * SHARDS + shard
        return pltpu.make_async_copy(zeros, pieces[piece][1].at[shard], out_sems.at[at])

    def each(lo, hi, act):
        def step(shard, carry):
            act(shard)
            return carry

        lax.fori_loop(lo, hi, step, 0)

    for piece in range(3):
        each(*owned_in(piece), lambda shard: copy_in(piece, shard).start())

    zeros[...] = jnp.zeros(zeros.shape, zeros.dtype)
    for piece in range(3):
        lo, hi = owned_in(piece)
        each(0, lo, lambda shard: copy_zero(piece, shard).start())
        each(hi, SHARDS, lambda shard: copy_zero(piece, shard).start())

    for edge in (shard_lo, jnp.maximum(shard_hi - 1, 0)):
        at = pl.multiple_of(edge * SHARD, SHARD)
        for slot in range(3):
            grads[slot, pl.ds(at, SHARD), :] = zero_shard

    for piece in range(3):

        def load(shard):
            copy_in(piece, shard).wait()
            at = pl.multiple_of((piece * SHARDS + shard) * SHARD, SHARD)
            for slot in range(4):
                rows[slot, pl.ds(at, SHARD), :] = held[piece * SHARDS + shard, slot].astype(jnp.float32)

        each(*owned_in(piece), load)

    def one_document(doc, carry):
        first = bounds_ref[doc] - window
        length = bounds_ref[doc + 1] - bounds_ref[doc]
        tiles = (length + STEP - 1) // STEP

        def fetch(tile, carry):
            at = pl.multiple_of(tile * STEP, STEP)
            inside = lax.broadcasted_iota(jnp.int32, (STEP, HD), 0) + at < length
            for slot, ref in enumerate((q_doc, k_doc, v_doc, g_doc)):
                part = jnp.where(inside, rows[slot, pl.ds(first + at, STEP), :], 0.0)
                ref[pl.ds(at, STEP), :] = part.astype(jnp.bfloat16)
                if slot == 1:
                    kt_doc[:, pl.ds(at, STEP)] = part.astype(jnp.bfloat16).T
            dk_acc[pl.ds(at, STEP), :] = zero_tile
            dv_acc[pl.ds(at, STEP), :] = zero_tile
            return carry

        lax.fori_loop(0, tiles, fetch, 0)

        def products(tile, to, size):
            at = pl.multiple_of(tile * STEP, STEP)
            s = lax.dot_general(
                k_doc[pl.ds(to, size), :], q_doc[pl.ds(at, STEP), :],
                (((1,), (1,)), ((), ())), preferred_element_type=jnp.float32)
            p = lax.dot_general(
                v_doc[pl.ds(to, size), :], g_doc[pl.ds(at, STEP), :],
                (((1,), (1,)), ((), ())), preferred_element_type=jnp.float32)
            return s, p

        def stats(scores, to, size, carry):
            s_all, p_all = scores
            for part in range(size // PART):
                top, total, dot = carry
                here = to + part * PART
                s = s_all[part * PART:(part + 1) * PART] * (SCALE * LOG2E)
                p = p_all[part * PART:(part + 1) * PART]
                if part >= (size - STEP) // PART:
                    inside = lax.broadcasted_iota(jnp.int32, (PART, STEP), 0) + here < length
                    s = jnp.where(inside, s, LOW)
                s = s.reshape(PART // 8, 8, STEP)
                new_top = jnp.maximum(top, jnp.max(s, axis=0))
                e = jnp.exp2(s - new_top[None])
                e_buf[pl.ds(here, PART), :] = e.reshape(PART, STEP)
                p_buf[pl.ds(here, PART), :] = p
                tops[to // PART + part] = new_top
                shrink = jnp.exp2(top - new_top)
                total = total * shrink + jnp.sum(e, axis=0)
                dot = dot * shrink + jnp.sum(e * p.reshape(PART // 8, 8, STEP), axis=0)
                carry = new_top, total, dot
            return carry

        def gradients(tile, to, size, norm, delta):
            at = pl.multiple_of(tile * STEP, STEP)
            weights, scores = [], []
            for part in range(size // PART):
                here = to + part * PART
                factor = jnp.exp2(tops[to // PART + part] - norm)
                e = e_buf[pl.ds(here, PART), :].reshape(PART // 8, 8, STEP) * factor[None]
                p = p_buf[pl.ds(here, PART), :].reshape(PART // 8, 8, STEP)
                scores.append((e * (p - delta[None])).reshape(PART, STEP).astype(jnp.bfloat16))
                weights.append(e.reshape(PART, STEP).astype(jnp.bfloat16))
            weights = jnp.concatenate(weights, axis=0)
            scores = jnp.concatenate(scores, axis=0)
            dv_acc[pl.ds(to, size), :] += jnp.dot(
                weights, g_doc[pl.ds(at, STEP), :], preferred_element_type=jnp.float32)
            dk_acc[pl.ds(to, size), :] += jnp.dot(
                scores, q_doc[pl.ds(at, STEP), :], preferred_element_type=jnp.float32)
            dq_acc[...] += jnp.dot(
                kt_doc[:, pl.ds(to, size)], scores, preferred_element_type=jnp.float32)

        def over_keys(body, carry):
            to = 0
            for wide in (4, 2, 1):
                size = wide * STEP
                steps = tiles // 4 if wide == 4 else (tiles // wide) % 2
                start = to

                def step(c, now, start=start, size=size):
                    return body(pl.multiple_of(start + c * size, STEP), size, now)

                carry = lax.fori_loop(0, steps, step, carry)
                to = start + steps * size
            return carry

        flat = jnp.zeros((8, STEP), jnp.float32)
        fresh = (flat + LOW, flat, flat)

        def joined(top, total, dot):
            peak = jnp.max(top, axis=0, keepdims=True)
            weight = jnp.exp2(top - peak)
            total = jnp.sum(total * weight, axis=0, keepdims=True)
            dot = jnp.sum(dot * weight, axis=0, keepdims=True)
            return flat + (peak + jnp.log2(total)), flat + dot / total

        def put_queries(tile):
            at = pl.multiple_of(tile * STEP, STEP)
            grads[0, pl.ds(first + at, STEP), :] = dq_acc[...].T * SCALE
            dq_acc[...] = jnp.zeros((HD, STEP), jnp.float32)

        dq_acc[...] = jnp.zeros((HD, STEP), jnp.float32)
        norm_now = joined(*over_keys(lambda to, size, now: stats(products(0, to, size), to, size, now), fresh))

        def query_tile(tile, norms):
            norm, delta = norms

            def both(to, size, now):
                scores = products(tile, to, size)
                gradients(tile - 1, to, size, norm, delta)
                return stats(scores, to, size, now)

            now = over_keys(both, fresh)
            put_queries(tile - 1)
            return joined(*now)

        norm, delta = lax.fori_loop(1, tiles, query_tile, norm_now)

        def rest(to, size, now):
            gradients(tiles - 1, to, size, norm, delta)
            return now

        over_keys(rest, 0)
        put_queries(tiles - 1)

        def put(tile, carry):
            at = pl.multiple_of(tile * STEP, STEP)
            grads[1, pl.ds(first + at, STEP), :] = dk_acc[pl.ds(at, STEP), :] * SCALE
            grads[2, pl.ds(first + at, STEP), :] = dv_acc[pl.ds(at, STEP), :]
            return carry

        lax.fori_loop(0, tiles, put, 0)
        return carry

    lax.fori_loop(doc_lo, doc_hi, one_document, 0)

    for piece in range(3):

        def store(shard):
            at = pl.multiple_of((piece * SHARDS + shard) * SHARD, SHARD)
            for slot in range(3):
                put_out[piece * SHARDS + shard, slot] = grads[slot, pl.ds(at, SHARD), :].astype(jnp.bfloat16)
            copy_out(piece, shard).start()

        each(*owned_in(piece), store)

    for piece in range(3):
        lo, hi = owned_in(piece)
        each(0, lo, lambda shard: copy_zero(piece, shard).wait())
        each(lo, hi, lambda shard: copy_out(piece, shard).wait())
        each(hi, SHARDS, lambda shard: copy_zero(piece, shard).wait())


def attention(bounds, span, left, own, right):
    shape = jax.ShapeDtypeStruct((SHARDS, 3, SHARD, HD), jnp.bfloat16)
    smem = pl.BlockSpec(memory_space=pltpu.SMEM)
    anywhere = pl.BlockSpec(memory_space=pl.ANY)
    padded = 3 * BLOCK + STEP
    return pl.pallas_call(
        attention_kernel,
        out_shape=(shape, shape, shape),
        in_specs=[smem, smem, anywhere, anywhere, anywhere],
        out_specs=(anywhere, anywhere, anywhere),
        scratch_shapes=[
            pltpu.VMEM((3 * SHARDS, 4, SHARD, HD), jnp.bfloat16),
            pltpu.VMEM((3 * SHARDS, 3, SHARD, HD), jnp.bfloat16),
            pltpu.VMEM((3, SHARD, HD), jnp.bfloat16),
            pltpu.SemaphoreType.DMA((3 * SHARDS,)),
            pltpu.SemaphoreType.DMA((3 * SHARDS,)),
            pltpu.VMEM((4, padded, HD), jnp.float32),
            pltpu.VMEM((3, padded, HD), jnp.float32),
            pltpu.VMEM((MOST, HD), jnp.bfloat16),
            pltpu.VMEM((MOST, HD), jnp.bfloat16),
            pltpu.VMEM((MOST, HD), jnp.bfloat16),
            pltpu.VMEM((MOST, HD), jnp.bfloat16),
            pltpu.VMEM((HD, MOST), jnp.bfloat16),
            pltpu.VMEM((MOST, HD), jnp.float32),
            pltpu.VMEM((MOST, HD), jnp.float32),
            pltpu.VMEM((HD, STEP), jnp.float32),
            pltpu.VMEM((MOST, STEP), jnp.float32),
            pltpu.VMEM((MOST, STEP), jnp.float32),
            pltpu.VMEM((MOST // PART, 8, STEP), jnp.float32),
        ],
        compiler_params=pltpu.CompilerParams(vmem_limit_bytes=VMEM_LIMIT),
        cost_estimate=pl.CostEstimate(
            flops=5 * 2 * MOST * MOST * HD, bytes_accessed=6 * 1024 * 1024, transcendentals=2 * MOST * MOST
        ),
        name="attention",
    )(bounds, span, left, own, right)


def from_left(shard):
    devices = lax.axis_size("ctx")
    return lax.ppermute(shard, "ctx", [(i, i + 1) for i in range(devices - 1)])


def from_right(shard):
    devices = lax.axis_size("ctx")
    return lax.ppermute(shard, "ctx", [(i + 1, i) for i in range(devices - 1)])


def swap_heads(shard):
    return lax.all_to_all(shard, "head", split_axis=0, concat_axis=0, tiled=True)


def on_device(queries, key_rows, value_rows, out_grad, bounds):
    owner = document_owner(bounds[:-1], bounds[1:])
    me = lax.axis_index("ctx")
    span = jnp.stack([jnp.sum(owner < me), jnp.sum(owner <= me)]).astype(jnp.int32)
    done = []
    for packed in pack(queries, key_rows, value_rows, out_grad):
        own = swap_heads(packed)
        left = from_left(own)
        right = from_right(own)
        left_grad, own_grad, right_grad = attention(bounds, span, left, own, right)
        own_grad = own_grad + from_left(right_grad) + from_right(left_grad)
        done.append(swap_heads(own_grad))
    return unpack(*done)


def solution(mesh):
    rows = P(("ctx", "head"), None)
    return jax.shard_map(
        on_device,
        mesh=mesh,
        in_specs=(rows, rows, rows, rows, P()),
        out_specs=(rows, rows, rows),
        check_vma=False,
    )
```

```python
import functools

import jax
import jax.numpy as jnp
from jax import lax
from jax.experimental import pallas as pl
from jax.experimental.pallas import tpu as pltpu
from jax.sharding import PartitionSpec as P

HD = 128
NDOC = 64
BLOCK_BITS = 10
BLOCK = 1 << BLOCK_BITS
SHARD_BITS = 7
SHARD = 1 << SHARD_BITS
SHARDS = BLOCK // SHARD
STEP = 256
PART = 128
MOST = 2048
SCALE = HD ** -0.5
LOG2E = 1.4426950408889634
LOW = -1.0e30
VMEM_LIMIT = 48 * 1024 * 1024
VMEM_ALL = 64 * 1024 * 1024 - 256 * 1024


def pack_kernel(parity, q_ref, k_ref, v_ref, g_ref, *refs):
    out_ref, held, sems = refs[-3:]
    copies = []
    for slot, ref in enumerate((q_ref, k_ref, v_ref, g_ref)):
        copies.append(pltpu.make_async_copy(ref, held.at[slot], sems.at[slot]))
    for copy in copies:
        copy.start()
    for slot, copy in enumerate(copies):
        copy.wait()
        for peer in range(SHARDS):
            out_ref[peer, slot] = held[slot, :, pl.ds((2 * peer + parity) * HD, HD)]


def pack(parity, arrays, after):
    return pl.pallas_call(
        functools.partial(pack_kernel, parity),
        out_shape=jax.ShapeDtypeStruct((SHARDS, 4, SHARD, HD), jnp.bfloat16),
        in_specs=[pl.BlockSpec(memory_space=pl.ANY)] * (4 + len(after)),
        scratch_shapes=[
            pltpu.VMEM((4, SHARD, 2 * SHARDS * HD), jnp.bfloat16),
            pltpu.SemaphoreType.DMA((4,)),
        ],
        compiler_params=pltpu.CompilerParams(vmem_limit_bytes=VMEM_LIMIT if after else VMEM_ALL),
        cost_estimate=pl.CostEstimate(flops=0, bytes_accessed=(64 if after else 3) * 1024 * 1024, transcendentals=0),
        name="pack",
    )(*arrays, *after)


def unpack_kernel(even_ref, odd_ref, dq_ref, dk_ref, dv_ref):
    for slot, ref in enumerate((dq_ref, dk_ref, dv_ref)):
        for peer in range(SHARDS):
            ref[:, pl.ds(2 * peer * HD, HD)] = even_ref[peer, slot]
            ref[:, pl.ds((2 * peer + 1) * HD, HD)] = odd_ref[peer, slot]


def unpack(even, odd):
    shape = jax.ShapeDtypeStruct((SHARD, 2 * SHARDS * HD), jnp.bfloat16)
    return pl.pallas_call(
        unpack_kernel,
        out_shape=(shape, shape, shape),
        compiler_params=pltpu.CompilerParams(vmem_limit_bytes=VMEM_LIMIT),
        name="unpack",
    )(even, odd)


def document_owner(first, end):
    first_block = first >> BLOCK_BITS
    last_block = (end - 1) >> BLOCK_BITS
    edge = last_block << BLOCK_BITS
    right_larger = (end - edge) > (edge - first)
    span = last_block - first_block
    return first_block + jnp.where((span == 2) | ((span == 1) & right_larger), 1, 0)


def attention_kernel(
    bounds_ref, span_ref, left_ref, own_ref, right_ref,
    left_out, own_out, right_out,
    rows, grads, q_doc, k_doc, v_doc, g_doc, kt_doc, dk_acc, dv_acc, dq_acc, e_buf, p_buf, tops,
):
    window = (lax.axis_index("ctx") - 1) * BLOCK
    pieces = ((left_ref, left_out, 0), (own_ref, own_out, SHARDS), (right_ref, right_out, 2 * SHARDS))

    doc_lo, doc_hi = span_ref[0], span_ref[1]
    some = doc_hi > doc_lo
    shard_lo = jnp.where(some, (bounds_ref[doc_lo] - window) >> SHARD_BITS, 0)
    shard_hi = jnp.where(some, (bounds_ref[doc_hi] - window + SHARD - 1) >> SHARD_BITS, 0)
    zero_tile = jnp.zeros((STEP, HD), jnp.float32)
    zero_shard = jnp.zeros((SHARD, HD), jnp.float32)

    for ref, _, base in pieces:
        lo = jnp.clip(shard_lo - base, 0, ref.shape[0])
        hi = jnp.clip(shard_hi - base, 0, ref.shape[0])

        def load(shard, carry, ref=ref, base=base):
            at = pl.multiple_of((base + shard) * SHARD, SHARD)
            for slot in range(4):
                rows[slot, pl.ds(at, SHARD), :] = ref[shard, slot].astype(jnp.float32)
            return carry

        lax.fori_loop(lo, hi, load, 0)

    for edge in (shard_lo, jnp.maximum(shard_hi - 1, 0)):
        at = pl.multiple_of(edge * SHARD, SHARD)
        for slot in range(3):
            grads[slot, pl.ds(at, SHARD), :] = zero_shard

    def one_document(doc, carry):
        first = bounds_ref[doc] - window
        length = bounds_ref[doc + 1] - bounds_ref[doc]
        tiles = (length + STEP - 1) // STEP

        def fetch(tile, carry):
            at = pl.multiple_of(tile * STEP, STEP)
            inside = lax.broadcasted_iota(jnp.int32, (STEP, HD), 0) + at < length
            for slot, ref in enumerate((q_doc, k_doc, v_doc, g_doc)):
                part = jnp.where(inside, rows[slot, pl.ds(first + at, STEP), :], 0.0)
                ref[pl.ds(at, STEP), :] = part.astype(jnp.bfloat16)
                if slot == 1:
                    kt_doc[:, pl.ds(at, STEP)] = part.astype(jnp.bfloat16).T
            dk_acc[pl.ds(at, STEP), :] = zero_tile
            dv_acc[pl.ds(at, STEP), :] = zero_tile
            return carry

        lax.fori_loop(0, tiles, fetch, 0)

        def products(tile, to, size):
            at = pl.multiple_of(tile * STEP, STEP)
            s = lax.dot_general(
                k_doc[pl.ds(to, size), :], q_doc[pl.ds(at, STEP), :],
                (((1,), (1,)), ((), ())), preferred_element_type=jnp.float32)
            p = lax.dot_general(
                v_doc[pl.ds(to, size), :], g_doc[pl.ds(at, STEP), :],
                (((1,), (1,)), ((), ())), preferred_element_type=jnp.float32)
            return s, p

        def stats(scores, to, size, carry):
            s_all, p_all = scores
            for part in range(size // PART):
                top, total, dot = carry
                here = to + part * PART
                s = s_all[part * PART:(part + 1) * PART] * (SCALE * LOG2E)
                p = p_all[part * PART:(part + 1) * PART]
                if part >= (size - STEP) // PART:
                    inside = lax.broadcasted_iota(jnp.int32, (PART, STEP), 0) + here < length
                    s = jnp.where(inside, s, LOW)
                s = s.reshape(PART // 8, 8, STEP)
                new_top = jnp.maximum(top, jnp.max(s, axis=0))
                e = jnp.exp2(s - new_top[None])
                e_buf[pl.ds(here, PART), :] = e.reshape(PART, STEP)
                p_buf[pl.ds(here, PART), :] = p
                tops[to // PART + part] = new_top
                shrink = jnp.exp2(top - new_top)
                total = total * shrink + jnp.sum(e, axis=0)
                dot = dot * shrink + jnp.sum(e * p.reshape(PART // 8, 8, STEP), axis=0)
                carry = new_top, total, dot
            return carry

        def gradients(tile, to, size, norm, delta):
            at = pl.multiple_of(tile * STEP, STEP)
            weights, scores = [], []
            for part in range(size // PART):
                here = to + part * PART
                factor = jnp.exp2(tops[to // PART + part] - norm)
                e = e_buf[pl.ds(here, PART), :].reshape(PART // 8, 8, STEP) * factor[None]
                p = p_buf[pl.ds(here, PART), :].reshape(PART // 8, 8, STEP)
                scores.append((e * (p - delta[None])).reshape(PART, STEP).astype(jnp.bfloat16))
                weights.append(e.reshape(PART, STEP).astype(jnp.bfloat16))
            weights = jnp.concatenate(weights, axis=0)
            scores = jnp.concatenate(scores, axis=0)
            dv_acc[pl.ds(to, size), :] += jnp.dot(
                weights, g_doc[pl.ds(at, STEP), :], preferred_element_type=jnp.float32)
            dk_acc[pl.ds(to, size), :] += jnp.dot(
                scores, q_doc[pl.ds(at, STEP), :], preferred_element_type=jnp.float32)
            dq_acc[...] += jnp.dot(
                kt_doc[:, pl.ds(to, size)], scores, preferred_element_type=jnp.float32)

        def over_keys(body, carry):
            to = 0
            for wide in (4, 2, 1):
                size = wide * STEP
                steps = tiles // 4 if wide == 4 else (tiles // wide) % 2
                start = to

                def step(c, now, start=start, size=size):
                    return body(pl.multiple_of(start + c * size, STEP), size, now)

                carry = lax.fori_loop(0, steps, step, carry)
                to = start + steps * size
            return carry

        flat = jnp.zeros((8, STEP), jnp.float32)
        fresh = (flat + LOW, flat, flat)

        def joined(top, total, dot):
            peak = jnp.max(top, axis=0, keepdims=True)
            weight = jnp.exp2(top - peak)
            total = jnp.sum(total * weight, axis=0, keepdims=True)
            dot = jnp.sum(dot * weight, axis=0, keepdims=True)
            return flat + (peak + jnp.log2(total)), flat + dot / total

        def put_queries(tile):
            at = pl.multiple_of(tile * STEP, STEP)
            grads[0, pl.ds(first + at, STEP), :] = dq_acc[...].T * SCALE
            dq_acc[...] = jnp.zeros((HD, STEP), jnp.float32)

        dq_acc[...] = jnp.zeros((HD, STEP), jnp.float32)
        norm_now = joined(*over_keys(lambda to, size, now: stats(products(0, to, size), to, size, now), fresh))

        def query_tile(tile, norms):
            norm, delta = norms

            def both(to, size, now):
                scores = products(tile, to, size)
                gradients(tile - 1, to, size, norm, delta)
                return stats(scores, to, size, now)

            now = over_keys(both, fresh)
            put_queries(tile - 1)
            return joined(*now)

        norm, delta = lax.fori_loop(1, tiles, query_tile, norm_now)

        def rest(to, size, now):
            gradients(tiles - 1, to, size, norm, delta)
            return now

        over_keys(rest, 0)
        put_queries(tiles - 1)

        def put(tile, carry):
            at = pl.multiple_of(tile * STEP, STEP)
            grads[1, pl.ds(first + at, STEP), :] = dk_acc[pl.ds(at, STEP), :] * SCALE
            grads[2, pl.ds(first + at, STEP), :] = dv_acc[pl.ds(at, STEP), :]
            return carry

        lax.fori_loop(0, tiles, put, 0)
        return carry

    lax.fori_loop(doc_lo, doc_hi, one_document, 0)

    for _, ref, base in pieces:
        lo = jnp.clip(shard_lo - base, 0, ref.shape[0])
        hi = jnp.clip(shard_hi - base, 0, ref.shape[0])

        def empty(shard, carry, ref=ref):
            for slot in range(3):
                ref[shard, slot] = zero_shard.astype(jnp.bfloat16)
            return carry

        def store(shard, carry, ref=ref, base=base):
            at = pl.multiple_of((base + shard) * SHARD, SHARD)
            for slot in range(3):
                ref[shard, slot] = grads[slot, pl.ds(at, SHARD), :].astype(jnp.bfloat16)
            return carry

        lax.fori_loop(0, lo, empty, 0)
        lax.fori_loop(lo, hi, store, 0)
        lax.fori_loop(hi, ref.shape[0], empty, 0)


def attention(bounds, span, left, own, right):
    def shape(like):
        return jax.ShapeDtypeStruct((like.shape[0], 3, SHARD, HD), jnp.bfloat16)

    smem = pl.BlockSpec(memory_space=pltpu.SMEM)
    vmem = pl.BlockSpec(memory_space=pltpu.VMEM)
    padded = 3 * BLOCK + STEP
    return pl.pallas_call(
        attention_kernel,
        out_shape=(shape(left), shape(own), shape(right)),
        in_specs=[smem, smem, vmem, vmem, vmem],
        out_specs=(vmem, vmem, vmem),
        scratch_shapes=[
            pltpu.VMEM((4, padded, HD), jnp.float32),
            pltpu.VMEM((3, padded, HD), jnp.float32),
            pltpu.VMEM((MOST, HD), jnp.bfloat16),
            pltpu.VMEM((MOST, HD), jnp.bfloat16),
            pltpu.VMEM((MOST, HD), jnp.bfloat16),
            pltpu.VMEM((MOST, HD), jnp.bfloat16),
            pltpu.VMEM((HD, MOST), jnp.bfloat16),
            pltpu.VMEM((MOST, HD), jnp.float32),
            pltpu.VMEM((MOST, HD), jnp.float32),
            pltpu.VMEM((HD, STEP), jnp.float32),
            pltpu.VMEM((MOST, STEP), jnp.float32),
            pltpu.VMEM((MOST, STEP), jnp.float32),
            pltpu.VMEM((MOST // PART, 8, STEP), jnp.float32),
        ],
        compiler_params=pltpu.CompilerParams(vmem_limit_bytes=VMEM_LIMIT),
        cost_estimate=pl.CostEstimate(
            flops=5 * 2 * MOST * MOST * HD, bytes_accessed=6 * 1024 * 1024, transcendentals=2 * MOST * MOST
        ),
        name="attention",
    )(bounds, span, left, own, right)


def from_left(shard):
    devices = lax.axis_size("ctx")
    return lax.ppermute(shard, "ctx", [(i, i + 1) for i in range(devices - 1)])


def from_right(shard):
    devices = lax.axis_size("ctx")
    return lax.ppermute(shard, "ctx", [(i + 1, i) for i in range(devices - 1)])


def swap_heads(shard):
    return lax.all_to_all(shard, "head", split_axis=0, concat_axis=0, tiled=True)


def on_device(queries, key_rows, value_rows, out_grad, bounds):
    arrays = (queries, key_rows, value_rows, out_grad)
    owner = document_owner(bounds[:-1], bounds[1:])
    me = lax.axis_index("ctx")
    span = jnp.stack([jnp.sum(owner < me), jnp.sum(owner <= me)]).astype(jnp.int32)
    done, after = [], ()
    for parity in range(2):
        own = swap_heads(pack(parity, arrays, after))
        after = (own,)
        left = from_left(own)
        right = from_right(own)
        left_grad, own_grad, right_grad = attention(bounds, span, left, own, right)
        own_grad = own_grad + from_left(right_grad) + from_right(left_grad)
        done.append(swap_heads(own_grad))
    return unpack(*done)


def solution(mesh):
    rows = P(("ctx", "head"), None)
    return jax.shard_map(
        on_device,
        mesh=mesh,
        in_specs=(rows, rows, rows, rows, P()),
        out_specs=(rows, rows, rows),
        check_vma=False,
    )
```

```python
import jax
import jax.numpy as jnp
from jax import lax
from jax.experimental import pallas as pl
from jax.experimental.pallas import tpu as pltpu
from jax.sharding import PartitionSpec as P

HD = 128
NDOC = 64
BLOCK_BITS = 10
BLOCK = 1 << BLOCK_BITS
SHARD_BITS = 7
SHARD = 1 << SHARD_BITS
SHARDS = BLOCK // SHARD
STEP = 256
PART = 128
MOST = 2048
SCALE = HD ** -0.5
LOG2E = 1.4426950408889634
LOW = -1.0e30
VMEM_LIMIT = 48 * 1024 * 1024
VMEM_ALL = 64 * 1024 * 1024 - 256 * 1024


def pack_kernel(q_ref, k_ref, v_ref, g_ref, even_ref, odd_ref, held, sems):
    copies = []
    for slot, ref in enumerate((q_ref, k_ref, v_ref, g_ref)):
        copies.append(pltpu.make_async_copy(ref, held.at[slot], sems.at[slot]))
    for copy in copies:
        copy.start()
    for slot, copy in enumerate(copies):
        copy.wait()
        for peer in range(SHARDS):
            even_ref[peer, slot] = held[slot, :, pl.ds(2 * peer * HD, HD)]
            odd_ref[peer, slot] = held[slot, :, pl.ds((2 * peer + 1) * HD, HD)]


def pack(queries, key_rows, value_rows, out_grad):
    shape = jax.ShapeDtypeStruct((SHARDS, 4, SHARD, HD), jnp.bfloat16)
    return pl.pallas_call(
        pack_kernel,
        out_shape=(shape, shape),
        in_specs=[pl.BlockSpec(memory_space=pltpu.HBM)] * 4,
        scratch_shapes=[
            pltpu.VMEM((4, SHARD, 2 * SHARDS * HD), jnp.bfloat16),
            pltpu.SemaphoreType.DMA((4,)),
        ],
        compiler_params=pltpu.CompilerParams(vmem_limit_bytes=VMEM_ALL),
        name="pack",
    )(queries, key_rows, value_rows, out_grad)


def unpack_kernel(even_ref, odd_ref, dq_ref, dk_ref, dv_ref):
    for slot, ref in enumerate((dq_ref, dk_ref, dv_ref)):
        for peer in range(SHARDS):
            ref[:, pl.ds(2 * peer * HD, HD)] = even_ref[peer, slot]
            ref[:, pl.ds((2 * peer + 1) * HD, HD)] = odd_ref[peer, slot]


def unpack(even, odd):
    shape = jax.ShapeDtypeStruct((SHARD, 2 * SHARDS * HD), jnp.bfloat16)
    return pl.pallas_call(
        unpack_kernel,
        out_shape=(shape, shape, shape),
        compiler_params=pltpu.CompilerParams(vmem_limit_bytes=VMEM_LIMIT),
        name="unpack",
    )(even, odd)


def document_owner(first, end):
    first_block = first >> BLOCK_BITS
    last_block = (end - 1) >> BLOCK_BITS
    edge = last_block << BLOCK_BITS
    right_larger = (end - edge) > (edge - first)
    span = last_block - first_block
    return first_block + jnp.where((span == 2) | ((span == 1) & right_larger), 1, 0)


def attention_kernel(
    bounds_ref, span_ref, pair_ref, other_ref,
    left_out, own_out, right_out,
    rows, grads, q_doc, k_doc, v_doc, g_doc, kt_doc, dk_acc, dv_acc, dq_acc, e_buf, p_buf, tops,
):
    window = (lax.axis_index("ctx") - 1) * BLOCK
    odd = lax.rem(lax.axis_index("ctx"), 2)
    pieces = ((left_out, 0), (own_out, SHARDS), (right_out, 2 * SHARDS))
    sources = (
        (other_ref, 0, 1 - odd, 0), (pair_ref, 0, odd, 0),
        (pair_ref, odd, 1, SHARDS),
        (pair_ref, 1, 1 - odd, 2 * SHARDS), (other_ref, 1, odd, 2 * SHARDS),
    )

    doc_lo, doc_hi = span_ref[0], span_ref[1]
    some = doc_hi > doc_lo
    shard_lo = jnp.where(some, (bounds_ref[doc_lo] - window) >> SHARD_BITS, 0)
    shard_hi = jnp.where(some, (bounds_ref[doc_hi] - window + SHARD - 1) >> SHARD_BITS, 0)
    zero_tile = jnp.zeros((STEP, HD), jnp.float32)
    zero_shard = jnp.zeros((SHARD, HD), jnp.float32)

    for ref, place, used, base in sources:
        lo = jnp.clip(shard_lo - base, 0, SHARDS)
        hi = jnp.clip(shard_hi - base, 0, SHARDS)

        def load(shard, carry, ref=ref, place=place, base=base):
            at = pl.multiple_of((base + shard) * SHARD, SHARD)
            for slot in range(4):
                rows[slot, pl.ds(at, SHARD), :] = ref[place, shard, slot].astype(jnp.float32)
            return carry

        lax.fori_loop(lo, lo + (hi - lo) * used, load, 0)

    for edge in (shard_lo, jnp.maximum(shard_hi - 1, 0)):
        at = pl.multiple_of(edge * SHARD, SHARD)
        for slot in range(3):
            grads[slot, pl.ds(at, SHARD), :] = zero_shard

    def one_document(doc, carry):
        first = bounds_ref[doc] - window
        length = bounds_ref[doc + 1] - bounds_ref[doc]
        tiles = (length + STEP - 1) // STEP

        def fetch(tile, carry):
            at = pl.multiple_of(tile * STEP, STEP)
            inside = lax.broadcasted_iota(jnp.int32, (STEP, HD), 0) + at < length
            for slot, ref in enumerate((q_doc, k_doc, v_doc, g_doc)):
                part = jnp.where(inside, rows[slot, pl.ds(first + at, STEP), :], 0.0)
                ref[pl.ds(at, STEP), :] = part.astype(jnp.bfloat16)
                if slot == 1:
                    kt_doc[:, pl.ds(at, STEP)] = part.astype(jnp.bfloat16).T
            dk_acc[pl.ds(at, STEP), :] = zero_tile
            dv_acc[pl.ds(at, STEP), :] = zero_tile
            return carry

        lax.fori_loop(0, tiles, fetch, 0)

        def products(tile, to, size):
            at = pl.multiple_of(tile * STEP, STEP)
            s = lax.dot_general(
                k_doc[pl.ds(to, size), :], q_doc[pl.ds(at, STEP), :],
                (((1,), (1,)), ((), ())), preferred_element_type=jnp.float32)
            p = lax.dot_general(
                v_doc[pl.ds(to, size), :], g_doc[pl.ds(at, STEP), :],
                (((1,), (1,)), ((), ())), preferred_element_type=jnp.float32)
            return s, p

        def stats(scores, to, size, carry):
            s_all, p_all = scores
            for part in range(size // PART):
                top, total, dot = carry
                here = to + part * PART
                s = s_all[part * PART:(part + 1) * PART] * (SCALE * LOG2E)
                p = p_all[part * PART:(part + 1) * PART]
                if part >= (size - STEP) // PART:
                    inside = lax.broadcasted_iota(jnp.int32, (PART, STEP), 0) + here < length
                    s = jnp.where(inside, s, LOW)
                s = s.reshape(PART // 8, 8, STEP)
                new_top = jnp.maximum(top, jnp.max(s, axis=0))
                e = jnp.exp2(s - new_top[None])
                e_buf[pl.ds(here, PART), :] = e.reshape(PART, STEP)
                p_buf[pl.ds(here, PART), :] = p
                tops[to // PART + part] = new_top
                shrink = jnp.exp2(top - new_top)
                total = total * shrink + jnp.sum(e, axis=0)
                dot = dot * shrink + jnp.sum(e * p.reshape(PART // 8, 8, STEP), axis=0)
                carry = new_top, total, dot
            return carry

        def gradients(tile, to, size, norm, delta):
            at = pl.multiple_of(tile * STEP, STEP)
            weights, scores = [], []
            for part in range(size // PART):
                here = to + part * PART
                factor = jnp.exp2(tops[to // PART + part] - norm)
                e = e_buf[pl.ds(here, PART), :].reshape(PART // 8, 8, STEP) * factor[None]
                p = p_buf[pl.ds(here, PART), :].reshape(PART // 8, 8, STEP)
                scores.append((e * (p - delta[None])).reshape(PART, STEP).astype(jnp.bfloat16))
                weights.append(e.reshape(PART, STEP).astype(jnp.bfloat16))
            weights = jnp.concatenate(weights, axis=0)
            scores = jnp.concatenate(scores, axis=0)
            dv_acc[pl.ds(to, size), :] += jnp.dot(
                weights, g_doc[pl.ds(at, STEP), :], preferred_element_type=jnp.float32)
            dk_acc[pl.ds(to, size), :] += jnp.dot(
                scores, q_doc[pl.ds(at, STEP), :], preferred_element_type=jnp.float32)
            dq_acc[...] += jnp.dot(
                kt_doc[:, pl.ds(to, size)], scores, preferred_element_type=jnp.float32)

        def over_keys(body, carry):
            to = 0
            for wide in (4, 2, 1):
                size = wide * STEP
                steps = tiles // 4 if wide == 4 else (tiles // wide) % 2
                start = to

                def step(c, now, start=start, size=size):
                    return body(pl.multiple_of(start + c * size, STEP), size, now)

                carry = lax.fori_loop(0, steps, step, carry)
                to = start + steps * size
            return carry

        flat = jnp.zeros((8, STEP), jnp.float32)
        fresh = (flat + LOW, flat, flat)

        def joined(top, total, dot):
            peak = jnp.max(top, axis=0, keepdims=True)
            weight = jnp.exp2(top - peak)
            total = jnp.sum(total * weight, axis=0, keepdims=True)
            dot = jnp.sum(dot * weight, axis=0, keepdims=True)
            return flat + (peak + jnp.log2(total)), flat + dot / total

        def put_queries(tile):
            at = pl.multiple_of(tile * STEP, STEP)
            grads[0, pl.ds(first + at, STEP), :] = dq_acc[...].T * SCALE
            dq_acc[...] = jnp.zeros((HD, STEP), jnp.float32)

        dq_acc[...] = jnp.zeros((HD, STEP), jnp.float32)
        norm_now = joined(*over_keys(lambda to, size, now: stats(products(0, to, size), to, size, now), fresh))

        def query_tile(tile, norms):
            norm, delta = norms

            def both(to, size, now):
                scores = products(tile, to, size)
                gradients(tile - 1, to, size, norm, delta)
                return stats(scores, to, size, now)

            now = over_keys(both, fresh)
            put_queries(tile - 1)
            return joined(*now)

        norm, delta = lax.fori_loop(1, tiles, query_tile, norm_now)

        def rest(to, size, now):
            gradients(tiles - 1, to, size, norm, delta)
            return now

        over_keys(rest, 0)
        put_queries(tiles - 1)

        def put(tile, carry):
            at = pl.multiple_of(tile * STEP, STEP)
            grads[1, pl.ds(first + at, STEP), :] = dk_acc[pl.ds(at, STEP), :] * SCALE
            grads[2, pl.ds(first + at, STEP), :] = dv_acc[pl.ds(at, STEP), :]
            return carry

        lax.fori_loop(0, tiles, put, 0)
        return carry

    lax.fori_loop(doc_lo, doc_hi, one_document, 0)

    for ref, base in pieces:
        lo = jnp.clip(shard_lo - base, 0, ref.shape[0])
        hi = jnp.clip(shard_hi - base, 0, ref.shape[0])

        def empty(shard, carry, ref=ref):
            for slot in range(3):
                ref[shard, slot] = zero_shard.astype(jnp.bfloat16)
            return carry

        def store(shard, carry, ref=ref, base=base):
            at = pl.multiple_of((base + shard) * SHARD, SHARD)
            for slot in range(3):
                ref[shard, slot] = grads[slot, pl.ds(at, SHARD), :].astype(jnp.bfloat16)
            return carry

        lax.fori_loop(0, lo, empty, 0)
        lax.fori_loop(lo, hi, store, 0)
        lax.fori_loop(hi, ref.shape[0], empty, 0)


def attention(bounds, span, pair, other):
    shape = jax.ShapeDtypeStruct((SHARDS, 3, SHARD, HD), jnp.bfloat16)
    smem = pl.BlockSpec(memory_space=pltpu.SMEM)
    vmem = pl.BlockSpec(memory_space=pltpu.VMEM)
    padded = 3 * BLOCK + STEP
    return pl.pallas_call(
        attention_kernel,
        out_shape=(shape, shape, shape),
        in_specs=[smem, smem, vmem, vmem],
        out_specs=(vmem, vmem, vmem),
        scratch_shapes=[
            pltpu.VMEM((4, padded, HD), jnp.float32),
            pltpu.VMEM((3, padded, HD), jnp.float32),
            pltpu.VMEM((MOST, HD), jnp.bfloat16),
            pltpu.VMEM((MOST, HD), jnp.bfloat16),
            pltpu.VMEM((MOST, HD), jnp.bfloat16),
            pltpu.VMEM((MOST, HD), jnp.bfloat16),
            pltpu.VMEM((HD, MOST), jnp.bfloat16),
            pltpu.VMEM((MOST, HD), jnp.float32),
            pltpu.VMEM((MOST, HD), jnp.float32),
            pltpu.VMEM((HD, STEP), jnp.float32),
            pltpu.VMEM((MOST, STEP), jnp.float32),
            pltpu.VMEM((MOST, STEP), jnp.float32),
            pltpu.VMEM((MOST // PART, 8, STEP), jnp.float32),
        ],
        compiler_params=pltpu.CompilerParams(vmem_limit_bytes=VMEM_ALL),
        cost_estimate=pl.CostEstimate(
            flops=5 * 2 * MOST * MOST * HD, bytes_accessed=6 * 1024 * 1024, transcendentals=2 * MOST * MOST
        ),
        name="attention",
    )(bounds, span, pair, other)


def with_neighbour(shard, shift):
    devices = lax.axis_size("ctx")
    groups = [[(i + shift) % devices, (i + 1 + shift) % devices] for i in range(0, devices, 2)]
    return lax.all_gather(shard, "ctx", axis_index_groups=groups)


def from_left(shard):
    devices = lax.axis_size("ctx")
    return lax.ppermute(shard, "ctx", [(i, i + 1) for i in range(devices - 1)])


def from_right(shard):
    devices = lax.axis_size("ctx")
    return lax.ppermute(shard, "ctx", [(i + 1, i) for i in range(devices - 1)])


def swap_heads(shard):
    return lax.all_to_all(shard, "head", split_axis=0, concat_axis=0, tiled=True)


def on_device(queries, key_rows, value_rows, out_grad, bounds):
    arrays = (queries, key_rows, value_rows, out_grad)
    owner = document_owner(bounds[:-1], bounds[1:])
    me = lax.axis_index("ctx")
    span = jnp.stack([jnp.sum(owner < me), jnp.sum(owner <= me)]).astype(jnp.int32)
    done = []
    for packed in pack(*arrays):
        own = swap_heads(packed)
        left_grad, own_grad, right_grad = attention(bounds, span, with_neighbour(own, 0), with_neighbour(own, 1))
        own_grad = own_grad + from_left(right_grad) + from_right(left_grad)
        done.append(swap_heads(own_grad))
    return unpack(*done)


def solution(mesh):
    rows = P(("ctx", "head"), None)
    return jax.shard_map(
        on_device,
        mesh=mesh,
        in_specs=(rows, rows, rows, rows, P()),
        out_specs=(rows, rows, rows),
        check_vma=False,
    )
```

```python
import jax
import jax.numpy as jnp
from jax import lax
from jax.experimental import pallas as pl
from jax.experimental.pallas import tpu as pltpu
from jax.sharding import PartitionSpec as P

HD = 128
NDOC = 64
BLOCK_BITS = 10
BLOCK = 1 << BLOCK_BITS
SHARD_BITS = 7
SHARD = 1 << SHARD_BITS
SHARDS = BLOCK // SHARD
STEP = 256
PART = 64
MOST = 2048
SCALE = HD ** -0.5
LOG2E = 1.4426950408889634
LOW = -1.0e30
VMEM_LIMIT = 48 * 1024 * 1024
VMEM_ALL = 64 * 1024 * 1024 - 256 * 1024


def pack_kernel(q_ref, k_ref, v_ref, g_ref, even_ref, odd_ref, held, sems):
    copies = []
    for slot, ref in enumerate((q_ref, k_ref, v_ref, g_ref)):
        copies.append(pltpu.make_async_copy(ref, held.at[slot], sems.at[slot]))
    for copy in copies:
        copy.start()
    for slot, copy in enumerate(copies):
        copy.wait()
        for peer in range(SHARDS):
            even_ref[peer, slot] = held[slot, :, pl.ds(2 * peer * HD, HD)]
            odd_ref[peer, slot] = held[slot, :, pl.ds((2 * peer + 1) * HD, HD)]


def pack(queries, key_rows, value_rows, out_grad):
    shape = jax.ShapeDtypeStruct((SHARDS, 4, SHARD, HD), jnp.bfloat16)
    return pl.pallas_call(
        pack_kernel,
        out_shape=(shape, shape),
        in_specs=[pl.BlockSpec(memory_space=pltpu.HBM)] * 4,
        scratch_shapes=[
            pltpu.VMEM((4, SHARD, 2 * SHARDS * HD), jnp.bfloat16),
            pltpu.SemaphoreType.DMA((4,)),
        ],
        compiler_params=pltpu.CompilerParams(vmem_limit_bytes=VMEM_ALL),
        name="pack",
    )(queries, key_rows, value_rows, out_grad)


def unpack_kernel(even_ref, odd_ref, dq_ref, dk_ref, dv_ref):
    for slot, ref in enumerate((dq_ref, dk_ref, dv_ref)):
        for peer in range(SHARDS):
            ref[:, pl.ds(2 * peer * HD, HD)] = even_ref[peer, slot]
            ref[:, pl.ds((2 * peer + 1) * HD, HD)] = odd_ref[peer, slot]


def unpack(even, odd):
    shape = jax.ShapeDtypeStruct((SHARD, 2 * SHARDS * HD), jnp.bfloat16)
    return pl.pallas_call(
        unpack_kernel,
        out_shape=(shape, shape, shape),
        compiler_params=pltpu.CompilerParams(vmem_limit_bytes=VMEM_LIMIT),
        name="unpack",
    )(even, odd)


def document_owner(first, end):
    first_block = first >> BLOCK_BITS
    last_block = (end - 1) >> BLOCK_BITS
    edge = last_block << BLOCK_BITS
    right_larger = (end - edge) > (edge - first)
    span = last_block - first_block
    return first_block + jnp.where((span == 2) | ((span == 1) & right_larger), 1, 0)


def attention_kernel(
    bounds_ref, span_ref, left_ref, own_ref, right_ref,
    left_out, own_out, right_out,
    rows, grads, q_doc, k_doc, v_doc, g_doc, kt_doc, dk_acc, dv_acc, dq_acc, e_buf, p_buf, tops,
):
    window = (lax.axis_index("ctx") - 1) * BLOCK
    pieces = ((left_ref, left_out, 0), (own_ref, own_out, SHARDS), (right_ref, right_out, 2 * SHARDS))

    doc_lo, doc_hi = span_ref[0], span_ref[1]
    some = doc_hi > doc_lo
    shard_lo = jnp.where(some, (bounds_ref[doc_lo] - window) >> SHARD_BITS, 0)
    shard_hi = jnp.where(some, (bounds_ref[doc_hi] - window + SHARD - 1) >> SHARD_BITS, 0)
    zero_tile = jnp.zeros((STEP, HD), jnp.float32)
    zero_shard = jnp.zeros((SHARD, HD), jnp.float32)

    for ref, _, base in pieces:
        lo = jnp.clip(shard_lo - base, 0, ref.shape[0])
        hi = jnp.clip(shard_hi - base, 0, ref.shape[0])

        def load(shard, carry, ref=ref, base=base):
            at = pl.multiple_of((base + shard) * SHARD, SHARD)
            for slot in range(4):
                rows[slot, pl.ds(at, SHARD), :] = ref[shard, slot].astype(jnp.float32)
            return carry

        lax.fori_loop(lo, hi, load, 0)

    for edge in (shard_lo, jnp.maximum(shard_hi - 1, 0)):
        at = pl.multiple_of(edge * SHARD, SHARD)
        for slot in range(3):
            grads[slot, pl.ds(at, SHARD), :] = zero_shard

    def one_document(doc, carry):
        first = bounds_ref[doc] - window
        length = bounds_ref[doc + 1] - bounds_ref[doc]
        tiles = (length + STEP - 1) // STEP

        def fetch(tile, carry):
            at = pl.multiple_of(tile * STEP, STEP)
            inside = lax.broadcasted_iota(jnp.int32, (STEP, HD), 0) + at < length
            for slot, ref in enumerate((q_doc, k_doc, v_doc, g_doc)):
                part = jnp.where(inside, rows[slot, pl.ds(first + at, STEP), :], 0.0)
                ref[pl.ds(at, STEP), :] = part.astype(jnp.bfloat16)
                if slot == 1:
                    kt_doc[:, pl.ds(at, STEP)] = part.astype(jnp.bfloat16).T
            dk_acc[pl.ds(at, STEP), :] = zero_tile
            dv_acc[pl.ds(at, STEP), :] = zero_tile
            return carry

        lax.fori_loop(0, tiles, fetch, 0)

        def products(tile, to, size):
            at = pl.multiple_of(tile * STEP, STEP)
            s = lax.dot_general(
                k_doc[pl.ds(to, size), :], q_doc[pl.ds(at, STEP), :],
                (((1,), (1,)), ((), ())), preferred_element_type=jnp.float32)
            p = lax.dot_general(
                v_doc[pl.ds(to, size), :], g_doc[pl.ds(at, STEP), :],
                (((1,), (1,)), ((), ())), preferred_element_type=jnp.float32)
            return s, p

        def stats(scores, to, size, carry):
            s_all, p_all = scores
            for part in range(size // PART):
                top, total, dot = carry
                here = to + part * PART
                s = s_all[part * PART:(part + 1) * PART] * (SCALE * LOG2E)
                p = p_all[part * PART:(part + 1) * PART]
                if part >= (size - STEP) // PART:
                    inside = lax.broadcasted_iota(jnp.int32, (PART, STEP), 0) + here < length
                    s = jnp.where(inside, s, LOW)
                s = s.reshape(PART // 8, 8, STEP)
                new_top = jnp.maximum(top, jnp.max(s, axis=0))
                e = jnp.exp2(s - new_top[None])
                e_buf[pl.ds(here, PART), :] = e.reshape(PART, STEP)
                p_buf[pl.ds(here, PART), :] = p
                tops[to // PART + part] = new_top
                shrink = jnp.exp2(top - new_top)
                total = total * shrink + jnp.sum(e, axis=0)
                dot = dot * shrink + jnp.sum(e * p.reshape(PART // 8, 8, STEP), axis=0)
                carry = new_top, total, dot
            return carry

        def gradients(tile, to, size, norm, delta):
            at = pl.multiple_of(tile * STEP, STEP)
            weights, scores = [], []
            for part in range(size // PART):
                here = to + part * PART
                factor = jnp.exp2(tops[to // PART + part] - norm)
                e = e_buf[pl.ds(here, PART), :].reshape(PART // 8, 8, STEP) * factor[None]
                p = p_buf[pl.ds(here, PART), :].reshape(PART // 8, 8, STEP)
                scores.append((e * (p - delta[None])).reshape(PART, STEP).astype(jnp.bfloat16))
                weights.append(e.reshape(PART, STEP).astype(jnp.bfloat16))
            weights = jnp.concatenate(weights, axis=0)
            scores = jnp.concatenate(scores, axis=0)
            dv_acc[pl.ds(to, size), :] += jnp.dot(
                weights, g_doc[pl.ds(at, STEP), :], preferred_element_type=jnp.float32)
            dk_acc[pl.ds(to, size), :] += jnp.dot(
                scores, q_doc[pl.ds(at, STEP), :], preferred_element_type=jnp.float32)
            dq_acc[...] += jnp.dot(
                kt_doc[:, pl.ds(to, size)], scores, preferred_element_type=jnp.float32)

        def over_keys(body, carry):
            to = 0
            for wide in (4, 2, 1):
                size = wide * STEP
                steps = tiles // 4 if wide == 4 else (tiles // wide) % 2
                start = to

                def step(c, now, start=start, size=size):
                    return body(pl.multiple_of(start + c * size, STEP), size, now)

                carry = lax.fori_loop(0, steps, step, carry)
                to = start + steps * size
            return carry

        flat = jnp.zeros((8, STEP), jnp.float32)
        fresh = (flat + LOW, flat, flat)

        def joined(top, total, dot):
            peak = jnp.max(top, axis=0, keepdims=True)
            weight = jnp.exp2(top - peak)
            total = jnp.sum(total * weight, axis=0, keepdims=True)
            dot = jnp.sum(dot * weight, axis=0, keepdims=True)
            return flat + (peak + jnp.log2(total)), flat + dot / total

        def put_queries(tile):
            at = pl.multiple_of(tile * STEP, STEP)
            grads[0, pl.ds(first + at, STEP), :] = dq_acc[...].T * SCALE
            dq_acc[...] = jnp.zeros((HD, STEP), jnp.float32)

        dq_acc[...] = jnp.zeros((HD, STEP), jnp.float32)
        norm_now = joined(*over_keys(lambda to, size, now: stats(products(0, to, size), to, size, now), fresh))

        def query_tile(tile, norms):
            norm, delta = norms

            def both(to, size, now):
                scores = products(tile, to, size)
                gradients(tile - 1, to, size, norm, delta)
                return stats(scores, to, size, now)

            now = over_keys(both, fresh)
            put_queries(tile - 1)
            return joined(*now)

        norm, delta = lax.fori_loop(1, tiles, query_tile, norm_now)

        def rest(to, size, now):
            gradients(tiles - 1, to, size, norm, delta)
            return now

        over_keys(rest, 0)
        put_queries(tiles - 1)

        def put(tile, carry):
            at = pl.multiple_of(tile * STEP, STEP)
            grads[1, pl.ds(first + at, STEP), :] = dk_acc[pl.ds(at, STEP), :] * SCALE
            grads[2, pl.ds(first + at, STEP), :] = dv_acc[pl.ds(at, STEP), :]
            return carry

        lax.fori_loop(0, tiles, put, 0)
        return carry

    lax.fori_loop(doc_lo, doc_hi, one_document, 0)

    for _, ref, base in pieces:
        lo = jnp.clip(shard_lo - base, 0, ref.shape[0])
        hi = jnp.clip(shard_hi - base, 0, ref.shape[0])

        def empty(shard, carry, ref=ref):
            for slot in range(3):
                ref[shard, slot] = zero_shard.astype(jnp.bfloat16)
            return carry

        def store(shard, carry, ref=ref, base=base):
            at = pl.multiple_of((base + shard) * SHARD, SHARD)
            for slot in range(3):
                ref[shard, slot] = grads[slot, pl.ds(at, SHARD), :].astype(jnp.bfloat16)
            return carry

        lax.fori_loop(0, lo, empty, 0)
        lax.fori_loop(lo, hi, store, 0)
        lax.fori_loop(hi, ref.shape[0], empty, 0)


def attention(bounds, span, left, own, right):
    shape = jax.ShapeDtypeStruct((SHARDS, 3, SHARD, HD), jnp.bfloat16)
    smem = pl.BlockSpec(memory_space=pltpu.SMEM)
    vmem = pl.BlockSpec(memory_space=pltpu.VMEM)
    padded = 3 * BLOCK + STEP
    return pl.pallas_call(
        attention_kernel,
        out_shape=(shape, shape, shape),
        in_specs=[smem, smem, vmem, vmem, vmem],
        out_specs=(vmem, vmem, vmem),
        scratch_shapes=[
            pltpu.VMEM((4, padded, HD), jnp.float32),
            pltpu.VMEM((3, padded, HD), jnp.float32),
            pltpu.VMEM((MOST, HD), jnp.bfloat16),
            pltpu.VMEM((MOST, HD), jnp.bfloat16),
            pltpu.VMEM((MOST, HD), jnp.bfloat16),
            pltpu.VMEM((MOST, HD), jnp.bfloat16),
            pltpu.VMEM((HD, MOST), jnp.bfloat16),
            pltpu.VMEM((MOST, HD), jnp.float32),
            pltpu.VMEM((MOST, HD), jnp.float32),
            pltpu.VMEM((HD, STEP), jnp.float32),
            pltpu.VMEM((MOST, STEP), jnp.float32),
            pltpu.VMEM((MOST, STEP), jnp.float32),
            pltpu.VMEM((MOST // PART, 8, STEP), jnp.float32),
        ],
        compiler_params=pltpu.CompilerParams(vmem_limit_bytes=VMEM_LIMIT),
        cost_estimate=pl.CostEstimate(
            flops=5 * 2 * MOST * MOST * HD, bytes_accessed=6 * 1024 * 1024, transcendentals=2 * MOST * MOST
        ),
        name="attention",
    )(bounds, span, left, own, right)


def from_left(shard):
    devices = lax.axis_size("ctx")
    return lax.ppermute(shard, "ctx", [(i, i + 1) for i in range(devices - 1)])


def from_right(shard):
    devices = lax.axis_size("ctx")
    return lax.ppermute(shard, "ctx", [(i + 1, i) for i in range(devices - 1)])


def swap_heads(shard):
    return lax.all_to_all(shard, "head", split_axis=0, concat_axis=0, tiled=True)


def on_device(queries, key_rows, value_rows, out_grad, bounds):
    owner = document_owner(bounds[:-1], bounds[1:])
    me = lax.axis_index("ctx")
    span = jnp.stack([jnp.sum(owner < me), jnp.sum(owner <= me)]).astype(jnp.int32)
    done = []
    for packed in pack(queries, key_rows, value_rows, out_grad):
        own = swap_heads(packed)
        left = from_left(own)
        right = from_right(own)
        left_grad, own_grad, right_grad = attention(bounds, span, left, own, right)
        own_grad = own_grad + from_left(right_grad) + from_right(left_grad)
        done.append(swap_heads(own_grad))
    return unpack(*done)


def solution(mesh):
    rows = P(("ctx", "head"), None)
    return jax.shard_map(
        on_device,
        mesh=mesh,
        in_specs=(rows, rows, rows, rows, P()),
        out_specs=(rows, rows, rows),
        check_vma=False,
    )
```

```python
import jax
import jax.numpy as jnp
from jax import lax
from jax.experimental import pallas as pl
from jax.experimental.pallas import tpu as pltpu
from jax.sharding import PartitionSpec as P

HD = 128
NDOC = 64
BLOCK_BITS = 10
BLOCK = 1 << BLOCK_BITS
SHARD_BITS = 7
SHARD = 1 << SHARD_BITS
SHARDS = BLOCK // SHARD
STEP = 256
QSTEP = 512
PART = 64
MOST = 2048
SCALE = HD ** -0.5
LOG2E = 1.4426950408889634
LOW = -1.0e30
VMEM_LIMIT = 48 * 1024 * 1024
VMEM_ALL = 64 * 1024 * 1024 - 256 * 1024


def pack_kernel(q_ref, k_ref, v_ref, g_ref, even_ref, odd_ref, held, sems):
    copies = []
    for slot, ref in enumerate((q_ref, k_ref, v_ref, g_ref)):
        copies.append(pltpu.make_async_copy(ref, held.at[slot], sems.at[slot]))
    for copy in copies:
        copy.start()
    for slot, copy in enumerate(copies):
        copy.wait()
        for peer in range(SHARDS):
            even_ref[peer, slot] = held[slot, :, pl.ds(2 * peer * HD, HD)]
            odd_ref[peer, slot] = held[slot, :, pl.ds((2 * peer + 1) * HD, HD)]


def pack(queries, key_rows, value_rows, out_grad):
    shape = jax.ShapeDtypeStruct((SHARDS, 4, SHARD, HD), jnp.bfloat16)
    return pl.pallas_call(
        pack_kernel,
        out_shape=(shape, shape),
        in_specs=[pl.BlockSpec(memory_space=pltpu.HBM)] * 4,
        scratch_shapes=[
            pltpu.VMEM((4, SHARD, 2 * SHARDS * HD), jnp.bfloat16),
            pltpu.SemaphoreType.DMA((4,)),
        ],
        compiler_params=pltpu.CompilerParams(vmem_limit_bytes=VMEM_ALL),
        name="pack",
    )(queries, key_rows, value_rows, out_grad)


def unpack_kernel(even_ref, odd_ref, dq_ref, dk_ref, dv_ref):
    for slot, ref in enumerate((dq_ref, dk_ref, dv_ref)):
        for peer in range(SHARDS):
            ref[:, pl.ds(2 * peer * HD, HD)] = even_ref[peer, slot]
            ref[:, pl.ds((2 * peer + 1) * HD, HD)] = odd_ref[peer, slot]


def unpack(even, odd):
    shape = jax.ShapeDtypeStruct((SHARD, 2 * SHARDS * HD), jnp.bfloat16)
    return pl.pallas_call(
        unpack_kernel,
        out_shape=(shape, shape, shape),
        compiler_params=pltpu.CompilerParams(vmem_limit_bytes=VMEM_LIMIT),
        name="unpack",
    )(even, odd)


def document_owner(first, end):
    first_block = first >> BLOCK_BITS
    last_block = (end - 1) >> BLOCK_BITS
    edge = last_block << BLOCK_BITS
    right_larger = (end - edge) > (edge - first)
    span = last_block - first_block
    return first_block + jnp.where((span == 2) | ((span == 1) & right_larger), 1, 0)


def attention_kernel(
    bounds_ref, span_ref, left_ref, own_ref, right_ref,
    left_out, own_out, right_out,
    rows, grads, q_doc, k_doc, v_doc, g_doc, kt_doc, dk_acc, dv_acc, dq_acc, e_buf, p_buf, tops,
):
    window = (lax.axis_index("ctx") - 1) * BLOCK
    pieces = ((left_ref, left_out, 0), (own_ref, own_out, SHARDS), (right_ref, right_out, 2 * SHARDS))

    doc_lo, doc_hi = span_ref[0], span_ref[1]
    some = doc_hi > doc_lo
    shard_lo = jnp.where(some, (bounds_ref[doc_lo] - window) >> SHARD_BITS, 0)
    shard_hi = jnp.where(some, (bounds_ref[doc_hi] - window + SHARD - 1) >> SHARD_BITS, 0)
    zero_tile = jnp.zeros((STEP, HD), jnp.float32)
    zero_shard = jnp.zeros((SHARD, HD), jnp.float32)

    for ref, _, base in pieces:
        lo = jnp.clip(shard_lo - base, 0, ref.shape[0])
        hi = jnp.clip(shard_hi - base, 0, ref.shape[0])

        def load(shard, carry, ref=ref, base=base):
            at = pl.multiple_of((base + shard) * SHARD, SHARD)
            for slot in range(4):
                rows[slot, pl.ds(at, SHARD), :] = ref[shard, slot].astype(jnp.float32)
            return carry

        lax.fori_loop(lo, hi, load, 0)

    for edge in (shard_lo, jnp.maximum(shard_hi - 1, 0)):
        at = pl.multiple_of(edge * SHARD, SHARD)
        for slot in range(3):
            grads[slot, pl.ds(at, SHARD), :] = zero_shard

    def one_document(doc, carry):
        first = bounds_ref[doc] - window
        length = bounds_ref[doc + 1] - bounds_ref[doc]
        tiles = (length + STEP - 1) // STEP
        q_tiles = (length + QSTEP - 1) // QSTEP

        def fetch(tile, carry):
            at = pl.multiple_of(tile * STEP, STEP)
            inside = lax.broadcasted_iota(jnp.int32, (STEP, HD), 0) + at < length
            for slot, ref in enumerate((q_doc, k_doc, v_doc, g_doc)):
                part = jnp.where(inside, rows[slot, pl.ds(first + at, STEP), :], 0.0)
                ref[pl.ds(at, STEP), :] = part.astype(jnp.bfloat16)
                if slot == 1:
                    kt_doc[:, pl.ds(at, STEP)] = part.astype(jnp.bfloat16).T
            dk_acc[pl.ds(at, STEP), :] = zero_tile
            dv_acc[pl.ds(at, STEP), :] = zero_tile
            return carry

        lax.fori_loop(0, q_tiles * (QSTEP // STEP), fetch, 0)

        def products(tile, to, size):
            at = pl.multiple_of(tile * QSTEP, QSTEP)
            s = lax.dot_general(
                k_doc[pl.ds(to, size), :], q_doc[pl.ds(at, QSTEP), :],
                (((1,), (1,)), ((), ())), preferred_element_type=jnp.float32)
            p = lax.dot_general(
                v_doc[pl.ds(to, size), :], g_doc[pl.ds(at, QSTEP), :],
                (((1,), (1,)), ((), ())), preferred_element_type=jnp.float32)
            return s, p

        def stats(scores, to, size, carry):
            s_all, p_all = scores
            for part in range(size // PART):
                top, total, dot = carry
                here = to + part * PART
                s = s_all[part * PART:(part + 1) * PART] * (SCALE * LOG2E)
                p = p_all[part * PART:(part + 1) * PART]
                if part >= (size - STEP) // PART:
                    inside = lax.broadcasted_iota(jnp.int32, (PART, QSTEP), 0) + here < length
                    s = jnp.where(inside, s, LOW)
                s = s.reshape(PART // 8, 8, QSTEP)
                new_top = jnp.maximum(top, jnp.max(s, axis=0))
                e = jnp.exp2(s - new_top[None])
                e_buf[pl.ds(here, PART), :] = e.reshape(PART, QSTEP)
                p_buf[pl.ds(here, PART), :] = p
                tops[to // PART + part] = new_top
                shrink = jnp.exp2(top - new_top)
                total = total * shrink + jnp.sum(e, axis=0)
                dot = dot * shrink + jnp.sum(e * p.reshape(PART // 8, 8, QSTEP), axis=0)
                carry = new_top, total, dot
            return carry

        def gradients(tile, to, size, norm, delta):
            at = pl.multiple_of(tile * QSTEP, QSTEP)
            weights, scores = [], []
            for part in range(size // PART):
                here = to + part * PART
                factor = jnp.exp2(tops[to // PART + part] - norm)
                e = e_buf[pl.ds(here, PART), :].reshape(PART // 8, 8, QSTEP) * factor[None]
                p = p_buf[pl.ds(here, PART), :].reshape(PART // 8, 8, QSTEP)
                scores.append((e * (p - delta[None])).reshape(PART, QSTEP).astype(jnp.bfloat16))
                weights.append(e.reshape(PART, QSTEP).astype(jnp.bfloat16))
            weights = jnp.concatenate(weights, axis=0)
            scores = jnp.concatenate(scores, axis=0)
            dv_acc[pl.ds(to, size), :] += jnp.dot(
                weights, g_doc[pl.ds(at, QSTEP), :], preferred_element_type=jnp.float32)
            dk_acc[pl.ds(to, size), :] += jnp.dot(
                scores, q_doc[pl.ds(at, QSTEP), :], preferred_element_type=jnp.float32)
            dq_acc[...] += jnp.dot(
                kt_doc[:, pl.ds(to, size)], scores, preferred_element_type=jnp.float32)

        def over_keys(body, carry):
            to = 0
            for wide in (4, 2, 1):
                size = wide * STEP
                steps = tiles // 4 if wide == 4 else (tiles // wide) % 2
                start = to

                def step(c, now, start=start, size=size):
                    return body(pl.multiple_of(start + c * size, STEP), size, now)

                carry = lax.fori_loop(0, steps, step, carry)
                to = start + steps * size
            return carry

        flat = jnp.zeros((8, QSTEP), jnp.float32)
        fresh = (flat + LOW, flat, flat)

        def joined(top, total, dot):
            peak = jnp.max(top, axis=0, keepdims=True)
            weight = jnp.exp2(top - peak)
            total = jnp.sum(total * weight, axis=0, keepdims=True)
            dot = jnp.sum(dot * weight, axis=0, keepdims=True)
            return flat + (peak + jnp.log2(total)), flat + dot / total

        def put_queries(tile):
            at = pl.multiple_of(tile * QSTEP, QSTEP)
            grads[0, pl.ds(first + at, QSTEP), :] = dq_acc[...].T * SCALE
            dq_acc[...] = jnp.zeros((HD, QSTEP), jnp.float32)

        dq_acc[...] = jnp.zeros((HD, QSTEP), jnp.float32)
        norm_now = joined(*over_keys(lambda to, size, now: stats(products(0, to, size), to, size, now), fresh))

        def query_tile(tile, norms):
            norm, delta = norms

            def both(to, size, now):
                scores = products(tile, to, size)
                gradients(tile - 1, to, size, norm, delta)
                return stats(scores, to, size, now)

            now = over_keys(both, fresh)
            put_queries(tile - 1)
            return joined(*now)

        norm, delta = lax.fori_loop(1, q_tiles, query_tile, norm_now)

        def rest(to, size, now):
            gradients(q_tiles - 1, to, size, norm, delta)
            return now

        over_keys(rest, 0)
        put_queries(q_tiles - 1)

        def put(tile, carry):
            at = pl.multiple_of(tile * STEP, STEP)
            grads[1, pl.ds(first + at, STEP), :] = dk_acc[pl.ds(at, STEP), :] * SCALE
            grads[2, pl.ds(first + at, STEP), :] = dv_acc[pl.ds(at, STEP), :]
            return carry

        lax.fori_loop(0, tiles, put, 0)
        return carry

    lax.fori_loop(doc_lo, doc_hi, one_document, 0)

    for _, ref, base in pieces:
        lo = jnp.clip(shard_lo - base, 0, ref.shape[0])
        hi = jnp.clip(shard_hi - base, 0, ref.shape[0])

        def empty(shard, carry, ref=ref):
            for slot in range(3):
                ref[shard, slot] = zero_shard.astype(jnp.bfloat16)
            return carry

        def store(shard, carry, ref=ref, base=base):
            at = pl.multiple_of((base + shard) * SHARD, SHARD)
            for slot in range(3):
                ref[shard, slot] = grads[slot, pl.ds(at, SHARD), :].astype(jnp.bfloat16)
            return carry

        lax.fori_loop(0, lo, empty, 0)
        lax.fori_loop(lo, hi, store, 0)
        lax.fori_loop(hi, ref.shape[0], empty, 0)


def attention(bounds, span, left, own, right):
    shape = jax.ShapeDtypeStruct((SHARDS, 3, SHARD, HD), jnp.bfloat16)
    smem = pl.BlockSpec(memory_space=pltpu.SMEM)
    vmem = pl.BlockSpec(memory_space=pltpu.VMEM)
    padded = 3 * BLOCK + QSTEP
    return pl.pallas_call(
        attention_kernel,
        out_shape=(shape, shape, shape),
        in_specs=[smem, smem, vmem, vmem, vmem],
        out_specs=(vmem, vmem, vmem),
        scratch_shapes=[
            pltpu.VMEM((4, padded, HD), jnp.float32),
            pltpu.VMEM((3, padded, HD), jnp.float32),
            pltpu.VMEM((MOST, HD), jnp.bfloat16),
            pltpu.VMEM((MOST, HD), jnp.bfloat16),
            pltpu.VMEM((MOST, HD), jnp.bfloat16),
            pltpu.VMEM((MOST, HD), jnp.bfloat16),
            pltpu.VMEM((HD, MOST), jnp.bfloat16),
            pltpu.VMEM((MOST, HD), jnp.float32),
            pltpu.VMEM((MOST, HD), jnp.float32),
            pltpu.VMEM((HD, QSTEP), jnp.float32),
            pltpu.VMEM((MOST, QSTEP), jnp.float32),
            pltpu.VMEM((MOST, QSTEP), jnp.float32),
            pltpu.VMEM((MOST // PART, 8, QSTEP), jnp.float32),
        ],
        compiler_params=pltpu.CompilerParams(vmem_limit_bytes=38 * 1024 * 1024),
        cost_estimate=pl.CostEstimate(
            flops=5 * 2 * MOST * MOST * HD, bytes_accessed=6 * 1024 * 1024, transcendentals=2 * MOST * MOST
        ),
        name="attention",
    )(bounds, span, left, own, right)


def from_left(shard):
    devices = lax.axis_size("ctx")
    return lax.ppermute(shard, "ctx", [(i, i + 1) for i in range(devices - 1)])


def from_right(shard):
    devices = lax.axis_size("ctx")
    return lax.ppermute(shard, "ctx", [(i + 1, i) for i in range(devices - 1)])


def swap_heads(shard):
    return lax.all_to_all(shard, "head", split_axis=0, concat_axis=0, tiled=True)


def on_device(queries, key_rows, value_rows, out_grad, bounds):
    owner = document_owner(bounds[:-1], bounds[1:])
    me = lax.axis_index("ctx")
    span = jnp.stack([jnp.sum(owner < me), jnp.sum(owner <= me)]).astype(jnp.int32)
    done = []
    for packed in pack(queries, key_rows, value_rows, out_grad):
        own = swap_heads(packed)
        left = from_left(own)
        right = from_right(own)
        left_grad, own_grad, right_grad = attention(bounds, span, left, own, right)
        own_grad = own_grad + from_left(right_grad) + from_right(left_grad)
        done.append(swap_heads(own_grad))
    return unpack(*done)


def solution(mesh):
    rows = P(("ctx", "head"), None)
    return jax.shard_map(
        on_device,
        mesh=mesh,
        in_specs=(rows, rows, rows, rows, P()),
        out_specs=(rows, rows, rows),
        check_vma=False,
    )
```

```python
import jax
import jax.numpy as jnp
from jax import lax
from jax.experimental import pallas as pl
from jax.experimental.pallas import tpu as pltpu
from jax.sharding import PartitionSpec as P

HD = 128
NDOC = 64
BLOCK_BITS = 10
BLOCK = 1 << BLOCK_BITS
SHARD_BITS = 7
SHARD = 1 << SHARD_BITS
SHARDS = BLOCK // SHARD
STEP = 256
QSTEP = 512
PART = 128
MOST = 2048
SCALE = HD ** -0.5
LOG2E = 1.4426950408889634
LOW = -1.0e30
VMEM_LIMIT = 48 * 1024 * 1024
VMEM_ALL = 64 * 1024 * 1024 - 256 * 1024


def pack_kernel(q_ref, k_ref, v_ref, g_ref, even_ref, odd_ref, held, sems):
    copies = []
    for slot, ref in enumerate((q_ref, k_ref, v_ref, g_ref)):
        copies.append(pltpu.make_async_copy(ref, held.at[slot], sems.at[slot]))
    for copy in copies:
        copy.start()
    for slot, copy in enumerate(copies):
        copy.wait()
        for peer in range(SHARDS):
            even_ref[peer, slot] = held[slot, :, pl.ds(2 * peer * HD, HD)]
            odd_ref[peer, slot] = held[slot, :, pl.ds((2 * peer + 1) * HD, HD)]


def pack(queries, key_rows, value_rows, out_grad):
    shape = jax.ShapeDtypeStruct((SHARDS, 4, SHARD, HD), jnp.bfloat16)
    return pl.pallas_call(
        pack_kernel,
        out_shape=(shape, shape),
        in_specs=[pl.BlockSpec(memory_space=pltpu.HBM)] * 4,
        scratch_shapes=[
            pltpu.VMEM((4, SHARD, 2 * SHARDS * HD), jnp.bfloat16),
            pltpu.SemaphoreType.DMA((4,)),
        ],
        compiler_params=pltpu.CompilerParams(vmem_limit_bytes=VMEM_ALL),
        name="pack",
    )(queries, key_rows, value_rows, out_grad)


def unpack_kernel(even_ref, odd_ref, dq_ref, dk_ref, dv_ref):
    for slot, ref in enumerate((dq_ref, dk_ref, dv_ref)):
        for peer in range(SHARDS):
            ref[:, pl.ds(2 * peer * HD, HD)] = even_ref[peer, slot]
            ref[:, pl.ds((2 * peer + 1) * HD, HD)] = odd_ref[peer, slot]


def unpack(even, odd):
    shape = jax.ShapeDtypeStruct((SHARD, 2 * SHARDS * HD), jnp.bfloat16)
    return pl.pallas_call(
        unpack_kernel,
        out_shape=(shape, shape, shape),
        compiler_params=pltpu.CompilerParams(vmem_limit_bytes=VMEM_LIMIT),
        name="unpack",
    )(even, odd)


def document_owner(first, end):
    first_block = first >> BLOCK_BITS
    last_block = (end - 1) >> BLOCK_BITS
    edge = last_block << BLOCK_BITS
    right_larger = (end - edge) > (edge - first)
    span = last_block - first_block
    return first_block + jnp.where((span == 2) | ((span == 1) & right_larger), 1, 0)


def attention_kernel(
    bounds_ref, span_ref, left_ref, own_ref, right_ref,
    left_out, own_out, right_out,
    rows, grads, q_doc, k_doc, v_doc, g_doc, kt_doc, dk_acc, dv_acc, dq_acc, e_buf, p_buf, tops,
):
    window = (lax.axis_index("ctx") - 1) * BLOCK
    pieces = ((left_ref, left_out, 0), (own_ref, own_out, SHARDS), (right_ref, right_out, 2 * SHARDS))

    doc_lo, doc_hi = span_ref[0], span_ref[1]
    some = doc_hi > doc_lo
    shard_lo = jnp.where(some, (bounds_ref[doc_lo] - window) >> SHARD_BITS, 0)
    shard_hi = jnp.where(some, (bounds_ref[doc_hi] - window + SHARD - 1) >> SHARD_BITS, 0)
    zero_tile = jnp.zeros((STEP, HD), jnp.float32)
    zero_shard = jnp.zeros((SHARD, HD), jnp.float32)

    for ref, _, base in pieces:
        lo = jnp.clip(shard_lo - base, 0, ref.shape[0])
        hi = jnp.clip(shard_hi - base, 0, ref.shape[0])

        def load(shard, carry, ref=ref, base=base):
            at = pl.multiple_of((base + shard) * SHARD, SHARD)
            for slot in range(4):
                rows[slot, pl.ds(at, SHARD), :] = ref[shard, slot].astype(jnp.float32)
            return carry

        lax.fori_loop(lo, hi, load, 0)

    for edge in (shard_lo, jnp.maximum(shard_hi - 1, 0)):
        at = pl.multiple_of(edge * SHARD, SHARD)
        for slot in range(3):
            grads[slot, pl.ds(at, SHARD), :] = zero_shard

    def one_document(doc, carry):
        first = bounds_ref[doc] - window
        length = bounds_ref[doc + 1] - bounds_ref[doc]
        tiles = (length + STEP - 1) // STEP
        q_tiles = (length + QSTEP - 1) // QSTEP

        def fetch(tile, carry):
            at = pl.multiple_of(tile * STEP, STEP)
            inside = lax.broadcasted_iota(jnp.int32, (STEP, HD), 0) + at < length
            for slot, ref in enumerate((q_doc, k_doc, v_doc, g_doc)):
                part = jnp.where(inside, rows[slot, pl.ds(first + at, STEP), :], 0.0)
                ref[pl.ds(at, STEP), :] = part.astype(jnp.bfloat16)
                if slot == 1:
                    kt_doc[:, pl.ds(at, STEP)] = part.astype(jnp.bfloat16).T
            dk_acc[pl.ds(at, STEP), :] = zero_tile
            dv_acc[pl.ds(at, STEP), :] = zero_tile
            return carry

        lax.fori_loop(0, q_tiles * (QSTEP // STEP), fetch, 0)

        def products(tile, to, size):
            at = pl.multiple_of(tile * QSTEP, QSTEP)
            s = lax.dot_general(
                k_doc[pl.ds(to, size), :], q_doc[pl.ds(at, QSTEP), :],
                (((1,), (1,)), ((), ())), preferred_element_type=jnp.float32)
            p = lax.dot_general(
                v_doc[pl.ds(to, size), :], g_doc[pl.ds(at, QSTEP), :],
                (((1,), (1,)), ((), ())), preferred_element_type=jnp.float32)
            return s, p

        def stats(scores, to, size, carry):
            s_all, p_all = scores
            for part in range(size // PART):
                top, total, dot = carry
                here = to + part * PART
                s = s_all[part * PART:(part + 1) * PART] * (SCALE * LOG2E)
                p = p_all[part * PART:(part + 1) * PART]
                if part >= (size - STEP) // PART:
                    inside = lax.broadcasted_iota(jnp.int32, (PART, QSTEP), 0) + here < length
                    s = jnp.where(inside, s, LOW)
                s = s.reshape(PART // 8, 8, QSTEP)
                new_top = jnp.maximum(top, jnp.max(s, axis=0))
                e = jnp.exp2(s - new_top[None])
                e_buf[pl.ds(here, PART), :] = e.reshape(PART, QSTEP)
                p_buf[pl.ds(here, PART), :] = p
                tops[to // PART + part] = new_top
                shrink = jnp.exp2(top - new_top)
                total = total * shrink + jnp.sum(e, axis=0)
                dot = dot * shrink + jnp.sum(e * p.reshape(PART // 8, 8, QSTEP), axis=0)
                carry = new_top, total, dot
            return carry

        def gradients(tile, to, size, norm, delta):
            at = pl.multiple_of(tile * QSTEP, QSTEP)
            weights, scores = [], []
            for part in range(size // PART):
                here = to + part * PART
                factor = jnp.exp2(tops[to // PART + part] - norm)
                e = e_buf[pl.ds(here, PART), :].reshape(PART // 8, 8, QSTEP) * factor[None]
                p = p_buf[pl.ds(here, PART), :].reshape(PART // 8, 8, QSTEP)
                scores.append((e * (p - delta[None])).reshape(PART, QSTEP).astype(jnp.bfloat16))
                weights.append(e.reshape(PART, QSTEP).astype(jnp.bfloat16))
            weights = jnp.concatenate(weights, axis=0)
            scores = jnp.concatenate(scores, axis=0)
            dv_acc[pl.ds(to, size), :] += jnp.dot(
                weights, g_doc[pl.ds(at, QSTEP), :], preferred_element_type=jnp.float32)
            dk_acc[pl.ds(to, size), :] += jnp.dot(
                scores, q_doc[pl.ds(at, QSTEP), :], preferred_element_type=jnp.float32)
            dq_acc[...] += jnp.dot(
                kt_doc[:, pl.ds(to, size)], scores, preferred_element_type=jnp.float32)

        def over_keys(body, carry):
            to = 0
            for wide in (2, 1):
                size = wide * STEP
                steps = tiles >> 1 if wide == 2 else tiles & 1
                start = to

                def step(c, now, start=start, size=size):
                    return body(pl.multiple_of(start + c * size, STEP), size, now)

                carry = lax.fori_loop(0, steps, step, carry)
                to = start + steps * size
            return carry

        flat = jnp.zeros((8, QSTEP), jnp.float32)
        fresh = (flat + LOW, flat, flat)

        def joined(top, total, dot):
            peak = jnp.max(top, axis=0, keepdims=True)
            weight = jnp.exp2(top - peak)
            total = jnp.sum(total * weight, axis=0, keepdims=True)
            dot = jnp.sum(dot * weight, axis=0, keepdims=True)
            return flat + (peak + jnp.log2(total)), flat + dot / total

        def put_queries(tile):
            at = pl.multiple_of(tile * QSTEP, QSTEP)
            grads[0, pl.ds(first + at, QSTEP), :] = dq_acc[...].T * SCALE
            dq_acc[...] = jnp.zeros((HD, QSTEP), jnp.float32)

        dq_acc[...] = jnp.zeros((HD, QSTEP), jnp.float32)
        norm_now = joined(*over_keys(lambda to, size, now: stats(products(0, to, size), to, size, now), fresh))

        def query_tile(tile, norms):
            norm, delta = norms

            def both(to, size, now):
                scores = products(tile, to, size)
                gradients(tile - 1, to, size, norm, delta)
                return stats(scores, to, size, now)

            now = over_keys(both, fresh)
            put_queries(tile - 1)
            return joined(*now)

        norm, delta = lax.fori_loop(1, q_tiles, query_tile, norm_now)

        def rest(to, size, now):
            gradients(q_tiles - 1, to, size, norm, delta)
            return now

        over_keys(rest, 0)
        put_queries(q_tiles - 1)

        def put(tile, carry):
            at = pl.multiple_of(tile * STEP, STEP)
            grads[1, pl.ds(first + at, STEP), :] = dk_acc[pl.ds(at, STEP), :] * SCALE
            grads[2, pl.ds(first + at, STEP), :] = dv_acc[pl.ds(at, STEP), :]
            return carry

        lax.fori_loop(0, tiles, put, 0)
        return carry

    lax.fori_loop(doc_lo, doc_hi, one_document, 0)

    for _, ref, base in pieces:
        lo = jnp.clip(shard_lo - base, 0, ref.shape[0])
        hi = jnp.clip(shard_hi - base, 0, ref.shape[0])

        def empty(shard, carry, ref=ref):
            for slot in range(3):
                ref[shard, slot] = zero_shard.astype(jnp.bfloat16)
            return carry

        def store(shard, carry, ref=ref, base=base):
            at = pl.multiple_of((base + shard) * SHARD, SHARD)
            for slot in range(3):
                ref[shard, slot] = grads[slot, pl.ds(at, SHARD), :].astype(jnp.bfloat16)
            return carry

        lax.fori_loop(0, lo, empty, 0)
        lax.fori_loop(lo, hi, store, 0)
        lax.fori_loop(hi, ref.shape[0], empty, 0)


def attention(bounds, span, left, own, right):
    shape = jax.ShapeDtypeStruct((SHARDS, 3, SHARD, HD), jnp.bfloat16)
    smem = pl.BlockSpec(memory_space=pltpu.SMEM)
    vmem = pl.BlockSpec(memory_space=pltpu.VMEM)
    padded = 3 * BLOCK + QSTEP
    return pl.pallas_call(
        attention_kernel,
        out_shape=(shape, shape, shape),
        in_specs=[smem, smem, vmem, vmem, vmem],
        out_specs=(vmem, vmem, vmem),
        scratch_shapes=[
            pltpu.VMEM((4, padded, HD), jnp.float32),
            pltpu.VMEM((3, padded, HD), jnp.float32),
            pltpu.VMEM((MOST, HD), jnp.bfloat16),
            pltpu.VMEM((MOST, HD), jnp.bfloat16),
            pltpu.VMEM((MOST, HD), jnp.bfloat16),
            pltpu.VMEM((MOST, HD), jnp.bfloat16),
            pltpu.VMEM((HD, MOST), jnp.bfloat16),
            pltpu.VMEM((MOST, HD), jnp.float32),
            pltpu.VMEM((MOST, HD), jnp.float32),
            pltpu.VMEM((HD, QSTEP), jnp.float32),
            pltpu.VMEM((MOST, QSTEP), jnp.float32),
            pltpu.VMEM((MOST, QSTEP), jnp.float32),
            pltpu.VMEM((MOST // PART, 8, QSTEP), jnp.float32),
        ],
        compiler_params=pltpu.CompilerParams(vmem_limit_bytes=38 * 1024 * 1024),
        cost_estimate=pl.CostEstimate(
            flops=5 * 2 * MOST * MOST * HD, bytes_accessed=6 * 1024 * 1024, transcendentals=2 * MOST * MOST
        ),
        name="attention",
    )(bounds, span, left, own, right)


def from_left(shard):
    devices = lax.axis_size("ctx")
    return lax.ppermute(shard, "ctx", [(i, i + 1) for i in range(devices - 1)])


def from_right(shard):
    devices = lax.axis_size("ctx")
    return lax.ppermute(shard, "ctx", [(i + 1, i) for i in range(devices - 1)])


def swap_heads(shard):
    return lax.all_to_all(shard, "head", split_axis=0, concat_axis=0, tiled=True)


def on_device(queries, key_rows, value_rows, out_grad, bounds):
    owner = document_owner(bounds[:-1], bounds[1:])
    me = lax.axis_index("ctx")
    span = jnp.stack([jnp.sum(owner < me), jnp.sum(owner <= me)]).astype(jnp.int32)
    done = []
    for packed in pack(queries, key_rows, value_rows, out_grad):
        own = swap_heads(packed)
        left = from_left(own)
        right = from_right(own)
        left_grad, own_grad, right_grad = attention(bounds, span, left, own, right)
        own_grad = own_grad + from_left(right_grad) + from_right(left_grad)
        done.append(swap_heads(own_grad))
    return unpack(*done)


def solution(mesh):
    rows = P(("ctx", "head"), None)
    return jax.shard_map(
        on_device,
        mesh=mesh,
        in_specs=(rows, rows, rows, rows, P()),
        out_specs=(rows, rows, rows),
        check_vma=False,
    )
```

```python
import jax
import jax.numpy as jnp
from jax import lax
from jax.experimental import pallas as pl
from jax.experimental.pallas import tpu as pltpu
from jax.sharding import PartitionSpec as P

HD = 128
NDOC = 64
BLOCK_BITS = 10
BLOCK = 1 << BLOCK_BITS
SHARD_BITS = 7
SHARD = 1 << SHARD_BITS
SHARDS = BLOCK // SHARD
STEP = 256
QSTEP = 512
PART = 64
MOST = 2048
SCALE = HD ** -0.5
LOG2E = 1.4426950408889634
LOW = -1.0e30
VMEM_LIMIT = 48 * 1024 * 1024
VMEM_ALL = 64 * 1024 * 1024 - 256 * 1024


def pack_kernel(q_ref, k_ref, v_ref, g_ref, even_ref, odd_ref, held, sems):
    copies = []
    for slot, ref in enumerate((q_ref, k_ref, v_ref, g_ref)):
        copies.append(pltpu.make_async_copy(ref, held.at[slot], sems.at[slot]))
    for copy in copies:
        copy.start()
    for slot, copy in enumerate(copies):
        copy.wait()
        for peer in range(SHARDS):
            even_ref[peer, slot] = held[slot, :, pl.ds(2 * peer * HD, HD)]
            odd_ref[peer, slot] = held[slot, :, pl.ds((2 * peer + 1) * HD, HD)]


def pack(queries, key_rows, value_rows, out_grad):
    shape = jax.ShapeDtypeStruct((SHARDS, 4, SHARD, HD), jnp.bfloat16)
    return pl.pallas_call(
        pack_kernel,
        out_shape=(shape, shape),
        in_specs=[pl.BlockSpec(memory_space=pltpu.HBM)] * 4,
        scratch_shapes=[
            pltpu.VMEM((4, SHARD, 2 * SHARDS * HD), jnp.bfloat16),
            pltpu.SemaphoreType.DMA((4,)),
        ],
        compiler_params=pltpu.CompilerParams(vmem_limit_bytes=VMEM_ALL),
        name="pack",
    )(queries, key_rows, value_rows, out_grad)


def unpack_kernel(even_ref, odd_ref, dq_ref, dk_ref, dv_ref):
    for slot, ref in enumerate((dq_ref, dk_ref, dv_ref)):
        for peer in range(SHARDS):
            ref[:, pl.ds(2 * peer * HD, HD)] = even_ref[peer, slot]
            ref[:, pl.ds((2 * peer + 1) * HD, HD)] = odd_ref[peer, slot]


def unpack(even, odd):
    shape = jax.ShapeDtypeStruct((SHARD, 2 * SHARDS * HD), jnp.bfloat16)
    return pl.pallas_call(
        unpack_kernel,
        out_shape=(shape, shape, shape),
        compiler_params=pltpu.CompilerParams(vmem_limit_bytes=VMEM_LIMIT),
        name="unpack",
    )(even, odd)


def document_owner(first, end):
    first_block = first >> BLOCK_BITS
    last_block = (end - 1) >> BLOCK_BITS
    edge = last_block << BLOCK_BITS
    right_larger = (end - edge) > (edge - first)
    span = last_block - first_block
    return first_block + jnp.where((span == 2) | ((span == 1) & right_larger), 1, 0)


def attention_kernel(
    bounds_ref, span_ref, left_ref, own_ref, right_ref,
    left_out, own_out, right_out,
    rows, grads, q_doc, k_doc, v_doc, g_doc, kt_doc, dk_acc, dv_acc, dq_acc, e_buf, p_buf, tops,
):
    window = (lax.axis_index("ctx") - 1) * BLOCK
    pieces = ((left_ref, left_out, 0), (own_ref, own_out, SHARDS), (right_ref, right_out, 2 * SHARDS))

    doc_lo, doc_hi = span_ref[0], span_ref[1]
    some = doc_hi > doc_lo
    shard_lo = jnp.where(some, (bounds_ref[doc_lo] - window) >> SHARD_BITS, 0)
    shard_hi = jnp.where(some, (bounds_ref[doc_hi] - window + SHARD - 1) >> SHARD_BITS, 0)
    zero_tile = jnp.zeros((STEP, HD), jnp.float32)
    zero_shard = jnp.zeros((SHARD, HD), jnp.float32)

    for ref, _, base in pieces:
        lo = jnp.clip(shard_lo - base, 0, ref.shape[0])
        hi = jnp.clip(shard_hi - base, 0, ref.shape[0])

        def load(shard, carry, ref=ref, base=base):
            at = pl.multiple_of((base + shard) * SHARD, SHARD)
            for slot in range(4):
                rows[slot, pl.ds(at, SHARD), :] = ref[shard, slot].astype(jnp.float32)
            return carry

        lax.fori_loop(lo, hi, load, 0)

    for edge in (shard_lo, jnp.maximum(shard_hi - 1, 0)):
        at = pl.multiple_of(edge * SHARD, SHARD)
        for slot in range(3):
            grads[slot, pl.ds(at, SHARD), :] = zero_shard

    def one_document(doc, carry):
        first = bounds_ref[doc] - window
        length = bounds_ref[doc + 1] - bounds_ref[doc]
        tiles = (length + STEP - 1) // STEP
        q_tiles = (length + QSTEP - 1) // QSTEP

        def fetch(tile, carry):
            at = pl.multiple_of(tile * STEP, STEP)
            inside = lax.broadcasted_iota(jnp.int32, (STEP, HD), 0) + at < length
            for slot, ref in enumerate((q_doc, k_doc, v_doc, g_doc)):
                part = jnp.where(inside, rows[slot, pl.ds(first + at, STEP), :], 0.0)
                ref[pl.ds(at, STEP), :] = part.astype(jnp.bfloat16)
                if slot == 1:
                    kt_doc[:, pl.ds(at, STEP)] = part.astype(jnp.bfloat16).T
            dk_acc[pl.ds(at, STEP), :] = zero_tile
            dv_acc[pl.ds(at, STEP), :] = zero_tile
            return carry

        lax.fori_loop(0, q_tiles * (QSTEP // STEP), fetch, 0)

        def products(tile, to, size):
            at = pl.multiple_of(tile * QSTEP, QSTEP)
            s = lax.dot_general(
                k_doc[pl.ds(to, size), :], q_doc[pl.ds(at, QSTEP), :],
                (((1,), (1,)), ((), ())), preferred_element_type=jnp.float32)
            p = lax.dot_general(
                v_doc[pl.ds(to, size), :], g_doc[pl.ds(at, QSTEP), :],
                (((1,), (1,)), ((), ())), preferred_element_type=jnp.float32)
            return s, p

        def stats(scores, to, size, carry):
            s_all, p_all = scores
            for part in range(size // PART):
                top, total, dot = carry
                here = to + part * PART
                s = s_all[part * PART:(part + 1) * PART] * (SCALE * LOG2E)
                p = p_all[part * PART:(part + 1) * PART]
                if part >= (size - STEP) // PART:
                    inside = lax.broadcasted_iota(jnp.int32, (PART, QSTEP), 0) + here < length
                    s = jnp.where(inside, s, LOW)
                s = s.reshape(PART // 8, 8, QSTEP)
                new_top = jnp.maximum(top, jnp.max(s, axis=0))
                e = jnp.exp2(s - new_top[None])
                e_buf[pl.ds(here, PART), :] = e.reshape(PART, QSTEP)
                p_buf[pl.ds(here, PART), :] = p
                tops[to // PART + part] = new_top
                shrink = jnp.exp2(top - new_top)
                total = total * shrink + jnp.sum(e, axis=0)
                dot = dot * shrink + jnp.sum(e * p.reshape(PART // 8, 8, QSTEP), axis=0)
                carry = new_top, total, dot
            return carry

        def gradients(tile, to, size, norm, delta):
            at = pl.multiple_of(tile * QSTEP, QSTEP)
            weights, scores = [], []
            for part in range(size // PART):
                here = to + part * PART
                factor = jnp.exp2(tops[to // PART + part] - norm)
                e = e_buf[pl.ds(here, PART), :].reshape(PART // 8, 8, QSTEP) * factor[None]
                p = p_buf[pl.ds(here, PART), :].reshape(PART // 8, 8, QSTEP)
                scores.append((e * (p - delta[None])).reshape(PART, QSTEP).astype(jnp.bfloat16))
                weights.append(e.reshape(PART, QSTEP).astype(jnp.bfloat16))
            weights = jnp.concatenate(weights, axis=0)
            scores = jnp.concatenate(scores, axis=0)
            dv_acc[pl.ds(to, size), :] += jnp.dot(
                weights, g_doc[pl.ds(at, QSTEP), :], preferred_element_type=jnp.float32)
            dk_acc[pl.ds(to, size), :] += jnp.dot(
                scores, q_doc[pl.ds(at, QSTEP), :], preferred_element_type=jnp.float32)
            dq_acc[...] += jnp.dot(
                kt_doc[:, pl.ds(to, size)], scores, preferred_element_type=jnp.float32)

        def over_keys(wide, body, carry):
            to = 0
            for size, steps in ((wide * STEP, tiles >> (wide // 2)), (STEP, tiles & (wide - 1))):
                start = to

                def step(c, now, start=start, size=size):
                    return body(pl.multiple_of(start + c * size, STEP), size, now)

                carry = lax.fori_loop(0, steps, step, carry)
                to = start + steps * size
            return carry

        flat = jnp.zeros((8, QSTEP), jnp.float32)
        fresh = (flat + LOW, flat, flat)

        def joined(top, total, dot):
            peak = jnp.max(top, axis=0, keepdims=True)
            weight = jnp.exp2(top - peak)
            total = jnp.sum(total * weight, axis=0, keepdims=True)
            dot = jnp.sum(dot * weight, axis=0, keepdims=True)
            return flat + (peak + jnp.log2(total)), flat + dot / total

        def put_queries(tile):
            at = pl.multiple_of(tile * QSTEP, QSTEP)
            grads[0, pl.ds(first + at, QSTEP), :] = dq_acc[...].T * SCALE
            dq_acc[...] = jnp.zeros((HD, QSTEP), jnp.float32)

        dq_acc[...] = jnp.zeros((HD, QSTEP), jnp.float32)
        norm_now = joined(*over_keys(2, lambda to, size, now: stats(products(0, to, size), to, size, now), fresh))

        def query_tile(tile, norms):
            norm, delta = norms

            def both(to, size, now):
                scores = products(tile, to, size)
                gradients(tile - 1, to, size, norm, delta)
                return stats(scores, to, size, now)

            now = over_keys(4, both, fresh)
            put_queries(tile - 1)
            return joined(*now)

        norm, delta = lax.fori_loop(1, q_tiles, query_tile, norm_now)

        def rest(to, size, now):
            gradients(q_tiles - 1, to, size, norm, delta)
            return now

        over_keys(2, rest, 0)
        put_queries(q_tiles - 1)

        def put(tile, carry):
            at = pl.multiple_of(tile * STEP, STEP)
            grads[1, pl.ds(first + at, STEP), :] = dk_acc[pl.ds(at, STEP), :] * SCALE
            grads[2, pl.ds(first + at, STEP), :] = dv_acc[pl.ds(at, STEP), :]
            return carry

        lax.fori_loop(0, tiles, put, 0)
        return carry

    lax.fori_loop(doc_lo, doc_hi, one_document, 0)

    for _, ref, base in pieces:
        lo = jnp.clip(shard_lo - base, 0, ref.shape[0])
        hi = jnp.clip(shard_hi - base, 0, ref.shape[0])

        def empty(shard, carry, ref=ref):
            for slot in range(3):
                ref[shard, slot] = zero_shard.astype(jnp.bfloat16)
            return carry

        def store(shard, carry, ref=ref, base=base):
            at = pl.multiple_of((base + shard) * SHARD, SHARD)
            for slot in range(3):
                ref[shard, slot] = grads[slot, pl.ds(at, SHARD), :].astype(jnp.bfloat16)
            return carry

        lax.fori_loop(0, lo, empty, 0)
        lax.fori_loop(lo, hi, store, 0)
        lax.fori_loop(hi, ref.shape[0], empty, 0)


def attention(bounds, span, left, own, right):
    shape = jax.ShapeDtypeStruct((SHARDS, 3, SHARD, HD), jnp.bfloat16)
    smem = pl.BlockSpec(memory_space=pltpu.SMEM)
    vmem = pl.BlockSpec(memory_space=pltpu.VMEM)
    padded = 3 * BLOCK + QSTEP
    return pl.pallas_call(
        attention_kernel,
        out_shape=(shape, shape, shape),
        in_specs=[smem, smem, vmem, vmem, vmem],
        out_specs=(vmem, vmem, vmem),
        scratch_shapes=[
            pltpu.VMEM((4, padded, HD), jnp.float32),
            pltpu.VMEM((3, padded, HD), jnp.float32),
            pltpu.VMEM((MOST, HD), jnp.bfloat16),
            pltpu.VMEM((MOST, HD), jnp.bfloat16),
            pltpu.VMEM((MOST, HD), jnp.bfloat16),
            pltpu.VMEM((MOST, HD), jnp.bfloat16),
            pltpu.VMEM((HD, MOST), jnp.bfloat16),
            pltpu.VMEM((MOST, HD), jnp.float32),
            pltpu.VMEM((MOST, HD), jnp.float32),
            pltpu.VMEM((HD, QSTEP), jnp.float32),
            pltpu.VMEM((MOST, QSTEP), jnp.float32),
            pltpu.VMEM((MOST, QSTEP), jnp.float32),
            pltpu.VMEM((MOST // PART, 8, QSTEP), jnp.float32),
        ],
        compiler_params=pltpu.CompilerParams(vmem_limit_bytes=38 * 1024 * 1024),
        cost_estimate=pl.CostEstimate(
            flops=5 * 2 * MOST * MOST * HD, bytes_accessed=6 * 1024 * 1024, transcendentals=2 * MOST * MOST
        ),
        name="attention",
    )(bounds, span, left, own, right)


def from_left(shard):
    devices = lax.axis_size("ctx")
    return lax.ppermute(shard, "ctx", [(i, i + 1) for i in range(devices - 1)])


def from_right(shard):
    devices = lax.axis_size("ctx")
    return lax.ppermute(shard, "ctx", [(i + 1, i) for i in range(devices - 1)])


def swap_heads(shard):
    return lax.all_to_all(shard, "head", split_axis=0, concat_axis=0, tiled=True)


def on_device(queries, key_rows, value_rows, out_grad, bounds):
    owner = document_owner(bounds[:-1], bounds[1:])
    me = lax.axis_index("ctx")
    span = jnp.stack([jnp.sum(owner < me), jnp.sum(owner <= me)]).astype(jnp.int32)
    done = []
    for packed in pack(queries, key_rows, value_rows, out_grad):
        own = swap_heads(packed)
        left = from_left(own)
        right = from_right(own)
        left_grad, own_grad, right_grad = attention(bounds, span, left, own, right)
        own_grad = own_grad + from_left(right_grad) + from_right(left_grad)
        done.append(swap_heads(own_grad))
    return unpack(*done)


def solution(mesh):
    rows = P(("ctx", "head"), None)
    return jax.shard_map(
        on_device,
        mesh=mesh,
        in_specs=(rows, rows, rows, rows, P()),
        out_specs=(rows, rows, rows),
        check_vma=False,
    )
```

```python
import jax
import jax.numpy as jnp
from jax import lax
from jax.experimental import pallas as pl
from jax.experimental.pallas import tpu as pltpu
from jax.sharding import PartitionSpec as P

HD = 128
NDOC = 64
BLOCK_BITS = 10
BLOCK = 1 << BLOCK_BITS
SHARD_BITS = 7
SHARD = 1 << SHARD_BITS
SHARDS = BLOCK // SHARD
STEP = 256
QSTEP = 512
PART = 64
MOST = 2048
SCALE = HD ** -0.5
LOG2E = 1.4426950408889634
LOW = -1.0e30
VMEM_LIMIT = 48 * 1024 * 1024
VMEM_ALL = 64 * 1024 * 1024 - 256 * 1024


def pack_kernel(q_ref, k_ref, v_ref, g_ref, even_ref, odd_ref, held, sems):
    copies = []
    for slot, ref in enumerate((q_ref, k_ref, v_ref, g_ref)):
        copies.append(pltpu.make_async_copy(ref, held.at[slot], sems.at[slot]))
    for copy in copies:
        copy.start()
    for slot, copy in enumerate(copies):
        copy.wait()
        for peer in range(SHARDS):
            even_ref[peer, slot] = held[slot, :, pl.ds(2 * peer * HD, HD)]
            odd_ref[peer, slot] = held[slot, :, pl.ds((2 * peer + 1) * HD, HD)]


def pack(queries, key_rows, value_rows, out_grad):
    shape = jax.ShapeDtypeStruct((SHARDS, 4, SHARD, HD), jnp.bfloat16)
    return pl.pallas_call(
        pack_kernel,
        out_shape=(shape, shape),
        in_specs=[pl.BlockSpec(memory_space=pltpu.HBM)] * 4,
        scratch_shapes=[
            pltpu.VMEM((4, SHARD, 2 * SHARDS * HD), jnp.bfloat16),
            pltpu.SemaphoreType.DMA((4,)),
        ],
        compiler_params=pltpu.CompilerParams(vmem_limit_bytes=VMEM_ALL),
        name="pack",
    )(queries, key_rows, value_rows, out_grad)


def unpack_kernel(even_ref, odd_ref, dq_ref, dk_ref, dv_ref):
    for slot, ref in enumerate((dq_ref, dk_ref, dv_ref)):
        for peer in range(SHARDS):
            ref[:, pl.ds(2 * peer * HD, HD)] = even_ref[peer, slot]
            ref[:, pl.ds((2 * peer + 1) * HD, HD)] = odd_ref[peer, slot]


def unpack(even, odd):
    shape = jax.ShapeDtypeStruct((SHARD, 2 * SHARDS * HD), jnp.bfloat16)
    return pl.pallas_call(
        unpack_kernel,
        out_shape=(shape, shape, shape),
        compiler_params=pltpu.CompilerParams(vmem_limit_bytes=VMEM_LIMIT),
        name="unpack",
    )(even, odd)


def document_owner(first, end):
    first_block = first >> BLOCK_BITS
    last_block = (end - 1) >> BLOCK_BITS
    edge = last_block << BLOCK_BITS
    right_larger = (end - edge) > (edge - first)
    span = last_block - first_block
    return first_block + jnp.where((span == 2) | ((span == 1) & right_larger), 1, 0)


def attention_kernel(
    bounds_ref, span_ref, left_ref, own_ref, right_ref,
    left_out, own_out, right_out,
    rows, grads, q_doc, k_doc, v_doc, g_doc, kt_doc, dk_acc, dv_acc, dq_acc, e_buf, p_buf, tops,
):
    window = (lax.axis_index("ctx") - 1) * BLOCK
    pieces = ((left_ref, left_out, 0), (own_ref, own_out, SHARDS), (right_ref, right_out, 2 * SHARDS))

    doc_lo, doc_hi = span_ref[0], span_ref[1]
    some = doc_hi > doc_lo
    shard_lo = jnp.where(some, (bounds_ref[doc_lo] - window) >> SHARD_BITS, 0)
    shard_hi = jnp.where(some, (bounds_ref[doc_hi] - window + SHARD - 1) >> SHARD_BITS, 0)
    zero_shard = jnp.zeros((SHARD, HD), jnp.float32)

    for ref, _, base in pieces:
        lo = jnp.clip(shard_lo - base, 0, ref.shape[0])
        hi = jnp.clip(shard_hi - base, 0, ref.shape[0])

        def load(shard, carry, ref=ref, base=base):
            at = pl.multiple_of((base + shard) * SHARD, SHARD)
            for slot in range(4):
                rows[slot, pl.ds(at, SHARD), :] = ref[shard, slot].astype(jnp.float32)
            return carry

        lax.fori_loop(lo, hi, load, 0)

    for edge in (shard_lo, jnp.maximum(shard_hi - 1, 0)):
        at = pl.multiple_of(edge * SHARD, SHARD)
        for slot in range(3):
            grads[slot, pl.ds(at, SHARD), :] = zero_shard

    def one_document(doc, carry):
        first = bounds_ref[doc] - window
        length = bounds_ref[doc + 1] - bounds_ref[doc]
        tiles = (length + STEP - 1) // STEP
        q_tiles = (length + QSTEP - 1) // QSTEP

        def fetch(part, carry):
            at = pl.multiple_of(part * SHARD, SHARD)
            inside = lax.broadcasted_iota(jnp.int32, (SHARD, HD), 0) + at < length
            for slot, ref in enumerate((q_doc, k_doc, v_doc, g_doc)):
                cut = jnp.where(inside, rows[slot, pl.ds(first + at, SHARD), :], 0.0).astype(jnp.bfloat16)
                ref[pl.ds(at, SHARD), :] = cut
                if slot == 1:
                    kt_doc[:, pl.ds(at, SHARD)] = cut.T
            dk_acc[pl.ds(at, SHARD), :] = zero_shard
            dv_acc[pl.ds(at, SHARD), :] = zero_shard
            return carry

        lax.fori_loop(0, q_tiles * (QSTEP // SHARD), fetch, 0)

        def products(tile, to, size):
            at = pl.multiple_of(tile * QSTEP, QSTEP)
            s = lax.dot_general(
                k_doc[pl.ds(to, size), :], q_doc[pl.ds(at, QSTEP), :],
                (((1,), (1,)), ((), ())), preferred_element_type=jnp.float32)
            p = lax.dot_general(
                v_doc[pl.ds(to, size), :], g_doc[pl.ds(at, QSTEP), :],
                (((1,), (1,)), ((), ())), preferred_element_type=jnp.float32)
            return s, p

        def stats(scores, to, size, carry):
            s_all, p_all = scores
            for part in range(size // PART):
                top, total, dot = carry
                here = to + part * PART
                s = s_all[part * PART:(part + 1) * PART] * (SCALE * LOG2E)
                p = p_all[part * PART:(part + 1) * PART]
                if part >= (size - STEP) // PART:
                    inside = lax.broadcasted_iota(jnp.int32, (PART, QSTEP), 0) + here < length
                    s = jnp.where(inside, s, LOW)
                s = s.reshape(PART // 8, 8, QSTEP)
                new_top = jnp.maximum(top, jnp.max(s, axis=0))
                e = jnp.exp2(s - new_top[None])
                e_buf[pl.ds(here, PART), :] = e.reshape(PART, QSTEP)
                p_buf[pl.ds(here, PART), :] = p
                tops[to // PART + part] = new_top
                shrink = jnp.exp2(top - new_top)
                total = total * shrink + jnp.sum(e, axis=0)
                dot = dot * shrink + jnp.sum(e * p.reshape(PART // 8, 8, QSTEP), axis=0)
                carry = new_top, total, dot
            return carry

        def gradients(tile, to, size, norm, delta):
            at = pl.multiple_of(tile * QSTEP, QSTEP)
            weights, scores = [], []
            for part in range(size // PART):
                here = to + part * PART
                factor = jnp.exp2(tops[to // PART + part] - norm)
                e = e_buf[pl.ds(here, PART), :].reshape(PART // 8, 8, QSTEP) * factor[None]
                p = p_buf[pl.ds(here, PART), :].reshape(PART // 8, 8, QSTEP)
                scores.append((e * (p - delta[None])).reshape(PART, QSTEP).astype(jnp.bfloat16))
                weights.append(e.reshape(PART, QSTEP).astype(jnp.bfloat16))
            weights = jnp.concatenate(weights, axis=0)
            scores = jnp.concatenate(scores, axis=0)
            dv_acc[pl.ds(to, size), :] += jnp.dot(
                weights, g_doc[pl.ds(at, QSTEP), :], preferred_element_type=jnp.float32)
            dk_acc[pl.ds(to, size), :] += jnp.dot(
                scores, q_doc[pl.ds(at, QSTEP), :], preferred_element_type=jnp.float32)
            dq_acc[...] += jnp.dot(
                kt_doc[:, pl.ds(to, size)], scores, preferred_element_type=jnp.float32)

        def over_keys(body, carry):
            to = 0
            for size, steps in ((4 * STEP, tiles >> 2), (STEP, tiles & 3)):
                start = to

                def step(c, now, start=start, size=size):
                    return body(pl.multiple_of(start + c * size, STEP), size, now)

                carry = lax.fori_loop(0, steps, step, carry)
                to = start + steps * size
            return carry

        flat = jnp.zeros((8, QSTEP), jnp.float32)
        fresh = (flat + LOW, flat, flat)

        def joined(top, total, dot):
            peak = jnp.max(top, axis=0, keepdims=True)
            weight = jnp.exp2(top - peak)
            total = jnp.sum(total * weight, axis=0, keepdims=True)
            dot = jnp.sum(dot * weight, axis=0, keepdims=True)
            return flat + (peak + jnp.log2(total)), flat + dot / total

        def put_queries(tile):
            def step(part, carry):
                at = pl.multiple_of(part * SHARD, SHARD)
                to = first + tile * QSTEP + at
                grads[0, pl.ds(to, SHARD), :] = dq_acc[:, pl.ds(at, SHARD)].T * SCALE
                dq_acc[:, pl.ds(at, SHARD)] = zero_shard
                return carry

            lax.fori_loop(0, QSTEP // SHARD, step, 0)

        dq_acc[...] = jnp.zeros((HD, QSTEP), jnp.float32)
        norm_now = joined(*over_keys(lambda to, size, now: stats(products(0, to, size), to, size, now), fresh))

        def query_tile(tile, norms):
            norm, delta = norms

            def both(to, size, now):
                scores = products(tile, to, size)
                gradients(tile - 1, to, size, norm, delta)
                return stats(scores, to, size, now)

            now = over_keys(both, fresh)
            put_queries(tile - 1)
            return joined(*now)

        norm, delta = lax.fori_loop(1, q_tiles, query_tile, norm_now)

        def rest(to, size, now):
            gradients(q_tiles - 1, to, size, norm, delta)
            return now

        over_keys(rest, 0)
        put_queries(q_tiles - 1)

        def put(part, carry):
            at = pl.multiple_of(part * SHARD, SHARD)
            grads[1, pl.ds(first + at, SHARD), :] = dk_acc[pl.ds(at, SHARD), :] * SCALE
            grads[2, pl.ds(first + at, SHARD), :] = dv_acc[pl.ds(at, SHARD), :]
            return carry

        lax.fori_loop(0, (length + SHARD - 1) >> SHARD_BITS, put, 0)
        return carry

    lax.fori_loop(doc_lo, doc_hi, one_document, 0)

    for _, ref, base in pieces:
        lo = jnp.clip(shard_lo - base, 0, ref.shape[0])
        hi = jnp.clip(shard_hi - base, 0, ref.shape[0])

        def empty(shard, carry, ref=ref):
            for slot in range(3):
                ref[shard, slot] = zero_shard.astype(jnp.bfloat16)
            return carry

        def store(shard, carry, ref=ref, base=base):
            at = pl.multiple_of((base + shard) * SHARD, SHARD)
            for slot in range(3):
                ref[shard, slot] = grads[slot, pl.ds(at, SHARD), :].astype(jnp.bfloat16)
            return carry

        lax.fori_loop(0, lo, empty, 0)
        lax.fori_loop(lo, hi, store, 0)
        lax.fori_loop(hi, ref.shape[0], empty, 0)


def attention(bounds, span, left, own, right):
    shape = jax.ShapeDtypeStruct((SHARDS, 3, SHARD, HD), jnp.bfloat16)
    smem = pl.BlockSpec(memory_space=pltpu.SMEM)
    vmem = pl.BlockSpec(memory_space=pltpu.VMEM)
    padded = 3 * BLOCK + QSTEP
    return pl.pallas_call(
        attention_kernel,
        out_shape=(shape, shape, shape),
        in_specs=[smem, smem, vmem, vmem, vmem],
        out_specs=(vmem, vmem, vmem),
        scratch_shapes=[
            pltpu.VMEM((4, padded, HD), jnp.float32),
            pltpu.VMEM((3, padded, HD), jnp.float32),
            pltpu.VMEM((MOST, HD), jnp.bfloat16),
            pltpu.VMEM((MOST, HD), jnp.bfloat16),
            pltpu.VMEM((MOST, HD), jnp.bfloat16),
            pltpu.VMEM((MOST, HD), jnp.bfloat16),
            pltpu.VMEM((HD, MOST), jnp.bfloat16),
            pltpu.VMEM((MOST, HD), jnp.float32),
            pltpu.VMEM((MOST, HD), jnp.float32),
            pltpu.VMEM((HD, QSTEP), jnp.float32),
            pltpu.VMEM((MOST, QSTEP), jnp.float32),
            pltpu.VMEM((MOST, QSTEP), jnp.float32),
            pltpu.VMEM((MOST // PART, 8, QSTEP), jnp.float32),
        ],
        compiler_params=pltpu.CompilerParams(vmem_limit_bytes=38 * 1024 * 1024),
        cost_estimate=pl.CostEstimate(
            flops=5 * 2 * MOST * MOST * HD, bytes_accessed=6 * 1024 * 1024, transcendentals=2 * MOST * MOST
        ),
        name="attention",
    )(bounds, span, left, own, right)


def from_left(shard):
    devices = lax.axis_size("ctx")
    return lax.ppermute(shard, "ctx", [(i, i + 1) for i in range(devices - 1)])


def from_right(shard):
    devices = lax.axis_size("ctx")
    return lax.ppermute(shard, "ctx", [(i + 1, i) for i in range(devices - 1)])


def swap_heads(shard):
    return lax.all_to_all(shard, "head", split_axis=0, concat_axis=0, tiled=True)


def on_device(queries, key_rows, value_rows, out_grad, bounds):
    owner = document_owner(bounds[:-1], bounds[1:])
    me = lax.axis_index("ctx")
    span = jnp.stack([jnp.sum(owner < me), jnp.sum(owner <= me)]).astype(jnp.int32)
    done = []
    for packed in pack(queries, key_rows, value_rows, out_grad):
        own = swap_heads(packed)
        left = from_left(own)
        right = from_right(own)
        left_grad, own_grad, right_grad = attention(bounds, span, left, own, right)
        own_grad = own_grad + from_left(right_grad) + from_right(left_grad)
        done.append(swap_heads(own_grad))
    return unpack(*done)


def solution(mesh):
    rows = P(("ctx", "head"), None)
    return jax.shard_map(
        on_device,
        mesh=mesh,
        in_specs=(rows, rows, rows, rows, P()),
        out_specs=(rows, rows, rows),
        check_vma=False,
    )
```

```python
import jax
import jax.numpy as jnp
from jax import lax
from jax.experimental import pallas as pl
from jax.experimental.pallas import tpu as pltpu
from jax.sharding import PartitionSpec as P

HD = 128
NDOC = 64
BLOCK_BITS = 10
BLOCK = 1 << BLOCK_BITS
SHARD_BITS = 7
SHARD = 1 << SHARD_BITS
SHARDS = BLOCK // SHARD
STEP = 256
QSTEP = 512
PART = 64
MOST = 2048
SCALE = HD ** -0.5
LOG2E = 1.4426950408889634
LOW = -1.0e30
VMEM_LIMIT = 48 * 1024 * 1024
VMEM_ALL = 64 * 1024 * 1024 - 256 * 1024


def pack_kernel(q_ref, k_ref, v_ref, g_ref, even_ref, odd_ref, held, sems):
    copies = []
    for slot, ref in enumerate((q_ref, k_ref, v_ref, g_ref)):
        copies.append(pltpu.make_async_copy(ref, held.at[slot], sems.at[slot]))
    for copy in copies:
        copy.start()
    for slot, copy in enumerate(copies):
        copy.wait()
        for peer in range(SHARDS):
            even_ref[peer, slot] = held[slot, :, pl.ds(2 * peer * HD, HD)]
            odd_ref[peer, slot] = held[slot, :, pl.ds((2 * peer + 1) * HD, HD)]


def pack(queries, key_rows, value_rows, out_grad):
    shape = jax.ShapeDtypeStruct((SHARDS, 4, SHARD, HD), jnp.bfloat16)
    return pl.pallas_call(
        pack_kernel,
        out_shape=(shape, shape),
        in_specs=[pl.BlockSpec(memory_space=pltpu.HBM)] * 4,
        scratch_shapes=[
            pltpu.VMEM((4, SHARD, 2 * SHARDS * HD), jnp.bfloat16),
            pltpu.SemaphoreType.DMA((4,)),
        ],
        compiler_params=pltpu.CompilerParams(vmem_limit_bytes=VMEM_ALL),
        name="pack",
    )(queries, key_rows, value_rows, out_grad)


def unpack_kernel(even_ref, odd_ref, dq_ref, dk_ref, dv_ref):
    for slot, ref in enumerate((dq_ref, dk_ref, dv_ref)):
        for peer in range(SHARDS):
            ref[:, pl.ds(2 * peer * HD, HD)] = even_ref[peer, slot]
            ref[:, pl.ds((2 * peer + 1) * HD, HD)] = odd_ref[peer, slot]


def unpack(even, odd):
    shape = jax.ShapeDtypeStruct((SHARD, 2 * SHARDS * HD), jnp.bfloat16)
    return pl.pallas_call(
        unpack_kernel,
        out_shape=(shape, shape, shape),
        compiler_params=pltpu.CompilerParams(vmem_limit_bytes=VMEM_LIMIT),
        name="unpack",
    )(even, odd)


def document_owner(first, end):
    first_block = first >> BLOCK_BITS
    last_block = (end - 1) >> BLOCK_BITS
    edge = last_block << BLOCK_BITS
    right_larger = (end - edge) > (edge - first)
    span = last_block - first_block
    return first_block + jnp.where((span == 2) | ((span == 1) & right_larger), 1, 0)


def attention_kernel(
    bounds_ref, span_ref, left_ref, own_ref, right_ref,
    left_out, own_out, right_out,
    rows, grads, q_doc, k_doc, v_doc, g_doc, kt_doc, dk_acc, dv_acc, dq_acc, e_buf, p_buf, tops,
):
    window = (lax.axis_index("ctx") - 1) * BLOCK
    pieces = ((left_ref, left_out, 0), (own_ref, own_out, SHARDS), (right_ref, right_out, 2 * SHARDS))

    doc_lo, doc_hi = span_ref[0], span_ref[1]
    some = doc_hi > doc_lo
    shard_lo = jnp.where(some, (bounds_ref[doc_lo] - window) >> SHARD_BITS, 0)
    shard_hi = jnp.where(some, (bounds_ref[doc_hi] - window + SHARD - 1) >> SHARD_BITS, 0)
    zero_tile = jnp.zeros((QSTEP, HD), jnp.float32)
    zero_shard = jnp.zeros((SHARD, HD), jnp.float32)

    for ref, _, base in pieces:
        lo = jnp.clip(shard_lo - base, 0, ref.shape[0])
        hi = jnp.clip(shard_hi - base, 0, ref.shape[0])

        def load(shard, carry, ref=ref, base=base):
            at = pl.multiple_of((base + shard) * SHARD, SHARD)
            for slot in range(4):
                rows[slot, pl.ds(at, SHARD), :] = ref[shard, slot].astype(jnp.float32)
            return carry

        lax.fori_loop(lo, hi, load, 0)

    for edge in (shard_lo, jnp.maximum(shard_hi - 1, 0)):
        at = pl.multiple_of(edge * SHARD, SHARD)
        for slot in range(3):
            grads[slot, pl.ds(at, SHARD), :] = zero_shard

    def one_document(doc, carry):
        first = bounds_ref[doc] - window
        length = bounds_ref[doc + 1] - bounds_ref[doc]
        tiles = (length + STEP - 1) // STEP
        q_tiles = (length + QSTEP - 1) // QSTEP

        def fetch(part, carry):
            at = pl.multiple_of(part * QSTEP, QSTEP)
            inside = lax.broadcasted_iota(jnp.int32, (QSTEP, HD), 0) + at < length
            for slot, ref in enumerate((q_doc, k_doc, v_doc, g_doc)):
                cut = jnp.where(inside, rows[slot, pl.ds(first + at, QSTEP), :], 0.0).astype(jnp.bfloat16)
                ref[pl.ds(at, QSTEP), :] = cut
                if slot == 1:
                    kt_doc[:, pl.ds(at, QSTEP)] = cut.T
            dk_acc[pl.ds(at, QSTEP), :] = zero_tile
            dv_acc[pl.ds(at, QSTEP), :] = zero_tile
            return carry

        lax.fori_loop(0, q_tiles, fetch, 0)

        def products(tile, to, size):
            at = pl.multiple_of(tile * QSTEP, QSTEP)
            s = lax.dot_general(
                k_doc[pl.ds(to, size), :], q_doc[pl.ds(at, QSTEP), :],
                (((1,), (1,)), ((), ())), preferred_element_type=jnp.float32)
            p = lax.dot_general(
                v_doc[pl.ds(to, size), :], g_doc[pl.ds(at, QSTEP), :],
                (((1,), (1,)), ((), ())), preferred_element_type=jnp.float32)
            return s, p

        def stats(scores, to, size, carry):
            s_all, p_all = scores
            for part in range(size // PART):
                top, total, dot = carry
                here = to + part * PART
                s = s_all[part * PART:(part + 1) * PART] * (SCALE * LOG2E)
                p = p_all[part * PART:(part + 1) * PART]
                if part >= (size - STEP) // PART:
                    inside = lax.broadcasted_iota(jnp.int32, (PART, QSTEP), 0) + here < length
                    s = jnp.where(inside, s, LOW)
                s = s.reshape(PART // 8, 8, QSTEP)
                new_top = jnp.maximum(top, jnp.max(s, axis=0))
                e = jnp.exp2(s - new_top[None])
                e_buf[pl.ds(here, PART), :] = e.reshape(PART, QSTEP)
                p_buf[pl.ds(here, PART), :] = p
                tops[to // PART + part] = new_top
                shrink = jnp.exp2(top - new_top)
                total = total * shrink + jnp.sum(e, axis=0)
                dot = dot * shrink + jnp.sum(e * p.reshape(PART // 8, 8, QSTEP), axis=0)
                carry = new_top, total, dot
            return carry

        def gradients(tile, to, size, norm, delta):
            at = pl.multiple_of(tile * QSTEP, QSTEP)
            weights, scores = [], []
            for part in range(size // PART):
                here = to + part * PART
                factor = jnp.exp2(tops[to // PART + part] - norm)
                e = e_buf[pl.ds(here, PART), :].reshape(PART // 8, 8, QSTEP) * factor[None]
                p = p_buf[pl.ds(here, PART), :].reshape(PART // 8, 8, QSTEP)
                scores.append((e * (p - delta[None])).reshape(PART, QSTEP).astype(jnp.bfloat16))
                weights.append(e.reshape(PART, QSTEP).astype(jnp.bfloat16))
            weights = jnp.concatenate(weights, axis=0)
            scores = jnp.concatenate(scores, axis=0)
            dv_acc[pl.ds(to, size), :] += jnp.dot(
                weights, g_doc[pl.ds(at, QSTEP), :], preferred_element_type=jnp.float32)
            dk_acc[pl.ds(to, size), :] += jnp.dot(
                scores, q_doc[pl.ds(at, QSTEP), :], preferred_element_type=jnp.float32)
            dq_acc[...] += jnp.dot(
                kt_doc[:, pl.ds(to, size)], scores, preferred_element_type=jnp.float32)

        def over_keys(body, carry):
            to = 0
            for size, steps in ((4 * STEP, tiles >> 2), (STEP, tiles & 3)):
                start = to

                def step(c, now, start=start, size=size):
                    return body(pl.multiple_of(start + c * size, STEP), size, now)

                carry = lax.fori_loop(0, steps, step, carry)
                to = start + steps * size
            return carry

        flat = jnp.zeros((8, QSTEP), jnp.float32)
        fresh = (flat + LOW, flat, flat)

        def joined(top, total, dot):
            peak = jnp.max(top, axis=0, keepdims=True)
            weight = jnp.exp2(top - peak)
            total = jnp.sum(total * weight, axis=0, keepdims=True)
            dot = jnp.sum(dot * weight, axis=0, keepdims=True)
            return flat + (peak + jnp.log2(total)), flat + dot / total

        def put_queries(tile):
            at = pl.multiple_of(tile * QSTEP, QSTEP)
            grads[0, pl.ds(first + at, QSTEP), :] = dq_acc[...].T * SCALE
            dq_acc[...] = jnp.zeros((HD, QSTEP), jnp.float32)

        dq_acc[...] = jnp.zeros((HD, QSTEP), jnp.float32)
        norm_now = joined(*over_keys(lambda to, size, now: stats(products(0, to, size), to, size, now), fresh))

        def query_tile(tile, norms):
            norm, delta = norms

            def both(to, size, now):
                scores = products(tile, to, size)
                gradients(tile - 1, to, size, norm, delta)
                return stats(scores, to, size, now)

            now = over_keys(both, fresh)
            put_queries(tile - 1)
            return joined(*now)

        norm, delta = lax.fori_loop(1, q_tiles, query_tile, norm_now)

        def rest(to, size, now):
            gradients(q_tiles - 1, to, size, norm, delta)
            return now

        over_keys(rest, 0)
        put_queries(q_tiles - 1)

        def put(part, carry):
            at = pl.multiple_of(part * QSTEP, QSTEP)
            grads[1, pl.ds(first + at, QSTEP), :] = dk_acc[pl.ds(at, QSTEP), :] * SCALE
            grads[2, pl.ds(first + at, QSTEP), :] = dv_acc[pl.ds(at, QSTEP), :]
            return carry

        lax.fori_loop(0, q_tiles, put, 0)
        return carry

    lax.fori_loop(doc_lo, doc_hi, one_document, 0)

    for _, ref, base in pieces:
        lo = jnp.clip(shard_lo - base, 0, ref.shape[0])
        hi = jnp.clip(shard_hi - base, 0, ref.shape[0])

        def empty(shard, carry, ref=ref):
            for slot in range(3):
                ref[shard, slot] = zero_shard.astype(jnp.bfloat16)
            return carry

        def store(shard, carry, ref=ref, base=base):
            at = pl.multiple_of((base + shard) * SHARD, SHARD)
            for slot in range(3):
                ref[shard, slot] = grads[slot, pl.ds(at, SHARD), :].astype(jnp.bfloat16)
            return carry

        lax.fori_loop(0, lo, empty, 0)
        lax.fori_loop(lo, hi, store, 0)
        lax.fori_loop(hi, ref.shape[0], empty, 0)


def attention(bounds, span, left, own, right):
    shape = jax.ShapeDtypeStruct((SHARDS, 3, SHARD, HD), jnp.bfloat16)
    smem = pl.BlockSpec(memory_space=pltpu.SMEM)
    vmem = pl.BlockSpec(memory_space=pltpu.VMEM)
    padded = 3 * BLOCK + QSTEP
    return pl.pallas_call(
        attention_kernel,
        out_shape=(shape, shape, shape),
        in_specs=[smem, smem, vmem, vmem, vmem],
        out_specs=(vmem, vmem, vmem),
        scratch_shapes=[
            pltpu.VMEM((4, padded, HD), jnp.float32),
            pltpu.VMEM((3, padded, HD), jnp.float32),
            pltpu.VMEM((MOST, HD), jnp.bfloat16),
            pltpu.VMEM((MOST, HD), jnp.bfloat16),
            pltpu.VMEM((MOST, HD), jnp.bfloat16),
            pltpu.VMEM((MOST, HD), jnp.bfloat16),
            pltpu.VMEM((HD, MOST), jnp.bfloat16),
            pltpu.VMEM((MOST, HD), jnp.float32),
            pltpu.VMEM((MOST, HD), jnp.float32),
            pltpu.VMEM((HD, QSTEP), jnp.float32),
            pltpu.VMEM((MOST, QSTEP), jnp.float32),
            pltpu.VMEM((MOST, QSTEP), jnp.float32),
            pltpu.VMEM((MOST // PART, 8, QSTEP), jnp.float32),
        ],
        compiler_params=pltpu.CompilerParams(vmem_limit_bytes=38 * 1024 * 1024),
        cost_estimate=pl.CostEstimate(
            flops=5 * 2 * MOST * MOST * HD, bytes_accessed=6 * 1024 * 1024, transcendentals=2 * MOST * MOST
        ),
        name="attention",
    )(bounds, span, left, own, right)


def from_left(shard):
    devices = lax.axis_size("ctx")
    return lax.ppermute(shard, "ctx", [(i, i + 1) for i in range(devices - 1)])


def from_right(shard):
    devices = lax.axis_size("ctx")
    return lax.ppermute(shard, "ctx", [(i + 1, i) for i in range(devices - 1)])


def swap_heads(shard):
    return lax.all_to_all(shard, "head", split_axis=0, concat_axis=0, tiled=True)


def on_device(queries, key_rows, value_rows, out_grad, bounds):
    owner = document_owner(bounds[:-1], bounds[1:])
    me = lax.axis_index("ctx")
    span = jnp.stack([jnp.sum(owner < me), jnp.sum(owner <= me)]).astype(jnp.int32)
    done = []
    for packed in pack(queries, key_rows, value_rows, out_grad):
        own = swap_heads(packed)
        left = from_left(own)
        right = from_right(own)
        left_grad, own_grad, right_grad = attention(bounds, span, left, own, right)
        own_grad = own_grad + from_left(right_grad) + from_right(left_grad)
        done.append(swap_heads(own_grad))
    return unpack(*done)


def solution(mesh):
    rows = P(("ctx", "head"), None)
    return jax.shard_map(
        on_device,
        mesh=mesh,
        in_specs=(rows, rows, rows, rows, P()),
        out_specs=(rows, rows, rows),
        check_vma=False,
    )
```

```python
import jax
import jax.numpy as jnp
from jax import lax
from jax.experimental import pallas as pl
from jax.experimental.pallas import tpu as pltpu
from jax.sharding import PartitionSpec as P

HD = 128
NDOC = 64
BLOCK_BITS = 10
BLOCK = 1 << BLOCK_BITS
SHARD_BITS = 7
SHARD = 1 << SHARD_BITS
SHARDS = BLOCK // SHARD
STEP = 256
QSTEP = 512
PART = 64
MOST = 2048
SCALE = HD ** -0.5
LOG2E = 1.4426950408889634
LOW = -1.0e30
VMEM_LIMIT = 48 * 1024 * 1024
VMEM_ALL = 64 * 1024 * 1024 - 256 * 1024


def pack_kernel(q_ref, k_ref, v_ref, g_ref, even_ref, odd_ref, held, packed, in_sems, out_sems):
    copies_in, copies_out = [], []
    for slot, ref in enumerate((q_ref, k_ref, v_ref, g_ref)):
        copies_in.append(pltpu.make_async_copy(ref, held.at[slot], in_sems.at[slot]))
        for parity, out_ref in enumerate((even_ref, odd_ref)):
            copies_out.append(pltpu.make_async_copy(
                packed.at[parity, slot], out_ref.at[:, slot], out_sems.at[2 * slot + parity]))
    for copy in copies_in:
        copy.start()
    for slot, copy in enumerate(copies_in):
        copy.wait()
        for parity in range(2):
            for peer in range(SHARDS):
                packed[parity, slot, peer] = held[slot, :, pl.ds((2 * peer + parity) * HD, HD)]
            copies_out[2 * slot + parity].start()
    for copy in copies_out:
        copy.wait()


def pack(queries, key_rows, value_rows, out_grad):
    shape = jax.ShapeDtypeStruct((SHARDS, 4, SHARD, HD), jnp.bfloat16)
    anywhere = pl.BlockSpec(memory_space=pl.ANY)
    return pl.pallas_call(
        pack_kernel,
        out_shape=(shape, shape),
        in_specs=[anywhere] * 4,
        out_specs=(anywhere, anywhere),
        scratch_shapes=[
            pltpu.VMEM((4, SHARD, 2 * SHARDS * HD), jnp.bfloat16),
            pltpu.VMEM((2, 4, SHARDS, SHARD, HD), jnp.bfloat16),
            pltpu.SemaphoreType.DMA((4,)),
            pltpu.SemaphoreType.DMA((8,)),
        ],
        compiler_params=pltpu.CompilerParams(vmem_limit_bytes=VMEM_ALL),
        name="pack",
    )(queries, key_rows, value_rows, out_grad)


def unpack_kernel(even_ref, odd_ref, dq_ref, dk_ref, dv_ref):
    for slot, ref in enumerate((dq_ref, dk_ref, dv_ref)):
        for peer in range(SHARDS):
            ref[:, pl.ds(2 * peer * HD, HD)] = even_ref[peer, slot]
            ref[:, pl.ds((2 * peer + 1) * HD, HD)] = odd_ref[peer, slot]


def unpack(even, odd):
    shape = jax.ShapeDtypeStruct((SHARD, 2 * SHARDS * HD), jnp.bfloat16)
    return pl.pallas_call(
        unpack_kernel,
        out_shape=(shape, shape, shape),
        compiler_params=pltpu.CompilerParams(vmem_limit_bytes=VMEM_LIMIT),
        name="unpack",
    )(even, odd)


def document_owner(first, end):
    first_block = first >> BLOCK_BITS
    last_block = (end - 1) >> BLOCK_BITS
    edge = last_block << BLOCK_BITS
    right_larger = (end - edge) > (edge - first)
    span = last_block - first_block
    return first_block + jnp.where((span == 2) | ((span == 1) & right_larger), 1, 0)


def attention_kernel(
    bounds_ref, span_ref, left_ref, own_ref, right_ref,
    left_out, own_out, right_out,
    rows, grads, q_doc, k_doc, v_doc, g_doc, kt_doc, dk_acc, dv_acc, dq_acc, e_buf, p_buf, tops,
):
    window = (lax.axis_index("ctx") - 1) * BLOCK
    pieces = ((left_ref, left_out, 0), (own_ref, own_out, SHARDS), (right_ref, right_out, 2 * SHARDS))

    doc_lo, doc_hi = span_ref[0], span_ref[1]
    some = doc_hi > doc_lo
    shard_lo = jnp.where(some, (bounds_ref[doc_lo] - window) >> SHARD_BITS, 0)
    shard_hi = jnp.where(some, (bounds_ref[doc_hi] - window + SHARD - 1) >> SHARD_BITS, 0)
    zero_tile = jnp.zeros((QSTEP, HD), jnp.float32)
    zero_shard = jnp.zeros((SHARD, HD), jnp.float32)

    for ref, _, base in pieces:
        lo = jnp.clip(shard_lo - base, 0, ref.shape[0])
        hi = jnp.clip(shard_hi - base, 0, ref.shape[0])

        def load(shard, carry, ref=ref, base=base):
            at = pl.multiple_of((base + shard) * SHARD, SHARD)
            for slot in range(4):
                rows[slot, pl.ds(at, SHARD), :] = ref[shard, slot].astype(jnp.float32)
            return carry

        lax.fori_loop(lo, hi, load, 0)

    for edge in (shard_lo, jnp.maximum(shard_hi - 1, 0)):
        at = pl.multiple_of(edge * SHARD, SHARD)
        for slot in range(3):
            grads[slot, pl.ds(at, SHARD), :] = zero_shard

    def one_document(doc, carry):
        first = bounds_ref[doc] - window
        length = bounds_ref[doc + 1] - bounds_ref[doc]
        tiles = (length + STEP - 1) // STEP
        q_tiles = (length + QSTEP - 1) // QSTEP

        def fetch(part, carry):
            at = pl.multiple_of(part * QSTEP, QSTEP)
            inside = lax.broadcasted_iota(jnp.int32, (QSTEP, HD), 0) + at < length
            for slot, ref in enumerate((q_doc, k_doc, v_doc, g_doc)):
                cut = jnp.where(inside, rows[slot, pl.ds(first + at, QSTEP), :], 0.0).astype(jnp.bfloat16)
                ref[pl.ds(at, QSTEP), :] = cut
                if slot == 1:
                    kt_doc[:, pl.ds(at, QSTEP)] = cut.T
            dk_acc[pl.ds(at, QSTEP), :] = zero_tile
            dv_acc[pl.ds(at, QSTEP), :] = zero_tile
            return carry

        lax.fori_loop(0, q_tiles, fetch, 0)

        def products(tile, to, size):
            at = pl.multiple_of(tile * QSTEP, QSTEP)
            s = lax.dot_general(
                k_doc[pl.ds(to, size), :], q_doc[pl.ds(at, QSTEP), :],
                (((1,), (1,)), ((), ())), preferred_element_type=jnp.float32)
            p = lax.dot_general(
                v_doc[pl.ds(to, size), :], g_doc[pl.ds(at, QSTEP), :],
                (((1,), (1,)), ((), ())), preferred_element_type=jnp.float32)
            return s, p

        def stats(scores, to, size, carry):
            s_all, p_all = scores
            for part in range(size // PART):
                top, total, dot = carry
                here = to + part * PART
                s = s_all[part * PART:(part + 1) * PART] * (SCALE * LOG2E)
                p = p_all[part * PART:(part + 1) * PART]
                if part >= (size - STEP) // PART:
                    inside = lax.broadcasted_iota(jnp.int32, (PART, QSTEP), 0) + here < length
                    s = jnp.where(inside, s, LOW)
                s = s.reshape(PART // 8, 8, QSTEP)
                new_top = jnp.maximum(top, jnp.max(s, axis=0))
                e = jnp.exp2(s - new_top[None])
                e_buf[pl.ds(here, PART), :] = e.reshape(PART, QSTEP)
                p_buf[pl.ds(here, PART), :] = p
                tops[to // PART + part] = new_top
                shrink = jnp.exp2(top - new_top)
                total = total * shrink + jnp.sum(e, axis=0)
                dot = dot * shrink + jnp.sum(e * p.reshape(PART // 8, 8, QSTEP), axis=0)
                carry = new_top, total, dot
            return carry

        def gradients(tile, to, size, norm, delta):
            at = pl.multiple_of(tile * QSTEP, QSTEP)
            weights, scores = [], []
            for part in range(size // PART):
                here = to + part * PART
                factor = jnp.exp2(tops[to // PART + part] - norm)
                e = e_buf[pl.ds(here, PART), :].reshape(PART // 8, 8, QSTEP) * factor[None]
                p = p_buf[pl.ds(here, PART), :].reshape(PART // 8, 8, QSTEP)
                scores.append((e * (p - delta[None])).reshape(PART, QSTEP).astype(jnp.bfloat16))
                weights.append(e.reshape(PART, QSTEP).astype(jnp.bfloat16))
            weights = jnp.concatenate(weights, axis=0)
            scores = jnp.concatenate(scores, axis=0)
            dv_acc[pl.ds(to, size), :] += jnp.dot(
                weights, g_doc[pl.ds(at, QSTEP), :], preferred_element_type=jnp.float32)
            dk_acc[pl.ds(to, size), :] += jnp.dot(
                scores, q_doc[pl.ds(at, QSTEP), :], preferred_element_type=jnp.float32)
            dq_acc[...] += jnp.dot(
                kt_doc[:, pl.ds(to, size)], scores, preferred_element_type=jnp.float32)

        def over_keys(body, carry):
            to = 0
            for size, steps in ((4 * STEP, tiles >> 2), (STEP, tiles & 3)):
                start = to

                def step(c, now, start=start, size=size):
                    return body(pl.multiple_of(start + c * size, STEP), size, now)

                carry = lax.fori_loop(0, steps, step, carry)
                to = start + steps * size
            return carry

        flat = jnp.zeros((8, QSTEP), jnp.float32)
        fresh = (flat + LOW, flat, flat)

        def joined(top, total, dot):
            peak = jnp.max(top, axis=0, keepdims=True)
            weight = jnp.exp2(top - peak)
            total = jnp.sum(total * weight, axis=0, keepdims=True)
            dot = jnp.sum(dot * weight, axis=0, keepdims=True)
            return flat + (peak + jnp.log2(total)), flat + dot / total

        def put_queries(tile):
            at = pl.multiple_of(tile * QSTEP, QSTEP)
            grads[0, pl.ds(first + at, QSTEP), :] = dq_acc[...].T * SCALE
            dq_acc[...] = jnp.zeros((HD, QSTEP), jnp.float32)

        dq_acc[...] = jnp.zeros((HD, QSTEP), jnp.float32)
        norm_now = joined(*over_keys(lambda to, size, now: stats(products(0, to, size), to, size, now), fresh))

        def query_tile(tile, norms):
            norm, delta = norms

            def both(to, size, now):
                scores = products(tile, to, size)
                gradients(tile - 1, to, size, norm, delta)
                return stats(scores, to, size, now)

            now = over_keys(both, fresh)
            put_queries(tile - 1)
            return joined(*now)

        norm, delta = lax.fori_loop(1, q_tiles, query_tile, norm_now)

        def rest(to, size, now):
            gradients(q_tiles - 1, to, size, norm, delta)
            return now

        over_keys(rest, 0)
        put_queries(q_tiles - 1)

        def put(part, carry):
            at = pl.multiple_of(part * QSTEP, QSTEP)
            grads[1, pl.ds(first + at, QSTEP), :] = dk_acc[pl.ds(at, QSTEP), :] * SCALE
            grads[2, pl.ds(first + at, QSTEP), :] = dv_acc[pl.ds(at, QSTEP), :]
            return carry

        lax.fori_loop(0, q_tiles, put, 0)
        return carry

    lax.fori_loop(doc_lo, doc_hi, one_document, 0)

    for _, ref, base in pieces:
        lo = jnp.clip(shard_lo - base, 0, ref.shape[0])
        hi = jnp.clip(shard_hi - base, 0, ref.shape[0])

        def empty(shard, carry, ref=ref):
            for slot in range(3):
                ref[shard, slot] = zero_shard.astype(jnp.bfloat16)
            return carry

        def store(shard, carry, ref=ref, base=base):
            at = pl.multiple_of((base + shard) * SHARD, SHARD)
            for slot in range(3):
                ref[shard, slot] = grads[slot, pl.ds(at, SHARD), :].astype(jnp.bfloat16)
            return carry

        lax.fori_loop(0, lo, empty, 0)
        lax.fori_loop(lo, hi, store, 0)
        lax.fori_loop(hi, ref.shape[0], empty, 0)


def attention(bounds, span, left, own, right):
    shape = jax.ShapeDtypeStruct((SHARDS, 3, SHARD, HD), jnp.bfloat16)
    smem = pl.BlockSpec(memory_space=pltpu.SMEM)
    vmem = pl.BlockSpec(memory_space=pltpu.VMEM)
    padded = 3 * BLOCK + QSTEP
    return pl.pallas_call(
        attention_kernel,
        out_shape=(shape, shape, shape),
        in_specs=[smem, smem, vmem, vmem, vmem],
        out_specs=(vmem, vmem, vmem),
        scratch_shapes=[
            pltpu.VMEM((4, padded, HD), jnp.float32),
            pltpu.VMEM((3, padded, HD), jnp.float32),
            pltpu.VMEM((MOST, HD), jnp.bfloat16),
            pltpu.VMEM((MOST, HD), jnp.bfloat16),
            pltpu.VMEM((MOST, HD), jnp.bfloat16),
            pltpu.VMEM((MOST, HD), jnp.bfloat16),
            pltpu.VMEM((HD, MOST), jnp.bfloat16),
            pltpu.VMEM((MOST, HD), jnp.float32),
            pltpu.VMEM((MOST, HD), jnp.float32),
            pltpu.VMEM((HD, QSTEP), jnp.float32),
            pltpu.VMEM((MOST, QSTEP), jnp.float32),
            pltpu.VMEM((MOST, QSTEP), jnp.float32),
            pltpu.VMEM((MOST // PART, 8, QSTEP), jnp.float32),
        ],
        compiler_params=pltpu.CompilerParams(vmem_limit_bytes=38 * 1024 * 1024),
        cost_estimate=pl.CostEstimate(
            flops=5 * 2 * MOST * MOST * HD, bytes_accessed=6 * 1024 * 1024, transcendentals=2 * MOST * MOST
        ),
        name="attention",
    )(bounds, span, left, own, right)


def total_kernel(own_ref, left_ref, right_ref, out_ref):
    def step(shard, carry):
        for slot in range(3):
            parts = [ref[shard, slot].astype(jnp.float32) for ref in (own_ref, left_ref, right_ref)]
            out_ref[shard, slot] = (parts[0] + parts[1] + parts[2]).astype(jnp.bfloat16)
        return carry

    lax.fori_loop(0, SHARDS, step, 0)


def total(own, left, right):
    vmem = pl.BlockSpec(memory_space=pltpu.VMEM)
    return pl.pallas_call(
        total_kernel,
        out_shape=jax.ShapeDtypeStruct(own.shape, own.dtype),
        in_specs=[vmem] * 3,
        out_specs=vmem,
        compiler_params=pltpu.CompilerParams(vmem_limit_bytes=16 * 1024 * 1024),
        cost_estimate=pl.CostEstimate(flops=0, bytes_accessed=3 * 1024 * 1024, transcendentals=0),
        name="total",
    )(own, left, right)


def from_left(shard):
    devices = lax.axis_size("ctx")
    return lax.ppermute(shard, "ctx", [(i, i + 1) for i in range(devices - 1)])


def from_right(shard):
    devices = lax.axis_size("ctx")
    return lax.ppermute(shard, "ctx", [(i + 1, i) for i in range(devices - 1)])


def swap_heads(shard):
    return lax.all_to_all(shard, "head", split_axis=0, concat_axis=0, tiled=True)


def on_device(queries, key_rows, value_rows, out_grad, bounds):
    owner = document_owner(bounds[:-1], bounds[1:])
    me = lax.axis_index("ctx")
    span = jnp.stack([jnp.sum(owner < me), jnp.sum(owner <= me)]).astype(jnp.int32)
    done = []
    for packed in pack(queries, key_rows, value_rows, out_grad):
        own = swap_heads(packed)
        left = from_left(own)
        right = from_right(own)
        left_grad, own_grad, right_grad = attention(bounds, span, left, own, right)
        own_grad = total(own_grad, from_left(right_grad), from_right(left_grad))
        done.append(swap_heads(own_grad))
    return unpack(*done)


def solution(mesh):
    rows = P(("ctx", "head"), None)
    return jax.shard_map(
        on_device,
        mesh=mesh,
        in_specs=(rows, rows, rows, rows, P()),
        out_specs=(rows, rows, rows),
        check_vma=False,
    )
```

```python
import jax
import jax.numpy as jnp
from jax import lax
from jax.experimental import pallas as pl
from jax.experimental.pallas import tpu as pltpu
from jax.sharding import PartitionSpec as P

HD = 128
NDOC = 64
BLOCK_BITS = 10
BLOCK = 1 << BLOCK_BITS
SHARD_BITS = 7
SHARD = 1 << SHARD_BITS
SHARDS = BLOCK // SHARD
STEP = 256
QSTEP = 512
PART = 64
MOST = 2048
SCALE = HD ** -0.5
LOG2E = 1.4426950408889634
LOW = -1.0e30
VMEM_LIMIT = 48 * 1024 * 1024
VMEM_ALL = 64 * 1024 * 1024 - 256 * 1024


def pack_kernel(q_ref, k_ref, v_ref, g_ref, even_ref, odd_ref, held, packed, in_sems, out_sems):
    copies_in, copies_out = [], []
    for slot, ref in enumerate((q_ref, k_ref, v_ref, g_ref)):
        copies_in.append(pltpu.make_async_copy(ref, held.at[slot], in_sems.at[slot]))
        for parity, out_ref in enumerate((even_ref, odd_ref)):
            copies_out.append(pltpu.make_async_copy(
                packed.at[parity, slot], out_ref.at[:, slot], out_sems.at[2 * slot + parity]))
    for copy in copies_in:
        copy.start()
    for slot, copy in enumerate(copies_in):
        copy.wait()
        for parity in range(2):
            for peer in range(SHARDS):
                packed[parity, slot, peer] = held[slot, :, pl.ds((2 * peer + parity) * HD, HD)]
            copies_out[2 * slot + parity].start()
    for copy in copies_out:
        copy.wait()


def pack(queries, key_rows, value_rows, out_grad):
    shape = jax.ShapeDtypeStruct((SHARDS, 4, SHARD, HD), jnp.bfloat16)
    anywhere = pl.BlockSpec(memory_space=pl.ANY)
    return pl.pallas_call(
        pack_kernel,
        out_shape=(shape, shape),
        in_specs=[anywhere] * 4,
        out_specs=(anywhere, anywhere),
        scratch_shapes=[
            pltpu.VMEM((4, SHARD, 2 * SHARDS * HD), jnp.bfloat16),
            pltpu.VMEM((2, 4, SHARDS, SHARD, HD), jnp.bfloat16),
            pltpu.SemaphoreType.DMA((4,)),
            pltpu.SemaphoreType.DMA((8,)),
        ],
        compiler_params=pltpu.CompilerParams(vmem_limit_bytes=VMEM_ALL),
        name="pack",
    )(queries, key_rows, value_rows, out_grad)


def unpack_kernel(even_ref, odd_ref, dq_ref, dk_ref, dv_ref):
    for slot, ref in enumerate((dq_ref, dk_ref, dv_ref)):
        for peer in range(SHARDS):
            ref[:, pl.ds(2 * peer * HD, HD)] = even_ref[peer, slot]
            ref[:, pl.ds((2 * peer + 1) * HD, HD)] = odd_ref[peer, slot]


def unpack(even, odd):
    shape = jax.ShapeDtypeStruct((SHARD, 2 * SHARDS * HD), jnp.bfloat16)
    return pl.pallas_call(
        unpack_kernel,
        out_shape=(shape, shape, shape),
        compiler_params=pltpu.CompilerParams(vmem_limit_bytes=VMEM_LIMIT),
        name="unpack",
    )(even, odd)


def document_owner(first, end):
    first_block = first >> BLOCK_BITS
    last_block = (end - 1) >> BLOCK_BITS
    edge = last_block << BLOCK_BITS
    right_larger = (end - edge) > (edge - first)
    span = last_block - first_block
    return first_block + jnp.where((span == 2) | ((span == 1) & right_larger), 1, 0)


def attention_kernel(
    bounds_ref, span_ref, left_ref, own_ref, right_ref,
    left_out, own_out, right_out,
    rows, grads, q_doc, k_doc, v_doc, g_doc, kt_doc, dk_acc, dv_acc, dq_acc, e_buf, p_buf, tops,
):
    window = (lax.axis_index("ctx") - 1) * BLOCK
    pieces = ((left_ref, left_out, 0), (own_ref, own_out, SHARDS), (right_ref, right_out, 2 * SHARDS))

    doc_lo, doc_hi = span_ref[0], span_ref[1]
    some = doc_hi > doc_lo
    shard_lo = jnp.where(some, (bounds_ref[doc_lo] - window) >> SHARD_BITS, 0)
    shard_hi = jnp.where(some, (bounds_ref[doc_hi] - window + SHARD - 1) >> SHARD_BITS, 0)
    zero_tile = jnp.zeros((QSTEP, HD), jnp.float32)
    zero_shard = jnp.zeros((SHARD, HD), jnp.float32)

    for ref, _, base in pieces:
        lo = jnp.clip(shard_lo - base, 0, ref.shape[0])
        hi = jnp.clip(shard_hi - base, 0, ref.shape[0])

        def load(shard, carry, ref=ref, base=base):
            at = pl.multiple_of((base + shard) * SHARD, SHARD)
            for slot in range(4):
                rows[slot, pl.ds(at, SHARD), :] = ref[shard, slot].astype(jnp.float32)
            return carry

        lax.fori_loop(lo, hi, load, 0)

    for edge in (shard_lo, jnp.maximum(shard_hi - 1, 0)):
        at = pl.multiple_of(edge * SHARD, SHARD)
        for slot in range(3):
            grads[slot, pl.ds(at, SHARD), :] = zero_shard

    def one_document(doc, carry):
        first = bounds_ref[doc] - window
        length = bounds_ref[doc + 1] - bounds_ref[doc]
        tiles = (length + STEP - 1) // STEP
        q_tiles = (length + QSTEP - 1) // QSTEP

        def fetch(part, carry):
            at = pl.multiple_of(part * QSTEP, QSTEP)
            inside = lax.broadcasted_iota(jnp.int32, (QSTEP, HD), 0) + at < length
            for slot, ref in enumerate((q_doc, k_doc, v_doc, g_doc)):
                cut = jnp.where(inside, rows[slot, pl.ds(first + at, QSTEP), :], 0.0).astype(jnp.bfloat16)
                ref[pl.ds(at, QSTEP), :] = cut
                if slot == 1:
                    kt_doc[:, pl.ds(at, QSTEP)] = cut.T
            dk_acc[pl.ds(at, QSTEP), :] = zero_tile
            dv_acc[pl.ds(at, QSTEP), :] = zero_tile
            return carry

        lax.fori_loop(0, q_tiles, fetch, 0)

        def products(tile, to, size):
            at = pl.multiple_of(tile * QSTEP, QSTEP)
            s = lax.dot_general(
                k_doc[pl.ds(to, size), :], q_doc[pl.ds(at, QSTEP), :],
                (((1,), (1,)), ((), ())), preferred_element_type=jnp.float32)
            p = lax.dot_general(
                v_doc[pl.ds(to, size), :], g_doc[pl.ds(at, QSTEP), :],
                (((1,), (1,)), ((), ())), preferred_element_type=jnp.float32)
            return s, p

        def stats(scores, to, size, carry):
            s_all, p_all = scores
            for part in range(size // PART):
                top, total, dot = carry
                here = to + part * PART
                s = s_all[part * PART:(part + 1) * PART] * (SCALE * LOG2E)
                p = p_all[part * PART:(part + 1) * PART]
                if part >= (size - STEP) // PART:
                    inside = lax.broadcasted_iota(jnp.int32, (PART, QSTEP), 0) + here < length
                    s = jnp.where(inside, s, LOW)
                s = s.reshape(PART // 8, 8, QSTEP)
                new_top = jnp.maximum(top, jnp.max(s, axis=0))
                e = jnp.exp2(s - new_top[None])
                e_buf[pl.ds(here, PART), :] = e.reshape(PART, QSTEP)
                p_buf[pl.ds(here, PART), :] = p
                tops[to // PART + part] = new_top
                shrink = jnp.exp2(top - new_top)
                total = total * shrink + jnp.sum(e, axis=0)
                dot = dot * shrink + jnp.sum(e * p.reshape(PART // 8, 8, QSTEP), axis=0)
                carry = new_top, total, dot
            return carry

        def gradients(tile, to, size, norm, delta):
            at = pl.multiple_of(tile * QSTEP, QSTEP)
            weights, scores = [], []
            for part in range(size // PART):
                here = to + part * PART
                factor = jnp.exp2(tops[to // PART + part] - norm)
                e = e_buf[pl.ds(here, PART), :].reshape(PART // 8, 8, QSTEP) * factor[None]
                p = p_buf[pl.ds(here, PART), :].reshape(PART // 8, 8, QSTEP)
                scores.append((e * (p - delta[None])).reshape(PART, QSTEP).astype(jnp.bfloat16))
                weights.append(e.reshape(PART, QSTEP).astype(jnp.bfloat16))
            weights = jnp.concatenate(weights, axis=0)
            scores = jnp.concatenate(scores, axis=0)
            dv_acc[pl.ds(to, size), :] += jnp.dot(
                weights, g_doc[pl.ds(at, QSTEP), :], preferred_element_type=jnp.float32)
            dk_acc[pl.ds(to, size), :] += jnp.dot(
                scores, q_doc[pl.ds(at, QSTEP), :], preferred_element_type=jnp.float32)
            dq_acc[...] += jnp.dot(
                kt_doc[:, pl.ds(to, size)], scores, preferred_element_type=jnp.float32)

        def over_keys(body, carry):
            to = 0
            for size, steps in ((4 * STEP, tiles >> 2), (STEP, tiles & 3)):
                start = to

                def step(c, now, start=start, size=size):
                    return body(pl.multiple_of(start + c * size, STEP), size, now)

                carry = lax.fori_loop(0, steps, step, carry)
                to = start + steps * size
            return carry

        flat = jnp.zeros((8, QSTEP), jnp.float32)
        fresh = (flat + LOW, flat, flat)

        def joined(top, total, dot):
            peak = jnp.max(top, axis=0, keepdims=True)
            weight = jnp.exp2(top - peak)
            total = jnp.sum(total * weight, axis=0, keepdims=True)
            dot = jnp.sum(dot * weight, axis=0, keepdims=True)
            return flat + (peak + jnp.log2(total)), flat + dot / total

        def put_queries(tile):
            at = pl.multiple_of(tile * QSTEP, QSTEP)
            grads[0, pl.ds(first + at, QSTEP), :] = dq_acc[...].T * SCALE
            dq_acc[...] = jnp.zeros((HD, QSTEP), jnp.float32)

        dq_acc[...] = jnp.zeros((HD, QSTEP), jnp.float32)
        norm_now = joined(*over_keys(lambda to, size, now: stats(products(0, to, size), to, size, now), fresh))

        def query_tile(tile, norms):
            norm, delta = norms

            def both(to, size, now):
                scores = products(tile, to, size)
                gradients(tile - 1, to, size, norm, delta)
                return stats(scores, to, size, now)

            now = over_keys(both, fresh)
            put_queries(tile - 1)
            return joined(*now)

        norm, delta = lax.fori_loop(1, q_tiles, query_tile, norm_now)

        def rest(to, size, now):
            gradients(q_tiles - 1, to, size, norm, delta)
            return now

        over_keys(rest, 0)
        put_queries(q_tiles - 1)

        def put(part, carry):
            at = pl.multiple_of(part * QSTEP, QSTEP)
            grads[1, pl.ds(first + at, QSTEP), :] = dk_acc[pl.ds(at, QSTEP), :] * SCALE
            grads[2, pl.ds(first + at, QSTEP), :] = dv_acc[pl.ds(at, QSTEP), :]
            return carry

        lax.fori_loop(0, q_tiles, put, 0)
        return carry

    lax.fori_loop(doc_lo, doc_hi, one_document, 0)

    for _, ref, base in pieces:
        lo = jnp.clip(shard_lo - base, 0, ref.shape[0])
        hi = jnp.clip(shard_hi - base, 0, ref.shape[0])

        def empty(shard, carry, ref=ref):
            for slot in range(3):
                ref[shard, slot] = zero_shard.astype(jnp.bfloat16)
            return carry

        def store(shard, carry, ref=ref, base=base):
            at = pl.multiple_of((base + shard) * SHARD, SHARD)
            for slot in range(3):
                ref[shard, slot] = grads[slot, pl.ds(at, SHARD), :].astype(jnp.bfloat16)
            return carry

        lax.fori_loop(0, lo, empty, 0)
        lax.fori_loop(lo, hi, store, 0)
        lax.fori_loop(hi, ref.shape[0], empty, 0)


def attention(bounds, span, left, own, right):
    shape = jax.ShapeDtypeStruct((SHARDS, 3, SHARD, HD), jnp.bfloat16)
    smem = pl.BlockSpec(memory_space=pltpu.SMEM)
    vmem = pl.BlockSpec(memory_space=pltpu.VMEM)
    padded = 3 * BLOCK + QSTEP
    return pl.pallas_call(
        attention_kernel,
        out_shape=(shape, shape, shape),
        in_specs=[smem, smem, vmem, vmem, vmem],
        out_specs=(vmem, vmem, vmem),
        scratch_shapes=[
            pltpu.VMEM((4, padded, HD), jnp.float32),
            pltpu.VMEM((3, padded, HD), jnp.float32),
            pltpu.VMEM((MOST, HD), jnp.bfloat16),
            pltpu.VMEM((MOST, HD), jnp.bfloat16),
            pltpu.VMEM((MOST, HD), jnp.bfloat16),
            pltpu.VMEM((MOST, HD), jnp.bfloat16),
            pltpu.VMEM((HD, MOST), jnp.bfloat16),
            pltpu.VMEM((MOST, HD), jnp.float32),
            pltpu.VMEM((MOST, HD), jnp.float32),
            pltpu.VMEM((HD, QSTEP), jnp.float32),
            pltpu.VMEM((MOST, QSTEP), jnp.float32),
            pltpu.VMEM((MOST, QSTEP), jnp.float32),
            pltpu.VMEM((MOST // PART, 8, QSTEP), jnp.float32),
        ],
        compiler_params=pltpu.CompilerParams(vmem_limit_bytes=38 * 1024 * 1024),
        cost_estimate=pl.CostEstimate(
            flops=5 * 2 * MOST * MOST * HD, bytes_accessed=6 * 1024 * 1024, transcendentals=2 * MOST * MOST
        ),
        name="attention",
    )(bounds, span, left, own, right)


def total_kernel(own_ref, left_ref, right_ref, out_ref):
    def step(shard, carry):
        for slot in range(3):
            parts = [ref[shard, slot].astype(jnp.float32) for ref in (own_ref, left_ref, right_ref)]
            out_ref[shard, slot] = (parts[0] + parts[1] + parts[2]).astype(jnp.bfloat16)
        return carry

    lax.fori_loop(0, SHARDS, step, 0)


def total(own, left, right):
    vmem = pl.BlockSpec(memory_space=pltpu.VMEM)
    return pl.pallas_call(
        total_kernel,
        out_shape=jax.ShapeDtypeStruct(own.shape, own.dtype),
        in_specs=[vmem] * 3,
        out_specs=vmem,
        compiler_params=pltpu.CompilerParams(vmem_limit_bytes=16 * 1024 * 1024),
        cost_estimate=pl.CostEstimate(flops=0, bytes_accessed=3 * 1024 * 1024, transcendentals=0),
        name="total",
    )(own, left, right)


def last_total_kernel(own_ref, left_ref, right_ref, out_ref, held, sems):
    copies = [
        pltpu.make_async_copy(ref, held.at[place], sems.at[place])
        for place, ref in enumerate((own_ref, left_ref, right_ref))
    ]
    for copy in copies:
        copy.start()
    for copy in copies:
        copy.wait()

    def step(shard, carry):
        for slot in range(3):
            parts = [held[place, shard, slot].astype(jnp.float32) for place in range(3)]
            out_ref[shard, slot] = (parts[0] + parts[1] + parts[2]).astype(jnp.bfloat16)
        return carry

    lax.fori_loop(0, SHARDS, step, 0)


def last_total(own, left, right):
    return pl.pallas_call(
        last_total_kernel,
        out_shape=jax.ShapeDtypeStruct(own.shape, own.dtype),
        in_specs=[pl.BlockSpec(memory_space=pl.ANY)] * 3,
        scratch_shapes=[pltpu.VMEM((3,) + own.shape, own.dtype), pltpu.SemaphoreType.DMA((3,))],
        compiler_params=pltpu.CompilerParams(vmem_limit_bytes=16 * 1024 * 1024),
        name="last_total",
    )(own, left, right)


def from_left(shard):
    devices = lax.axis_size("ctx")
    return lax.ppermute(shard, "ctx", [(i, i + 1) for i in range(devices - 1)])


def from_right(shard):
    devices = lax.axis_size("ctx")
    return lax.ppermute(shard, "ctx", [(i + 1, i) for i in range(devices - 1)])


def swap_heads(shard):
    return lax.all_to_all(shard, "head", split_axis=0, concat_axis=0, tiled=True)


def on_device(queries, key_rows, value_rows, out_grad, bounds):
    owner = document_owner(bounds[:-1], bounds[1:])
    me = lax.axis_index("ctx")
    span = jnp.stack([jnp.sum(owner < me), jnp.sum(owner <= me)]).astype(jnp.int32)
    done = []
    for packed, add in zip(pack(queries, key_rows, value_rows, out_grad), (total, last_total)):
        own = swap_heads(packed)
        left = from_left(own)
        right = from_right(own)
        left_grad, own_grad, right_grad = attention(bounds, span, left, own, right)
        own_grad = add(own_grad, from_left(right_grad), from_right(left_grad))
        done.append(swap_heads(own_grad))
    return unpack(*done)


def solution(mesh):
    rows = P(("ctx", "head"), None)
    return jax.shard_map(
        on_device,
        mesh=mesh,
        in_specs=(rows, rows, rows, rows, P()),
        out_specs=(rows, rows, rows),
        check_vma=False,
    )
```
